128 devices in a mesh: space: 32 (over x, y, core), dir: 4 (over z).
Axes of the slice: x: 4, y: 4, z: 4, core: 2. Of those that a mesh axis runs over, the one named last changes fastest.
Arguments:
- currents: bfloat16 [1024, 2, 32, 256], P('space'), may hold values from -6 to 6
- near_blocks: bfloat16 [1024, 6, 2, 256, 256], P('space', None, None, 'dir'), may hold values from -0.15625 to 0.15625
- near_list: int32 [1024, 6], P('space'), may hold values from 0 to 1023, as said below
- near_count: int32 [1024], P('space'), may hold values from 3 to 6, as said below
- radiate: bfloat16 [1024, 2, 128, 256], P('space', None, 'dir'), may hold values from -0.375 to 0.375
- receive: float32 [1024, 2, 128, 256], P('space', None, 'dir'), may hold values from -0.0625 to 0.0625
- phase_one: float32 [4, 512], replicated, may hold values from -3.140625 to 3.140625
- phase_two: float32 [4, 2048], replicated, may hold values from -3.140625 to 3.140625
- interp_one: float32 [512, 128], replicated, may hold values from -0.5 to 0.5
- interp_two: float32 [2048, 512], replicated, may hold values from -0.25 to 0.25
- trans_one: float32 [40, 2, 512], P(None, None, 'dir'), may hold values from -2 to 2
- kind_one: int32 [256, 8], P('space'), may hold values from 0 to 39
- list_one: int32 [256, 8], P('space'), may hold values from 0 to 255, as said below
- trans_two: float32 [40, 2, 2048], P(None, None, 'dir'), may hold values from -2 to 2
- kind_two: int32 [64, 8], replicated, may hold values from 0 to 39
- list_two: int32 [64, 8], replicated, may hold values from 0 to 63
Outputs:
- fields: float32 [1024, 2, 32, 256], P('space', None, None, 'dir')
The draws below stay inside these ranges and needn't reach their ends.
Inputs may be any that keep to these rules, and one draw needn't show every extreme that they name: `near_list`: row b names box b in slot 0, the box exactly 32 below b in slot 1 (above, for b < 32) and the box exactly 32 above b in slot 2 (below, for the last 32 boxes); every entry lies within 32 boxes of b. `near_count`: box 0 uses all slots. `list_one`: every entry of row p lies within 8 parents of p, and slot 0 exactly 8 away.
All inputs are finite; a program needn't handle non-finite values.
Results may differ from the reference program's by a relative error of at most 0.0018.
Values may be sent and summed in bfloat16 or wider, within the bound.
No kernel may reach another device: no remote copies, remote signals or barrier semaphores. Data moves between devices by JAX's collectives and lax.ppermute only.
A program may use at most 128 MiB of HBM per device.

```python
import jax
import jax.numpy as jnp
from jax import lax

P_SIZE = 256
Q0 = 128
Q1 = 512
Q2 = 2048
OFFS = 40
NRHS = 32
BOX_DEV = 32
NEAR_K = 6
K1 = 8
K2 = 8
BOXES = 1024
PARENTS = 256
GRAND = 64
PAR_DEV = 8


def draw_near_list(key, part):
    key = jax.random.fold_in(key, 1)
    boxes = jnp.arange(BOXES, dtype=jnp.int32)[:, None]
    below = jnp.where(boxes >= BOX_DEV, boxes - BOX_DEV, boxes + BOX_DEV)
    above = jnp.where(boxes < BOXES - BOX_DEV, boxes + BOX_DEV, boxes - BOX_DEV)
    step = jax.random.randint(key, (BOXES, NEAR_K - 3), -BOX_DEV, BOX_DEV + 1, dtype=jnp.int32)
    others = jnp.clip(boxes + step, 0, BOXES - 1)
    return jnp.concatenate([boxes, below, above, others], axis=1)


def draw_near_count(key, part):
    key = jax.random.fold_in(key, 2)
    first, second = jax.random.split(key)
    level = jax.random.randint(first, (BOXES // BOX_DEV,), 3, NEAR_K + 1, dtype=jnp.int32)
    raw = jax.random.randint(second, (BOXES,), 3, NEAR_K + 1, dtype=jnp.int32)
    count = jnp.minimum(raw, jnp.repeat(level, BOX_DEV))
    return count.at[0].set(NEAR_K)


def draw_list_one(key, part):
    key = jax.random.fold_in(key, 3)
    parents = jnp.arange(PARENTS, dtype=jnp.int32)[:, None]
    step = jax.random.randint(key, (PARENTS, K1 - 1), -PAR_DEV, PAR_DEV + 1, dtype=jnp.int32)
    others = jnp.clip(parents + step, 0, PARENTS - 1)
    partner = jnp.where(parents >= PAR_DEV, parents - PAR_DEV, parents + PAR_DEV)
    return jnp.concatenate([partner, others], axis=1)


def with_ends(result, own_key, least, top_value):
    index_at = [jax.random.randint(jax.random.fold_in(own_key, axis), (), 0, length) for axis, length in enumerate(result.shape)]
    widest = result.shape.index(max(result.shape))
    beside = index_at[:widest] + [(index_at[widest] + 1) % result.shape[widest]] + index_at[widest + 1:]
    return result.at[tuple(index_at)].set(least).at[tuple(beside)].set(top_value)


def block_levels(key, shape, cuts, low, largest):
    def one(position, shards_of):
        draws = jax.random.uniform(jax.random.fold_in(jax.random.fold_in(key, 6), position), (shards_of,), jnp.float32, low / len(cuts), largest / len(cuts))
        return jnp.repeat(jnp.exp(draws), shape[position] // shards_of).reshape((-1,) + (1,) * (len(shape) - position - 1))

    level = one(*cuts[0])
    for cut in cuts[1:]:
        level = level * one(*cut)
    return level


def noise(stream_key, dims, scale, limit, cuts=(), kind=jnp.bfloat16):
    entries = scale * jax.random.normal(stream_key, dims, jnp.float32)
    if cuts:
        entries = entries * block_levels(stream_key, dims, cuts, -0.22, 0.18)
    return jnp.clip(entries, -limit, limit).astype(kind)


def setup_inputs(seed: int = 0) -> dict:
    streams_of = jax.random.split(jax.random.key(seed), 17)
    return {
        "currents": noise(streams_of[0], (BOXES, 2, NRHS, P_SIZE), 1.0, 6.0, ((0, 32),)),
        "near_blocks": noise(streams_of[1], (BOXES, NEAR_K, 2, P_SIZE, P_SIZE), (P_SIZE * NEAR_K) ** -0.5, 0.15625, ((0, 32), (3, 4))),
        "near_list": draw_near_list(jax.random.fold_in(streams_of[16], 71), 0),
        "near_count": draw_near_count(jax.random.fold_in(streams_of[16], 71), 0),
        "radiate": noise(streams_of[4], (BOXES, 2, Q0, P_SIZE), P_SIZE ** -0.5, 0.375, ((0, 32), (2, 4))),
        "receive": noise(streams_of[5], (BOXES, 2, Q0, P_SIZE), (64 * Q0) ** -0.5, 0.0625, ((0, 32), (2, 4)), jnp.float32),
        "phase_one": jnp.clip(jax.random.uniform(streams_of[6], (4, Q1), jnp.float32, -3.140625, 3.140625), -3.140625, 3.140625),
        "phase_two": jnp.clip(jax.random.uniform(streams_of[7], (4, Q2), jnp.float32, -3.140625, 3.140625), -3.140625, 3.140625),
        "interp_one": noise(streams_of[8], (Q1, Q0), Q0 ** -0.5, 0.5, (), jnp.float32),
        "interp_two": noise(streams_of[9], (Q2, Q1), Q1 ** -0.5, 0.25, (), jnp.float32),
        "trans_one": noise(streams_of[10], (OFFS, 2, Q1), K1 ** -0.5, 2.0, ((2, 4),), jnp.float32),
        "kind_one": with_ends(jax.random.randint(streams_of[11], (PARENTS, K1), 0, OFFS), jax.random.fold_in(streams_of[11], 1), 0, OFFS - 1).astype(jnp.int32),
        "list_one": draw_list_one(jax.random.fold_in(streams_of[16], 71), 0),
        "trans_two": noise(streams_of[13], (OFFS, 2, Q2), K2 ** -0.5, 2.0, ((2, 4),), jnp.float32),
        "kind_two": with_ends(jax.random.randint(streams_of[14], (GRAND, K2), 0, OFFS), jax.random.fold_in(streams_of[14], 1), 0, OFFS - 1).astype(jnp.int32),
        "list_two": with_ends(jax.random.randint(streams_of[15], (GRAND, K2), 0, GRAND), jax.random.fold_in(streams_of[15], 1), 0, GRAND - 1).astype(jnp.int32),
    }


HIGH = lax.Precision.HIGHEST


def lift_level(weights, phases, sample_re, sample_im):
    up_re = jnp.einsum("qc,csb->qsb", weights, sample_re, precision=HIGH)
    up_im = jnp.einsum("qc,csb->qsb", weights, sample_im, precision=HIGH)
    count, width, boxes = up_re.shape
    up_re = up_re.reshape(count, width, boxes // 4, 4)
    up_im = up_im.reshape(count, width, boxes // 4, 4)
    cosine = jnp.cos(phases).T[:, None, None, :]
    sine = jnp.sin(phases).T[:, None, None, :]
    out_re = jnp.sum(cosine * up_re - sine * up_im, axis=3)
    out_im = jnp.sum(cosine * up_im + sine * up_re, axis=3)
    return jnp.stack([out_re, out_im], axis=1)


def lower_level(weights, phases, sample_re, sample_im):
    cosine = jnp.cos(phases).T[:, None, None, :]
    sine = jnp.sin(phases).T[:, None, None, :]
    child_re = cosine * sample_re[..., None] + sine * sample_im[..., None]
    child_im = cosine * sample_im[..., None] - sine * sample_re[..., None]
    shape = sample_re.shape
    child_re = child_re.reshape(shape[0], shape[1], shape[2] * 4)
    child_im = child_im.reshape(shape[0], shape[1], shape[2] * 4)
    down_re = jnp.einsum("qc,qsb->csb", weights, child_re, precision=HIGH)
    down_im = jnp.einsum("qc,qsb->csb", weights, child_im, precision=HIGH)
    return jnp.stack([down_re, down_im], axis=1)


def translate(source, table):
    coeff = jnp.transpose(table, (3, 2, 0, 1))
    coeff_re = coeff[:, 0][:, None]
    coeff_im = coeff[:, 1][:, None]
    out_re = jnp.sum(coeff_re * source[:, 0] - coeff_im * source[:, 1], axis=-1)
    out_im = jnp.sum(coeff_re * source[:, 1] + coeff_im * source[:, 0], axis=-1)
    return jnp.stack([out_re, out_im], axis=1)


def near_box(pair):
    blocks, vectors = pair
    blocks = blocks.astype(jnp.float32)
    vectors = vectors.astype(jnp.float32)
    part_re = jnp.einsum("kip,ksp->si", blocks[:, 0], vectors[:, 0], precision=HIGH) - jnp.einsum("kip,ksp->si", blocks[:, 1], vectors[:, 1], precision=HIGH)
    part_im = jnp.einsum("kip,ksp->si", blocks[:, 0], vectors[:, 1], precision=HIGH) + jnp.einsum("kip,ksp->si", blocks[:, 1], vectors[:, 0], precision=HIGH)
    return jnp.stack([part_re, part_im], axis=0)


def reference(currents, near_blocks, near_list, near_count, radiate, receive, phase_one, phase_two, interp_one, interp_two, trans_one, kind_one, list_one, trans_two, kind_two, list_two):
    slots = jnp.arange(NEAR_K, dtype=jnp.int32)
    live = (slots[None, :] < near_count[:, None]).astype(jnp.bfloat16)
    picked = currents[near_list] * live[:, :, None, None, None]
    near_part = lax.map(near_box, (near_blocks, picked))
    values = currents.astype(jnp.float32)
    matrix = radiate.astype(jnp.float32)
    leaf_re = jnp.einsum("bqp,bsp->qsb", matrix[:, 0], values[:, 0], precision=HIGH) - jnp.einsum("bqp,bsp->qsb", matrix[:, 1], values[:, 1], precision=HIGH)
    leaf_im = jnp.einsum("bqp,bsp->qsb", matrix[:, 0], values[:, 1], precision=HIGH) + jnp.einsum("bqp,bsp->qsb", matrix[:, 1], values[:, 0], precision=HIGH)
    parent = lift_level(interp_one, phase_one, leaf_re, leaf_im)
    near_one = translate(parent[..., list_one], trans_one[kind_one])
    top = lift_level(interp_two, phase_two, parent[:, 0], parent[:, 1])
    top_local = translate(top[..., list_two], trans_two[kind_two])
    local_one = near_one + lower_level(interp_two, phase_two, top_local[:, 0], top_local[:, 1])
    local_leaf = lower_level(interp_one, phase_one, local_one[:, 0], local_one[:, 1])
    far_re = jnp.einsum("bqp,qsb->bsp", receive[:, 0], local_leaf[:, 0], precision=HIGH) - jnp.einsum("bqp,qsb->bsp", receive[:, 1], local_leaf[:, 1], precision=HIGH)
    far_im = jnp.einsum("bqp,qsb->bsp", receive[:, 0], local_leaf[:, 1], precision=HIGH) + jnp.einsum("bqp,qsb->bsp", receive[:, 1], local_leaf[:, 0], precision=HIGH)
    return near_part + jnp.stack([far_re, far_im], axis=1)
```

```python
import jax
import jax.numpy as jnp
from jax import lax
from jax.experimental import pallas as pl
from jax.experimental.pallas import tpu as pltpu
from jax.sharding import PartitionSpec as P

F32 = jnp.float32
BF16 = jnp.bfloat16
VMEM = pl.BlockSpec(memory_space=pltpu.VMEM)
SMEM = pl.BlockSpec(memory_space=pltpu.SMEM)
LIMIT = 48 * 1024 * 1024


def call(kernel, outs, operands, scalars, scratch=(), flops=0, moved=0, name=None):
    shapes = tuple(jax.ShapeDtypeStruct(shape, kind) for shape, kind in outs)
    return pl.pallas_call(
        kernel,
        out_shape=shapes,
        in_specs=[SMEM] * len(scalars) + [VMEM] * len(operands),
        out_specs=tuple(VMEM for _ in outs),
        scratch_shapes=list(scratch),
        compiler_params=pltpu.CompilerParams(vmem_limit_bytes=LIMIT),
        cost_estimate=pl.CostEstimate(flops=flops, bytes_accessed=moved, transcendentals=0),
        name=name,
    )(*scalars, *operands)


def rows_by_rows(a, b):
    return lax.dot_general(a, b, (((1,), (1,)), ((), ())), preferred_element_type=F32)


def rows_by_cols(a, b):
    return lax.dot_general(a, b, (((1,), (0,)), ((), ())), preferred_element_type=F32)


def halves(x):
    high = x.astype(BF16)
    return high, (x - high.astype(F32)).astype(BF16)


def product(dot, x, high, low):
    x_high, x_low = halves(x)
    return dot(x_high, high) + (dot(x_high, low) + dot(x_low, high))


def lanes_of(shape):
    return lax.broadcasted_iota(jnp.int32, shape, len(shape) - 1)


def swap_half(x):
    return pltpu.roll(x, 64, x.ndim - 1)


def leaf_kernel(ids, cur, rad, out0, out1, out2, out3, held):
    lane = lanes_of((32, 128)) // 32
    for p in range(8):
        boxes = cur[4 * p : 4 * p + 4].reshape(256, 256)
        re_rows = rad[4 * p : 4 * p + 4, 0].reshape(128, 256)
        im_rows = rad[4 * p : 4 * p + 4, 1].reshape(128, 256)
        with_re = rows_by_rows(boxes, re_rows)
        with_im = rows_by_rows(boxes, im_rows)
        re = jnp.zeros((32, 128), F32)
        im = jnp.zeros((32, 128), F32)
        for j in range(4):
            a = with_re[64 * j : 64 * j + 64]
            b = with_im[64 * j : 64 * j + 64]
            re = jnp.where(lane == j, a[:32] - b[32:], re)
            im = jnp.where(lane == j, a[32:] + b[:32], im)
        for e in range(4):
            held[e, p, 0] = re[8 * e : 8 * e + 8]
            held[e, p, 1] = im[8 * e : 8 * e + 8]
    own = ids[0]
    for k, out in enumerate((out0, out1, out2, out3)):
        out[...] = held[lax.rem(own + k, 4)]


def split_kernel(one, two, one_high, one_low, two_high, two_low):
    high, low = halves(one[...])
    one_high[...] = high
    one_low[...] = low

    def body(t, carry):
        rows = pl.ds(pl.multiple_of(t * 128, 128), 128)
        high, low = halves(two[rows, :])
        two_high[rows, :] = high
        two_low[rows, :] = low
        return carry

    lax.fori_loop(0, 16, body, 0)


def pack_kernel(ids, rec, out0, out1, out2, out3):
    own = ids[0]
    lane = lanes_of((32, 128)) < 64

    def body(b, carry):
        packs = []
        for m in range(2):
            re = rec[b, 0, :, 128 * m : 128 * m + 128]
            im = rec[b, 1, :, 128 * m : 128 * m + 128]
            packs.append(jnp.where(lane, re, swap_half(im)))
            packs.append(jnp.where(lane, swap_half(re), im))
        for k, out in enumerate((out0, out1, out2, out3)):
            e = lax.rem(own + k, 4)
            value = packs[3]
            for n in range(3):
                value = jnp.where(e == n, packs[n], value)
            out[b] = value
        return carry

    lax.fori_loop(0, 32, body, 0)


def lift_kernel(ids, r0, r1, r2, r3, w1h, w1l, w2h, w2l, cos1, sin1, cos2, sin2, parent, halo, message, held, top):
    own = ids[0]
    for k, r in enumerate((r0, r1, r2, r3)):
        held[lax.rem(own + 4 - k, 4)] = r[...].reshape(128, 128)
    lane = lanes_of((128, 128)) // 32
    rows = []
    for j in range(4):
        x = jnp.zeros((128, 128), F32)
        for e in range(4):
            piece = held[e]
            shift = (32 * (e - j)) % 128
            if shift:
                piece = pltpu.roll(piece, shift, 1)
            x = jnp.where(lane == e, piece, x)
        rows.append(x)
    up = product(rows_by_rows, jnp.concatenate(rows, axis=0), w1h[...], w1l[...])
    up = up.reshape(4, 8, 2, 8, 512)
    re = jnp.zeros((8, 8, 512), F32)
    im = jnp.zeros((8, 8, 512), F32)
    for j in range(4):
        c = cos1[j : j + 1, :][None]
        s = sin1[j : j + 1, :][None]
        re = re + (c * up[j, :, 0] - s * up[j, :, 1])
        im = im + (c * up[j, :, 1] + s * up[j, :, 0])
    parent[:, 0] = re
    parent[:, 1] = im
    whole = parent[...].reshape(128, 512)
    halo[...] = whole.astype(BF16)
    top[...] = product(rows_by_rows, whole, w2h[...], w2l[...]).reshape(2, 4, 2, 8, 2048)
    lane = lanes_of((16, 128)) < 64
    for m in range(16):
        at = slice(128 * m, 128 * m + 128)
        re = jnp.zeros((2, 8, 128), F32)
        im = jnp.zeros((2, 8, 128), F32)
        for j in range(4):
            c = cos2[j : j + 1, at][None]
            s = sin2[j : j + 1, at][None]
            u_re = top[:, j, 0, :, at]
            u_im = top[:, j, 1, :, at]
            re = re + (c * u_re - s * u_im)
            im = im + (c * u_im + s * u_re)
        re = re.reshape(16, 128)
        im = im.reshape(16, 128)
        message[2 * m] = jnp.where(lane, re, swap_half(im))
        message[2 * m + 1] = jnp.where(lane, swap_half(re), im)


def top_kernel(ids, kinds, lists, top, m0, m1, m2, m3, out, swapped, first, second):
    want = lax.rem(ids[0] + 4 - ids[1] // 8, 4)
    table = m3[80:120]
    for n, m in enumerate((m0, m1, m2)):
        table = jnp.where(want == n, m[80:120], table)
    lane = lanes_of((40, 128)) < 64
    turned = swap_half(table)
    first[...] = jnp.where(lane, table, turned)
    second[...] = jnp.where(lane, -turned, table)
    swapped[...] = swap_half(top[...])

    def body(g, carry):
        total = jnp.zeros((8, 128), F32)
        for k in range(8):
            kind = kinds[g, k]
            source = lists[g, k]
            total = total + first[pl.ds(kind, 1), :] * top[source]
            total = total + second[pl.ds(kind, 1), :] * swapped[source]
        out[g] = total
        return carry

    lax.fori_loop(0, 64, body, 0, unroll=4)


def parent_kernel(ids, kinds, lists, before, parent, after, m0, m1, m2, m3, out, held, table):
    own = ids[0]
    base = ids[1] * 8 - 8
    held[0:8] = before[...].astype(F32).reshape(8, 2, 8, 512)
    held[8:16] = parent[...]
    held[16:24] = after[...].astype(F32).reshape(8, 2, 8, 512)
    for k, m in enumerate((m0, m1, m2, m3)):
        table[lax.rem(own + 4 - k, 4)] = m[0:80]

    def body(p, carry):
        re = [jnp.zeros((8, 128), F32) for _ in range(4)]
        im = [jnp.zeros((8, 128), F32) for _ in range(4)]
        for k in range(8):
            kind = kinds[p, k]
            source = lists[p, k] - base
            for m in range(4):
                at = slice(128 * m, 128 * m + 128)
                s_re = held[source, 0, :, at]
                s_im = held[source, 1, :, at]
                c_re = table[m, pl.ds(kind, 1), :]
                c_im = table[m, pl.ds(kind + 40, 1), :]
                re[m] = re[m] + (c_re * s_re - c_im * s_im)
                im[m] = im[m] + (c_re * s_im + c_im * s_re)
        for m in range(4):
            at = slice(128 * m, 128 * m + 128)
            out[p, 0, :, at] = re[m]
            out[p, 1, :, at] = im[m]
        return carry

    lax.fori_loop(0, 8, body, 0)


def lower_kernel(arrived, near_one, w1h, w1l, w2h, w2l, cos1, sin1, cos2, sin2, out, child_high, child_low):
    lane = lanes_of((16, 128)) < 64
    for m in range(16):
        at = slice(128 * m, 128 * m + 128)
        a = arrived[2 * m]
        b = arrived[2 * m + 1]
        re = jnp.where(lane, a, swap_half(b)).reshape(2, 8, 128)
        im = jnp.where(lane, swap_half(a), b).reshape(2, 8, 128)
        for j in range(4):
            c = cos2[j : j + 1, at][None]
            s = sin2[j : j + 1, at][None]
            both = jnp.concatenate([(c * re + s * im)[:, None], (c * im - s * re)[:, None]], axis=1)
            high, low = halves(both.reshape(2, 16, 128))
            for g in range(2):
                rows = slice(64 * g + 16 * j, 64 * g + 16 * j + 16)
                child_high[rows, at] = high[g]
                child_low[rows, at] = low[g]
    high = child_high[...]
    local = rows_by_cols(high, w2h[...]) + (rows_by_cols(high, w2l[...]) + rows_by_cols(child_low[...], w2h[...]))
    local = local.reshape(8, 2, 8, 512) + near_one[...]
    re = local[:, 0]
    im = local[:, 1]
    for j in range(4):
        c = cos1[j : j + 1, :][None]
        s = sin1[j : j + 1, :][None]
        both = jnp.concatenate([(c * re + s * im)[:, None], (c * im - s * re)[:, None]], axis=1)
        down = product(rows_by_cols, both.reshape(128, 512), w1h[...], w1l[...])
        out[j] = down.reshape(8, 2, 8, 128)


def near_kernel(ids, lists, counts, before, current, after, blocks, out, held):
    step = pl.program_id(0)

    @pl.when(step == 0)
    def _():
        held[0:32] = before[...]
        held[32:64] = current[...]
        held[64:96] = after[...]
        held[96] = jnp.zeros((64, 256), BF16)

    base = ids[1] * 32 - 32
    for n in range(4):
        box = step * 4 + n
        total = jnp.zeros((64, 128), F32)
        for k in range(6):
            source = jnp.where(k < counts[box], lists[box, k] - base, 96)
            total = total + rows_by_rows(held[source], blocks[n, k].reshape(128, 256))
        out[n] = total


def receive_kernel(ids, l0, l1, l2, l3, x0, x1, x2, x3, near, out, samples, matrix):
    own = ids[0]
    for k, (l, x) in enumerate(((l0, x0), (l1, x1), (l2, x2), (l3, x3))):
        e = lax.rem(own + 4 - k, 4)
        samples[:, :, :, e] = l[...]
        matrix[:, e] = x[...]

    def body(p, carry):
        for j in range(4):
            b = 4 * p + j
            left = samples[j, p].reshape(64, 128)
            high, low = halves(matrix[b].reshape(128, 128))
            total = near[b] + product(rows_by_cols, left, high, low)
            turned = swap_half(total)
            out[b, 0] = (total[:32] - turned[32:])[:, :64]
            out[b, 1] = (total[32:] + turned[:32])[:, :64]
        return carry

    lax.fori_loop(0, 8, body, 0)


def around(x, axis, peers, k):
    return lax.ppermute(x, axis, [(i, (i + k) % peers) for i in range(peers)])


def shards(
    currents,
    near_blocks,
    near_list,
    near_count,
    radiate,
    receive,
    phase_one,
    phase_two,
    interp_one,
    interp_two,
    trans_one,
    kind_one,
    list_one,
    trans_two,
    kind_two,
    list_two,
):
    space_id = lax.axis_index("space")
    dir_id = lax.axis_index("dir")
    n_space = lax.axis_size("space")
    n_dir = lax.axis_size("dir")
    ids = jnp.stack([dir_id, space_id]).astype(jnp.int32)
    up = [(i, i + 1) for i in range(n_space - 1)]
    down = [(i + 1, i) for i in range(n_space - 1)]

    block = ((8, 2, 8, 128), F32)
    leaf = call(
        leaf_kernel,
        [block] * 4,
        [currents, radiate],
        [ids],
        [pltpu.VMEM((4, 8, 2, 8, 128), F32)],
        flops=2 * 2**27,
        moved=5 * 2**19,
        name="leaf",
    )
    leaf = [leaf[0]] + [around(leaf[k], "dir", n_dir, k) for k in (1, 2, 3)]

    flat = currents.reshape(32, 64, 256)
    before = lax.ppermute(flat, "space", up)
    after = lax.ppermute(flat, "space", down)

    cut = lax.dynamic_slice_in_dim(trans_two, 64 * (space_id % 8), 64, 2).reshape(40, 128)
    tables = jnp.concatenate([trans_one[:, 0], trans_one[:, 1], cut], axis=0)
    tables = [tables] + [around(tables, "dir", n_dir, k) for k in (1, 2, 3)]

    w1h, w1l, w2h, w2l = call(
        split_kernel,
        [((512, 128), BF16)] * 2 + [((2048, 512), BF16)] * 2,
        [interp_one, interp_two],
        [],
        flops=2**22,
        moved=9 * 2**20,
        name="split",
    )
    weights = [w1h, w1l, w2h, w2l, jnp.cos(phase_one), jnp.sin(phase_one), jnp.cos(phase_two), jnp.sin(phase_two)]

    packed = call(
        pack_kernel,
        [((32, 32, 128), F32)] * 4,
        [receive],
        [ids],
        flops=2**21,
        moved=2**22,
        name="pack",
    )
    packed = [packed[0]] + [around(packed[k], "dir", n_dir, k) for k in (1, 2, 3)]

    parent, halo, message = call(
        lift_kernel,
        [((8, 2, 8, 512), F32), ((128, 512), BF16), ((32, 16, 128), F32)],
        leaf + weights,
        [ids],
        [pltpu.VMEM((4, 128, 128), F32), pltpu.VMEM((2, 4, 2, 8, 2048), F32)],
        flops=2**30,
        moved=6 * 2**20,
        name="lift",
    )
    top = lax.all_to_all(message, "space", 0, 0)
    parents_before = lax.ppermute(halo, "space", up)
    parents_after = lax.ppermute(halo, "space", down)

    near = pl.pallas_call(
        near_kernel,
        out_shape=jax.ShapeDtypeStruct((32, 64, 128), F32),
        grid=(8,),
        in_specs=[SMEM] * 3
        + [pl.BlockSpec((32, 64, 256), lambda i: (0, 0, 0))] * 3
        + [pl.BlockSpec((4, 6, 2, 64, 256), lambda i: (i, 0, 0, 0, 0))],
        out_specs=pl.BlockSpec((4, 64, 128), lambda i: (i, 0, 0)),
        scratch_shapes=[pltpu.VMEM((97, 64, 256), BF16)],
        compiler_params=pltpu.CompilerParams(vmem_limit_bytes=LIMIT),
        cost_estimate=pl.CostEstimate(flops=2 * 64 * 128 * 256 * 192, bytes_accessed=16 * 2**20, transcendentals=0),
        name="near",
    )(ids, near_list, near_count, before, flat, after, near_blocks)

    (moved,) = call(
        top_kernel,
        [((64, 8, 128), F32)],
        [top.reshape(64, 8, 128)] + tables,
        [ids, kind_two, list_two],
        [pltpu.VMEM((64, 8, 128), F32), pltpu.VMEM((40, 128), F32), pltpu.VMEM((40, 128), F32)],
        flops=2**21,
        moved=2**20,
        name="translate_two",
    )
    arrived = lax.all_to_all(moved.reshape(32, 16, 128), "space", 0, 0)

    (near_one,) = call(
        parent_kernel,
        [((8, 2, 8, 512), F32)],
        [parents_before, parent, parents_after] + tables,
        [ids, kind_one, list_one],
        [pltpu.VMEM((24, 2, 8, 512), F32), pltpu.VMEM((4, 80, 128), F32)],
        flops=2**22,
        moved=2**20,
        name="translate_one",
    )

    (lowered,) = call(
        lower_kernel,
        [((4, 8, 2, 8, 128), F32)],
        [arrived, near_one] + weights,
        [],
        [pltpu.VMEM((128, 2048), BF16), pltpu.VMEM((128, 2048), BF16)],
        flops=2**30,
        moved=6 * 2**20,
        name="lower",
    )
    lowered = [lowered] + [around(lowered, "dir", n_dir, k) for k in (1, 2, 3)]

    (fields,) = call(
        receive_kernel,
        [((32, 2, 32, 64), F32)],
        lowered + packed + [near],
        [ids],
        [pltpu.VMEM((4, 8, 2, 4, 8, 128), F32), pltpu.VMEM((32, 4, 32, 128), F32)],
        flops=2**28,
        moved=5 * 2**20,
        name="receive",
    )
    return fields


def solution(mesh):
    in_specs = (
        P("space", None, None, None),
        P("space", None, None, "dir", None),
        P("space", None),
        P("space"),
        P("space", None, "dir", None),
        P("space", None, "dir", None),
        P(),
        P(),
        P(),
        P(),
        P(None, None, "dir"),
        P("space", None),
        P("space", None),
        P(None, None, "dir"),
        P(),
        P(),
    )
    out_specs = P("space", None, None, "dir")
    return jax.shard_map(shards, mesh=mesh, in_specs=in_specs, out_specs=out_specs, check_vma=False)
```

```python
import jax
import jax.numpy as jnp
from jax import lax
from jax.experimental import pallas as pl
from jax.experimental.pallas import tpu as pltpu
from jax.sharding import PartitionSpec as P

F32 = jnp.float32
BF16 = jnp.bfloat16
I32 = jnp.int32
I16 = jnp.int16
IN_HBM = pl.BlockSpec(memory_space=pltpu.HBM)
MIB = 1024 * 1024
SMALL = 2**12
LARGE = 2**36


def call(kernel, outs, operands, scratch, copies, cost, name, more=()):
    shapes = tuple(jax.ShapeDtypeStruct(shape, kind) for shape, kind in outs)
    return pl.pallas_call(
        kernel,
        out_shape=shapes,
        in_specs=[IN_HBM] * len(operands),
        out_specs=tuple(IN_HBM for _ in outs),
        scratch_shapes=[*scratch, pltpu.SemaphoreType.DMA((copies,)), *more],
        compiler_params=pltpu.CompilerParams(vmem_limit_bytes=60 * MIB),
        cost_estimate=pl.CostEstimate(flops=cost, bytes_accessed=cost, transcendentals=0),
        name=name,
    )(*operands)


def begin(sems, *pairs, first=0):
    copies = [pltpu.make_async_copy(source, target, sems.at[first + n]) for n, (source, target) in enumerate(pairs)]
    for copy in copies:
        copy.start()
    return copies


def finish(*copies):
    for copy in copies:
        copy.wait()


def rows_by_rows(a, b):
    return lax.dot_general(a, b, (((1,), (1,)), ((), ())), preferred_element_type=F32)


def rows_by_cols(a, b):
    return lax.dot_general(a, b, (((1,), (0,)), ((), ())), preferred_element_type=F32)


def halves(x):
    high = x.astype(BF16)
    return high, (x - high.astype(F32)).astype(BF16)


def product(dot, x, high, low):
    x_high, x_low = halves(x)
    return dot(x_high, high) + (dot(x_high, low) + dot(x_low, high))


def lanes_of(shape):
    return lax.broadcasted_iota(I32, shape, len(shape) - 1)


def swap_half(x):
    return pltpu.roll(x, 64, x.ndim - 1)


def sender(k):
    return lax.rem(lax.axis_index("dir") + 4 - k, 4)


def receiver(k):
    return lax.rem(lax.axis_index("dir") + k, 4)


def leaf_kernel(cur_from, rad_from, one_from, two_from, out0, out1, out2, out3, cur, rad, one, trans, held, sems):
    near_half, far_half = slice(0, 16), slice(16, 32)
    copies = begin(
        sems,
        (cur_from.at[near_half], cur.at[near_half]),
        (rad_from.at[near_half], rad.at[near_half]),
        (cur_from.at[far_half], cur.at[far_half]),
        (rad_from.at[far_half], rad.at[far_half]),
        (one_from, one),
        (two_from, trans),
    )
    lane = lanes_of((32, 128)) // 32
    for p in range(8):
        if p == 0:
            finish(*copies[0:2])
        if p == 4:
            finish(*copies[2:4])
        boxes = cur[4 * p : 4 * p + 4].reshape(256, 256)
        re_rows = rad[4 * p : 4 * p + 4, 0].reshape(128, 256)
        im_rows = rad[4 * p : 4 * p + 4, 1].reshape(128, 256)
        with_re = rows_by_rows(boxes, re_rows)
        with_im = rows_by_rows(boxes, im_rows)
        re = jnp.zeros((32, 128), F32)
        im = jnp.zeros((32, 128), F32)
        for j in range(4):
            a = with_re[64 * j : 64 * j + 64]
            b = with_im[64 * j : 64 * j + 64]
            re = jnp.where(lane == j, a[:32] - b[32:], re)
            im = jnp.where(lane == j, a[32:] + b[:32], im)
        for e in range(4):
            held[e, 16 * p : 16 * p + 8] = re[8 * e : 8 * e + 8]
            held[e, 16 * p + 8 : 16 * p + 16] = im[8 * e : 8 * e + 8]
    finish(*copies[4:6])
    part = lax.rem(lax.axis_index("space"), 8)
    at = pl.ds(pl.multiple_of(part // 2 * 128, 128), 128)
    odd = part % 2
    re = trans[:, 0, at]
    im = trans[:, 1, at]
    lane = lanes_of((40, 128)) < 64
    even_cut = jnp.where(lane, re, swap_half(im))
    odd_cut = jnp.where(lane, swap_half(re), im)
    cut = jnp.where(odd == 1, odd_cut, even_cut)
    for e in range(4):
        held[e, 128:168] = cut
        held[e, 168:208] = one[:, 0, :]
        held[e, 208:248] = one[:, 1, :]
    finish(*begin(sems, *[(held.at[receiver(k)], out) for k, out in enumerate((out0, out1, out2, out3))]))


def pack_kernel(rec_from, out0, out1, out2, out3, rec, held, sems):
    copies = begin(
        sems,
        (rec_from.at[0:16], rec.at[0:16]),
        (rec_from.at[16:32], rec.at[16:32]),
    )
    lane = lanes_of((32, 128)) < 64
    for t in range(2):
        finish(copies[t])

        def body(n, carry):
            b = 16 * t + n
            rows = pl.ds(pl.multiple_of(b * 32, 32), 32)
            for m in range(2):
                re = rec[b, 0, :, 128 * m : 128 * m + 128]
                im = rec[b, 1, :, 128 * m : 128 * m + 128]
                held[2 * m, rows, :] = jnp.where(lane, re, swap_half(im))
                held[2 * m + 1, rows, :] = jnp.where(lane, swap_half(re), im)
            return carry

        lax.fori_loop(0, 16, body, 0, unroll=4)
    finish(*begin(sems, *[(held.at[receiver(k)], out) for k, out in enumerate((out0, out1, out2, out3))]))


def lift_kernel(r0, r1, r2, r3, *refs):
    one_from, two_from, *angles_from = refs[:6]
    parent_to, halo_to, message_to, *weights_to = refs[6:13]
    one, two, cos1, sin1, cos2, sin2 = refs[13:19]
    w1h, w1l, w2h, w2l = refs[19:23]
    parent, halo, message, held, top, sems = refs[23:]
    copies = begin(
        sems,
        *[(r.at[0:128], held.at[sender(k)]) for k, r in enumerate((r0, r1, r2, r3))],
        (one_from, one),
        *zip(angles_from, (cos1, sin1, cos2, sin2)),
        *[(two_from.at[512 * t : 512 * t + 512], two.at[512 * t : 512 * t + 512]) for t in range(4)],
    )
    finish(*copies[0:9])
    high, low = halves(one[...])
    w1h[...] = high
    w1l[...] = low
    copies += begin(sems, (w1h, weights_to[0]), (w1l, weights_to[1]), first=13)
    lane = lanes_of((128, 128)) // 32
    rows = []
    for j in range(4):
        x = jnp.zeros((128, 128), F32)
        for e in range(4):
            piece = held[e]
            shift = (32 * (e - j)) % 128
            if shift:
                piece = pltpu.roll(piece, shift, 1)
            x = jnp.where(lane == e, piece, x)
        rows.append(x)
    up = product(rows_by_rows, jnp.concatenate(rows, axis=0), w1h[...], w1l[...])
    up = up.reshape(4, 8, 2, 8, 512)
    re = jnp.zeros((8, 8, 512), F32)
    im = jnp.zeros((8, 8, 512), F32)
    for j in range(4):
        c = cos1[j : j + 1, :][None]
        s = sin1[j : j + 1, :][None]
        re = re + (c * up[j, :, 0] - s * up[j, :, 1])
        im = im + (c * up[j, :, 1] + s * up[j, :, 0])
    parent[:, 0] = re
    parent[:, 1] = im
    whole = parent[...].reshape(128, 512)
    halo[...] = whole.astype(BF16)
    copies += begin(sems, (parent, parent_to), (halo, halo_to), first=15)
    x_high, x_low = halves(whole)
    for t in range(4):
        finish(copies[9 + t])
        rows = slice(512 * t, 512 * t + 512)
        high, low = halves(two[rows, :])
        w2h[rows, :] = high
        w2l[rows, :] = low
        part = rows_by_rows(x_high, high) + (rows_by_rows(x_high, low) + rows_by_rows(x_low, high))
        top[:, :, :, :, rows] = part.reshape(2, 4, 2, 8, 512)
        copies += begin(
            sems, (w2h.at[rows], weights_to[2].at[rows]), (w2l.at[rows], weights_to[3].at[rows]), first=17 + 2 * t
        )
    lane = lanes_of((16, 128)) < 64
    for m in range(16):
        at = slice(128 * m, 128 * m + 128)
        re = jnp.zeros((2, 8, 128), F32)
        im = jnp.zeros((2, 8, 128), F32)
        for j in range(4):
            c = cos2[j : j + 1, at][None]
            s = sin2[j : j + 1, at][None]
            u_re = top[:, j, 0, :, at]
            u_im = top[:, j, 1, :, at]
            re = re + (c * u_re - s * u_im)
            im = im + (c * u_im + s * u_re)
        re = re.reshape(16, 128)
        im = im.reshape(16, 128)
        message[2 * m] = jnp.where(lane, re, swap_half(im))
        message[2 * m + 1] = jnp.where(lane, swap_half(re), im)
    copies += begin(sems, (message, message_to), first=25)
    finish(*copies[13:])


def top_kernel(kinds_from, lists_from, top_from, m0, m1, m2, m3, out_to, kinds, lists, top, cuts, first, second, out, sems):
    finish(
        *begin(
            sems,
            (kinds_from, kinds),
            (lists_from, lists),
            (top_from, top),
            *[(m.at[128:168], cuts.at[sender(k)]) for k, m in enumerate((m0, m1, m2, m3))],
        )
    )
    table = cuts[lax.axis_index("space") // 8]
    lane = lanes_of((40, 128)) < 64
    turned = swap_half(table)
    first[...] = jnp.where(lane, table, turned)
    second[...] = jnp.where(lane, turned, -table)

    def body(g, carry):
        straight = jnp.zeros((8, 128), F32)
        crossed = jnp.zeros((8, 128), F32)
        for k in range(8):
            kind = kinds[k, g]
            value = top[lists[k, g]]
            straight = straight + first[pl.ds(kind, 1), :] * value
            crossed = crossed + second[pl.ds(kind, 1), :] * value
        out[g] = straight + swap_half(crossed)
        return carry

    lax.fori_loop(0, 64, body, 0, unroll=8)
    finish(*begin(sems, (out, out_to)))


def parent_kernel(
    kinds_from, lists_from, before_from, parent_from, after_from, m0, m1, m2, m3,
    out_to,
    kinds, lists, before, after, held, table, out, sems,
):
    finish(
        *begin(
            sems,
            (kinds_from, kinds),
            (lists_from, lists),
            (before_from, before),
            (parent_from, held.at[8:16]),
            (after_from, after),
            *[(m.at[168:248], table.at[sender(k)]) for k, m in enumerate((m0, m1, m2, m3))],
        )
    )
    base = lax.axis_index("space") * 8 - 8
    held[0:8] = before[...].astype(F32).reshape(8, 2, 8, 512)
    held[16:24] = after[...].astype(F32).reshape(8, 2, 8, 512)

    def body(p, carry):
        re = [jnp.zeros((8, 128), F32) for _ in range(4)]
        im = [jnp.zeros((8, 128), F32) for _ in range(4)]
        for k in range(8):
            kind = kinds[p, k]
            source = lists[p, k] - base
            for m in range(4):
                at = slice(128 * m, 128 * m + 128)
                s_re = held[source, 0, :, at]
                s_im = held[source, 1, :, at]
                c_re = table[m, pl.ds(kind, 1), :]
                c_im = table[m, pl.ds(kind + 40, 1), :]
                re[m] = re[m] + (c_re * s_re - c_im * s_im)
                im[m] = im[m] + (c_re * s_im + c_im * s_re)
        for m in range(4):
            at = slice(128 * m, 128 * m + 128)
            out[p, 0, :, at] = re[m]
            out[p, 1, :, at] = im[m]
        return carry

    lax.fori_loop(0, 8, body, 0)
    finish(*begin(sems, (out, out_to)))


def lower_kernel(arrived_from, near_one_from, *refs):
    sources = refs[:8]
    out_to = refs[8]
    cos1, sin1, cos2, sin2, w1h, w1l, w2h, w2l = refs[9:17]
    arrived, near_one, child_high, child_low, held, out, sems = refs[17:]
    copies = begin(
        sems,
        (arrived_from, arrived),
        (near_one_from, near_one),
        *zip(sources[:6], refs[9:15]),
        *[
            (source.at[512 * t : 512 * t + 512], target.at[512 * t : 512 * t + 512])
            for t in range(4)
            for source, target in zip(sources[6:], (w2h, w2l))
        ],
    )
    finish(copies[0], *copies[4:6])
    lane = lanes_of((16, 128)) < 64
    for m in range(16):
        at = slice(128 * m, 128 * m + 128)
        a = arrived[2 * m]
        b = arrived[2 * m + 1]
        re = jnp.where(lane, a, swap_half(b)).reshape(2, 8, 128)
        im = jnp.where(lane, swap_half(a), b).reshape(2, 8, 128)
        for j in range(4):
            c = cos2[j : j + 1, at][None]
            s = sin2[j : j + 1, at][None]
            both = jnp.concatenate([(c * re + s * im)[:, None], (c * im - s * re)[:, None]], axis=1)
            high, low = halves(both.reshape(2, 16, 128))
            for g in range(2):
                rows = slice(64 * g + 16 * j, 64 * g + 16 * j + 16)
                child_high[rows, at] = high[g]
                child_low[rows, at] = low[g]
    local = jnp.zeros((128, 512), F32)
    for t in range(4):
        finish(*copies[8 + 2 * t : 10 + 2 * t])
        at = slice(512 * t, 512 * t + 512)
        high = child_high[:, at]
        local = local + (
            rows_by_cols(high, w2h[at, :]) + (rows_by_cols(high, w2l[at, :]) + rows_by_cols(child_low[:, at], w2h[at, :]))
        )
    finish(*copies[1:4], *copies[6:8])
    local = local.reshape(8, 2, 8, 512) + near_one[...]
    re = local[:, 0]
    im = local[:, 1]
    for j in range(4):
        c = cos1[j : j + 1, :][None]
        s = sin1[j : j + 1, :][None]
        both = jnp.concatenate([(c * re + s * im)[:, None], (c * im - s * re)[:, None]], axis=1)
        down = product(rows_by_cols, both.reshape(128, 512), w1h[...], w1l[...])
        held[128 * j : 128 * j + 128] = down
    largest = jnp.max(jnp.abs(held[...]), keepdims=True)
    power = jnp.ceil(jnp.log2(jnp.maximum(largest, 2.0**-100)))
    out[0:512] = jnp.round(held[...] * jnp.exp2(14.0 - power)).astype(I32).astype(I16)
    out[512:528] = jnp.broadcast_to(power, (16, 128)).astype(I32).astype(I16)
    finish(*begin(sems, (out, out_to)))


def near_kernel(lists_from, counts_from, before, current, after, blocks_from, out_to, lists, counts, held, blocks, out, sems, block_sems):
    def first_slots(box):
        return pltpu.make_async_copy(blocks_from.at[box, 0:3], blocks.at[box, 0:3], block_sems.at[box, 0])

    def slot(box, k):
        return pltpu.make_async_copy(blocks_from.at[box, k], blocks.at[box, k], block_sems.at[box, k - 2])

    copies = begin(sems, (lists_from, lists), (counts_from, counts), (before, held.at[0:32]), (current, held.at[32:64]), (after, held.at[64:96]))
    finish(copies[1])

    def request(box, carry):
        first_slots(box).start()
        for k in range(3, 6):

            @pl.when(k < counts[box])
            def _():
                slot(box, k).start()

        return carry

    lax.fori_loop(0, 32, request, 0)
    finish(copies[0], *copies[2:5])
    base = lax.axis_index("space") * 32 - 32

    def body(step, carry):
        for n in range(4):
            box = 4 * step + n
            first_slots(box).wait()
            for k in range(3, 6):

                @pl.when(k < counts[box])
                def _():
                    slot(box, k).wait()

        for n in range(4):
            box = 4 * step + n
            total = jnp.zeros((64, 128), F32)
            for k in range(6):
                block = blocks[box, k].reshape(128, 256)
                if k >= 3:
                    block = jnp.where(k < counts[box], block, jnp.zeros_like(block))
                total = total + rows_by_rows(held[lists[k, box] - base], block)
            out[box] = total
        return carry

    lax.fori_loop(0, 8, body, 0)
    finish(*begin(sems, (out, out_to)))


def receive_kernel(l0, l1, l2, l3, x0, x1, x2, x3, near_from, out_to, codes, samples, matrix, near, out, sems):
    copies = begin(
        sems,
        *[(l, codes.at[k]) for k, l in enumerate((l0, l1, l2, l3))],
        *[(x.reshape(32, 32, 128), matrix.at[:, sender(k)]) for k, x in enumerate((x0, x1, x2, x3))],
        (near_from, near),
    )
    finish(*copies[0:4])
    for k in range(4):
        unit = jnp.exp2(codes[k, 512:528].astype(I32).astype(F32)[0:1] - 14.0)
        values = codes[k, 0:512].astype(I32).astype(F32) * unit
        samples[:, :, :, sender(k)] = values.reshape(4, 8, 2, 8, 128)
    finish(*copies[4:9])

    def body(p, carry):
        for j in range(4):
            b = 4 * p + j
            left_high, left_low = halves(samples[j, p].reshape(64, 128))
            high, low = halves(matrix[b].reshape(128, 128))
            left = jnp.concatenate([left_high, left_low], axis=1)
            right = jnp.concatenate(
                [jnp.concatenate([high, low], axis=1), jnp.concatenate([high, jnp.zeros_like(low)], axis=1)], axis=0
            )
            both = rows_by_cols(left, right)
            total = near[b] + (both[:, :128] + both[:, 128:])
            turned = swap_half(total)
            out[b, 0] = (total[:32] - turned[32:])[:, :64]
            out[b, 1] = (total[32:] + turned[:32])[:, :64]
        return carry

    for t in range(4):
        lax.fori_loop(2 * t, 2 * t + 2, body, 0, unroll=2)
        part = slice(8 * t, 8 * t + 8)
        copies += begin(sems, (out.at[part], out_to.at[part]), first=9 + t)
    finish(*copies[9:])


def around(x, axis, peers, k):
    return lax.ppermute(x, axis, [(i, (i + k) % peers) for i in range(peers)])


def after_all(values, *tokens):
    return lax.optimization_barrier((*values, *tokens))[: len(values)]


def shards(
    currents,
    near_blocks,
    near_list,
    near_count,
    radiate,
    receive,
    phase_one,
    phase_two,
    interp_one,
    interp_two,
    trans_one,
    kind_one,
    list_one,
    trans_two,
    kind_two,
    list_two,
):
    n_space = lax.axis_size("space")
    n_dir = lax.axis_size("dir")
    up = [(i, i + 1) for i in range(n_space - 1)]
    down = [(i + 1, i) for i in range(n_space - 1)]

    flat = currents.reshape(32, 64, 256)
    before = lax.ppermute(flat, "space", up)
    after = lax.ppermute(flat, "space", down)

    leaf = call(
        leaf_kernel,
        [((248, 128), F32)] * 4,
        [currents, radiate, trans_one, trans_two],
        [
            pltpu.VMEM((32, 2, 32, 256), BF16),
            pltpu.VMEM((32, 2, 32, 256), BF16),
            pltpu.VMEM((40, 2, 128), F32),
            pltpu.VMEM((40, 2, 512), F32),
            pltpu.VMEM((4, 248, 128), F32),
        ],
        6,
        LARGE,
        "leaf",
    )
    own_leaf = leaf[0]
    leaf = [own_leaf] + [around(leaf[k], "dir", n_dir, k) for k in (1, 2, 3)]
    packed = call(
        pack_kernel,
        [((1024, 128), F32)] * 4,
        list(after_all((receive,), own_leaf)),
        [pltpu.VMEM((32, 2, 32, 256), F32), pltpu.VMEM((4, 1024, 128), F32)],
        4,
        SMALL,
        "pack",
    )
    leaf, packed, before, after = lax.optimization_barrier((leaf, packed, before, after))
    packed = [packed[0]] + [around(packed[k], "dir", n_dir, k) for k in (1, 2, 3)]

    angles = [jnp.cos(phase_one), jnp.sin(phase_one), jnp.cos(phase_two), jnp.sin(phase_two)]
    angle_room = [*[pltpu.VMEM((4, 512), F32)] * 2, *[pltpu.VMEM((4, 2048), F32)] * 2]
    weight_room = [*[pltpu.VMEM((512, 128), BF16)] * 2, *[pltpu.VMEM((2048, 512), BF16)] * 2]

    parent, halo, message, *weights = call(
        lift_kernel,
        [((8, 2, 8, 512), F32), ((128, 512), BF16), ((32, 16, 128), F32)]
        + [((512, 128), BF16)] * 2
        + [((2048, 512), BF16)] * 2,
        leaf + [interp_one, interp_two] + angles,
        [
            pltpu.VMEM((512, 128), F32),
            pltpu.VMEM((2048, 512), F32),
            *angle_room,
            *weight_room,
            pltpu.VMEM((8, 2, 8, 512), F32),
            pltpu.VMEM((128, 512), BF16),
            pltpu.VMEM((32, 16, 128), F32),
            pltpu.VMEM((4, 128, 128), F32),
            pltpu.VMEM((2, 4, 2, 8, 2048), F32),
        ],
        26,
        LARGE,
        "lift",
    )
    top = lax.all_to_all(message, "space", 0, 0)
    parents_before = lax.ppermute(halo, "space", up)
    parents_after = lax.ppermute(halo, "space", down)

    (moved,) = call(
        top_kernel,
        [((64, 8, 128), F32)],
        [kind_two.T, list_two.T, top.reshape(64, 8, 128)] + leaf,
        [
            pltpu.SMEM((8, 64), I32),
            pltpu.SMEM((8, 64), I32),
            pltpu.VMEM((64, 8, 128), F32),
            pltpu.VMEM((4, 40, 128), F32),
            pltpu.VMEM((40, 128), F32),
            pltpu.VMEM((40, 128), F32),
            pltpu.VMEM((64, 8, 128), F32),
        ],
        7,
        LARGE,
        "translate_two",
    )
    arrived = lax.all_to_all(moved.reshape(32, 16, 128), "space", 0, 0)

    packed, parents_before, parents_after = lax.optimization_barrier((packed, parents_before, parents_after))
    (near_one,) = call(
        parent_kernel,
        [((8, 2, 8, 512), F32)],
        [kind_one, list_one, parents_before, parent, parents_after] + leaf,
        [
            pltpu.SMEM((8, 8), I32),
            pltpu.SMEM((8, 8), I32),
            pltpu.VMEM((128, 512), BF16),
            pltpu.VMEM((128, 512), BF16),
            pltpu.VMEM((24, 2, 8, 512), F32),
            pltpu.VMEM((4, 80, 128), F32),
            pltpu.VMEM((8, 2, 8, 512), F32),
        ],
        9,
        SMALL,
        "translate_one",
    )

    (lowered,) = call(
        lower_kernel,
        [((528, 128), I16)],
        [arrived, near_one] + angles + weights,
        [
            *angle_room,
            *weight_room,
            pltpu.VMEM((32, 16, 128), F32),
            pltpu.VMEM((8, 2, 8, 512), F32),
            pltpu.VMEM((128, 2048), BF16),
            pltpu.VMEM((128, 2048), BF16),
            pltpu.VMEM((512, 128), F32),
            pltpu.VMEM((528, 128), I16),
        ],
        16,
        LARGE,
        "lower",
    )
    shared = [around(lowered, "dir", n_dir, k) for k in (1, 2, 3)]

    (near,) = call(
        near_kernel,
        [((32, 64, 128), F32)],
        [near_list.T, near_count, before, flat, after, near_blocks],
        [
            pltpu.SMEM((6, 32), I32),
            pltpu.SMEM((32,), I32),
            pltpu.VMEM((96, 64, 256), BF16),
            pltpu.VMEM((32, 6, 2, 64, 256), BF16),
            pltpu.VMEM((32, 64, 128), F32),
        ],
        5,
        SMALL,
        "near",
        more=[pltpu.SemaphoreType.DMA((32, 4))],
    )
    (fields,) = call(
        receive_kernel,
        [((32, 2, 32, 64), F32)],
        [lowered] + shared + packed + [near],
        [
            pltpu.VMEM((4, 528, 128), I16),
            pltpu.VMEM((4, 8, 2, 4, 8, 128), F32),
            pltpu.VMEM((32, 4, 32, 128), F32),
            pltpu.VMEM((32, 64, 128), F32),
            pltpu.VMEM((32, 2, 32, 64), F32),
        ],
        13,
        LARGE,
        "receive",
    )
    return fields


def solution(mesh):
    in_specs = (
        P("space", None, None, None),
        P("space", None, None, "dir", None),
        P("space", None),
        P("space"),
        P("space", None, "dir", None),
        P("space", None, "dir", None),
        P(),
        P(),
        P(),
        P(),
        P(None, None, "dir"),
        P("space", None),
        P("space", None),
        P(None, None, "dir"),
        P(),
        P(),
    )
    out_specs = P("space", None, None, "dir")
    return jax.shard_map(shards, mesh=mesh, in_specs=in_specs, out_specs=out_specs, check_vma=False)
```

```python
import jax
import jax.numpy as jnp
from jax import lax
from jax.experimental import pallas as pl
from jax.experimental.pallas import tpu as pltpu
from jax.sharding import PartitionSpec as P

F32 = jnp.float32
BF16 = jnp.bfloat16
I32 = jnp.int32
I16 = jnp.int16
IN_HBM = pl.BlockSpec(memory_space=pltpu.HBM)
ANYWHERE = pl.BlockSpec(memory_space=pl.ANY)
MIB = 1024 * 1024
SMALL = 2**12
LARGE = 2**36


def call(kernel, outs, operands, scratch, copies, cost, name, landed=()):
    shapes = tuple(jax.ShapeDtypeStruct(shape, kind) for shape, kind in outs)
    return pl.pallas_call(
        kernel,
        out_shape=shapes,
        in_specs=[ANYWHERE if n in landed else IN_HBM for n in range(len(operands))],
        out_specs=tuple(IN_HBM for _ in outs),
        scratch_shapes=[*scratch, pltpu.SemaphoreType.DMA((copies,))],
        compiler_params=pltpu.CompilerParams(vmem_limit_bytes=52 * MIB),
        cost_estimate=pl.CostEstimate(flops=cost, bytes_accessed=cost, transcendentals=0),
        name=name,
    )(*operands)


def begin(sems, *pairs, first=0):
    copies = [pltpu.make_async_copy(source, target, sems.at[first + n]) for n, (source, target) in enumerate(pairs)]
    for copy in copies:
        copy.start()
    return copies


def finish(*copies):
    for copy in copies:
        copy.wait()


def rows_by_rows(a, b):
    return lax.dot_general(a, b, (((1,), (1,)), ((), ())), preferred_element_type=F32)


def rows_by_cols(a, b):
    return lax.dot_general(a, b, (((1,), (0,)), ((), ())), preferred_element_type=F32)


def halves(x):
    high = x.astype(BF16)
    return high, (x - high.astype(F32)).astype(BF16)


def product(dot, x, high, low):
    x_high, x_low = halves(x)
    return dot(x_high, high) + (dot(x_high, low) + dot(x_low, high))


def lanes_of(shape):
    return lax.broadcasted_iota(I32, shape, len(shape) - 1)


def swap_half(x):
    return pltpu.roll(x, 64, x.ndim - 1)


def sender(k):
    return lax.rem(lax.axis_index("dir") + 4 - k, 4)


def receiver(k):
    return lax.rem(lax.axis_index("dir") + k, 4)


def power_of(largest):
    return jnp.ceil(jnp.log2(jnp.maximum(largest, 2.0**-100)))


def code_of(scaled):
    return jnp.round(scaled).astype(I32).astype(I16)


def value_of(code):
    return code.astype(I32).astype(F32)


def unit_of(rows):
    return jnp.exp2(value_of(rows)[0:1] - 14.0)


def leaf_kernel(cur_from, rad_from, one_from, two_from, out0, out1, out2, out3, cur, rad, one, trans, held, sems):
    near_half, far_half = slice(0, 16), slice(16, 32)
    copies = begin(
        sems,
        (cur_from.at[near_half], cur.at[near_half]),
        (rad_from.at[near_half], rad.at[near_half]),
        (cur_from.at[far_half], cur.at[far_half]),
        (rad_from.at[far_half], rad.at[far_half]),
        (one_from, one),
        (two_from, trans),
    )
    lane = lanes_of((32, 128)) // 32
    for p in range(8):
        if p == 0:
            finish(*copies[0:2])
        if p == 4:
            finish(*copies[2:4])
        boxes = cur[4 * p : 4 * p + 4].reshape(256, 256)
        re_rows = rad[4 * p : 4 * p + 4, 0].reshape(128, 256)
        im_rows = rad[4 * p : 4 * p + 4, 1].reshape(128, 256)
        with_re = rows_by_rows(boxes, re_rows)
        with_im = rows_by_rows(boxes, im_rows)
        re = jnp.zeros((32, 128), F32)
        im = jnp.zeros((32, 128), F32)
        for j in range(4):
            a = with_re[64 * j : 64 * j + 64]
            b = with_im[64 * j : 64 * j + 64]
            re = jnp.where(lane == j, a[:32] - b[32:], re)
            im = jnp.where(lane == j, a[32:] + b[:32], im)
        for e in range(4):
            held[e, 16 * p : 16 * p + 8] = re[8 * e : 8 * e + 8]
            held[e, 16 * p + 8 : 16 * p + 16] = im[8 * e : 8 * e + 8]
    finish(*copies[4:6])
    part = lax.rem(lax.axis_index("space"), 8)
    at = pl.ds(pl.multiple_of(part // 2 * 128, 128), 128)
    odd = part % 2
    re = trans[:, 0, at]
    im = trans[:, 1, at]
    lane = lanes_of((40, 128)) < 64
    even_cut = jnp.where(lane, re, swap_half(im))
    odd_cut = jnp.where(lane, swap_half(re), im)
    cut = jnp.where(odd == 1, odd_cut, even_cut)
    for e in range(4):
        held[e, 128:168] = cut
        held[e, 168:208] = one[:, 0, :]
        held[e, 208:248] = one[:, 1, :]
    finish(*begin(sems, *[(held.at[receiver(k)], out) for k, out in enumerate((out0, out1, out2, out3))]))


def pack_kernel(rec_from, one_from, two_from, *refs):
    outs = refs[:4]
    angles_to = refs[4:8]
    rec, one, two, cos1, sin1, cos2, sin2, held, sems = refs[8:]
    copies = begin(
        sems, (one_from, one), (two_from, two), (rec_from.at[0:16], rec.at[0:16]), (rec_from.at[16:32], rec.at[16:32])
    )
    finish(*copies[0:2])
    cos1[...] = jnp.cos(one[...])
    sin1[...] = jnp.sin(one[...])
    cos2[...] = jnp.cos(two[...])
    sin2[...] = jnp.sin(two[...])
    angle_copies = begin(sems, *zip((cos1, sin1, cos2, sin2), angles_to), first=4)
    largest = jnp.zeros((32, 256), F32)
    for t in range(2):
        finish(copies[2 + t])

        def look(b, found):
            return jnp.maximum(found, jnp.maximum(jnp.abs(rec[b, 0]), jnp.abs(rec[b, 1])))

        largest = lax.fori_loop(16 * t, 16 * t + 16, look, largest, unroll=4)
    power = power_of(jnp.max(largest, keepdims=True))
    unit = jnp.exp2(14.0 - power)
    for e in range(4):
        held[e, 1024:1040] = jnp.broadcast_to(power, (16, 128)).astype(I32).astype(I16)
    lane = lanes_of((32, 128)) < 64

    def body(b, carry):
        rows = pl.ds(pl.multiple_of(b * 32, 32), 32)
        for m in range(2):
            re = rec[b, 0, :, 128 * m : 128 * m + 128] * unit
            im = rec[b, 1, :, 128 * m : 128 * m + 128] * unit
            held[2 * m, rows, :] = code_of(jnp.where(lane, re, swap_half(im)))
            held[2 * m + 1, rows, :] = code_of(jnp.where(lane, swap_half(re), im))
        return carry

    lax.fori_loop(0, 32, body, 0, unroll=4)
    finish(*begin(sems, *[(held.at[receiver(k)], out) for k, out in enumerate(outs)]), *angle_copies)


def lift_kernel(r0, r1, r2, r3, *refs):
    one_from, two_from, *angles_from = refs[:6]
    parent_to, halo_to, message_to, *weights_to = refs[6:13]
    one, two, cos1, sin1, cos2, sin2 = refs[13:19]
    w1h, w1l, w2h, w2l = refs[19:23]
    parent, halo, message, held, top, sems = refs[23:]
    copies = begin(
        sems,
        *[(r.at[0:128], held.at[sender(k)]) for k, r in enumerate((r0, r1, r2, r3))],
        (one_from, one),
        *zip(angles_from, (cos1, sin1, cos2, sin2)),
        *[(two_from.at[512 * t : 512 * t + 512], two.at[512 * t : 512 * t + 512]) for t in range(4)],
    )
    finish(*copies[0:9])
    high, low = halves(one[...])
    w1h[...] = high
    w1l[...] = low
    copies += begin(sems, (w1h, weights_to[0]), (w1l, weights_to[1]), first=13)
    lane = lanes_of((128, 128)) // 32
    rows = []
    for j in range(4):
        x = jnp.zeros((128, 128), F32)
        for e in range(4):
            piece = held[e]
            shift = (32 * (e - j)) % 128
            if shift:
                piece = pltpu.roll(piece, shift, 1)
            x = jnp.where(lane == e, piece, x)
        rows.append(x)
    up = product(rows_by_rows, jnp.concatenate(rows, axis=0), w1h[...], w1l[...])
    up = up.reshape(4, 8, 2, 8, 512)
    re = jnp.zeros((8, 8, 512), F32)
    im = jnp.zeros((8, 8, 512), F32)
    for j in range(4):
        c = cos1[j : j + 1, :][None]
        s = sin1[j : j + 1, :][None]
        re = re + (c * up[j, :, 0] - s * up[j, :, 1])
        im = im + (c * up[j, :, 1] + s * up[j, :, 0])
    parent[:, 0] = re
    parent[:, 1] = im
    whole = parent[...].reshape(128, 512)
    halo[...] = whole.astype(BF16)
    copies += begin(sems, (parent, parent_to), (halo, halo_to), first=15)
    x_high, x_low = halves(whole)
    for t in range(4):
        finish(copies[9 + t])
        rows = slice(512 * t, 512 * t + 512)
        high, low = halves(two[rows, :])
        w2h[rows, :] = high
        w2l[rows, :] = low
        part = rows_by_rows(x_high, high) + (rows_by_rows(x_high, low) + rows_by_rows(x_low, high))
        top[:, :, :, :, rows] = part.reshape(2, 4, 2, 8, 512)
        copies += begin(
            sems, (w2h.at[rows], weights_to[2].at[rows]), (w2l.at[rows], weights_to[3].at[rows]), first=17 + 2 * t
        )
    lane = lanes_of((16, 128)) < 64
    for m in range(16):
        at = slice(128 * m, 128 * m + 128)
        re = jnp.zeros((2, 8, 128), F32)
        im = jnp.zeros((2, 8, 128), F32)
        for j in range(4):
            c = cos2[j : j + 1, at][None]
            s = sin2[j : j + 1, at][None]
            u_re = top[:, j, 0, :, at]
            u_im = top[:, j, 1, :, at]
            re = re + (c * u_re - s * u_im)
            im = im + (c * u_im + s * u_re)
        re = re.reshape(16, 128)
        im = im.reshape(16, 128)
        message[2 * m] = jnp.where(lane, re, swap_half(im))
        message[2 * m + 1] = jnp.where(lane, swap_half(re), im)
    copies += begin(sems, (message, message_to), first=25)
    finish(*copies[13:])


def top_kernel(kinds_from, lists_from, top_from, m0, m1, m2, m3, out_to, kinds, lists, top, cuts, first, second, out, sems):
    finish(
        *begin(
            sems,
            (kinds_from, kinds),
            (lists_from, lists),
            (top_from, top),
            *[(m.at[128:168], cuts.at[sender(k)]) for k, m in enumerate((m0, m1, m2, m3))],
        )
    )
    table = cuts[lax.axis_index("space") // 8]
    lane = lanes_of((40, 128)) < 64
    turned = swap_half(table)
    first[...] = jnp.where(lane, table, turned)
    second[...] = jnp.where(lane, turned, -table)

    def body(g, carry):
        straight = jnp.zeros((8, 128), F32)
        crossed = jnp.zeros((8, 128), F32)
        for k in range(8):
            kind = kinds[k, g]
            value = top[lists[k, g]]
            straight = straight + first[pl.ds(kind, 1), :] * value
            crossed = crossed + second[pl.ds(kind, 1), :] * value
        out[g] = straight + swap_half(crossed)
        return carry

    lax.fori_loop(0, 64, body, 0, unroll=8)
    finish(*begin(sems, (out, out_to)))


def parent_kernel(
    kinds_from, lists_from, before_from, parent_from, after_from, m0, m1, m2, m3,
    out_to,
    kinds, lists, before, after, held, table, out, sems,
):
    finish(
        *begin(
            sems,
            (kinds_from, kinds),
            (lists_from, lists),
            (before_from, before),
            (parent_from, held.at[8:16]),
            (after_from, after),
            *[(m.at[168:248], table.at[sender(k)]) for k, m in enumerate((m0, m1, m2, m3))],
        )
    )
    base = lax.axis_index("space") * 8 - 8
    held[0:8] = before[...].astype(F32).reshape(8, 2, 8, 512)
    held[16:24] = after[...].astype(F32).reshape(8, 2, 8, 512)

    def body(p, carry):
        re = [jnp.zeros((8, 128), F32) for _ in range(4)]
        im = [jnp.zeros((8, 128), F32) for _ in range(4)]
        for k in range(8):
            kind = kinds[p, k]
            source = lists[p, k] - base
            for m in range(4):
                at = slice(128 * m, 128 * m + 128)
                s_re = held[source, 0, :, at]
                s_im = held[source, 1, :, at]
                c_re = table[m, pl.ds(kind, 1), :]
                c_im = table[m, pl.ds(kind + 40, 1), :]
                re[m] = re[m] + (c_re * s_re - c_im * s_im)
                im[m] = im[m] + (c_re * s_im + c_im * s_re)
        for m in range(4):
            at = slice(128 * m, 128 * m + 128)
            out[p, 0, :, at] = re[m]
            out[p, 1, :, at] = im[m]
        return carry

    lax.fori_loop(0, 8, body, 0)
    finish(*begin(sems, (out, out_to)))


def lower_kernel(arrived_from, near_one_from, *refs):
    sources = refs[:8]
    out_to = refs[8]
    cos1, sin1, cos2, sin2, w1h, w1l, w2h, w2l = refs[9:17]
    arrived, near_one, child_high, child_low, held, out, sems = refs[17:]
    copies = begin(
        sems,
        (arrived_from, arrived),
        (near_one_from, near_one),
        *zip(sources[:6], refs[9:15]),
        *[
            (source.at[512 * t : 512 * t + 512], target.at[512 * t : 512 * t + 512])
            for t in range(4)
            for source, target in zip(sources[6:], (w2h, w2l))
        ],
    )
    finish(copies[0], *copies[4:6])
    lane = lanes_of((16, 128)) < 64
    for m in range(16):
        at = slice(128 * m, 128 * m + 128)
        a = arrived[2 * m]
        b = arrived[2 * m + 1]
        re = jnp.where(lane, a, swap_half(b)).reshape(2, 8, 128)
        im = jnp.where(lane, swap_half(a), b).reshape(2, 8, 128)
        for j in range(4):
            c = cos2[j : j + 1, at][None]
            s = sin2[j : j + 1, at][None]
            both = jnp.concatenate([(c * re + s * im)[:, None], (c * im - s * re)[:, None]], axis=1)
            high, low = halves(both.reshape(2, 16, 128))
            for g in range(2):
                rows = slice(64 * g + 16 * j, 64 * g + 16 * j + 16)
                child_high[rows, at] = high[g]
                child_low[rows, at] = low[g]
    local = jnp.zeros((128, 512), F32)
    for t in range(4):
        finish(*copies[8 + 2 * t : 10 + 2 * t])
        at = slice(512 * t, 512 * t + 512)
        high = child_high[:, at]
        local = local + (
            rows_by_cols(high, w2h[at, :]) + (rows_by_cols(high, w2l[at, :]) + rows_by_cols(child_low[:, at], w2h[at, :]))
        )
    finish(*copies[1:4], *copies[6:8])
    local = local.reshape(8, 2, 8, 512) + near_one[...]
    re = local[:, 0]
    im = local[:, 1]
    for j in range(4):
        c = cos1[j : j + 1, :][None]
        s = sin1[j : j + 1, :][None]
        both = jnp.concatenate([(c * re + s * im)[:, None], (c * im - s * re)[:, None]], axis=1)
        down = product(rows_by_cols, both.reshape(128, 512), w1h[...], w1l[...])
        held[128 * j : 128 * j + 128] = down
    largest = jnp.max(jnp.abs(held[...]), keepdims=True)
    power = power_of(largest)
    out[0:512] = code_of(held[...] * jnp.exp2(14.0 - power))
    out[512:528] = jnp.broadcast_to(power, (16, 128)).astype(I32).astype(I16)
    finish(*begin(sems, (out, out_to)))


def near_kernel(lists_from, counts_from, before, current, after, blocks_from, out_to, lists, counts, held, blocks, out, sems):
    copies = begin(
        sems,
        (lists_from, lists),
        (counts_from, counts),
        (before, held.at[0:32]),
        (current, held.at[32:64]),
        (after, held.at[64:96]),
        *[(blocks_from.at[4 * t : 4 * t + 4], blocks.at[4 * t : 4 * t + 4]) for t in range(8)],
    )
    held[96] = jnp.zeros((64, 256), BF16)
    finish(*copies[0:5])
    base = lax.axis_index("space") * 32 - 32

    for t in range(8):
        finish(copies[5 + t])

        def body(n, carry):
            for box in (4 * t + 2 * n, 4 * t + 2 * n + 1):
                total = jnp.zeros((64, 128), F32)
                for k in range(6):
                    source = jnp.where(k < counts[box], lists[k, box] - base, 96)
                    total = total + rows_by_rows(held[source], blocks[box, k].reshape(128, 256))
                out[box] = total
            return carry

        lax.fori_loop(0, 2, body, 0, unroll=2)
        copies += begin(sems, (out.at[4 * t : 4 * t + 4], out_to.at[4 * t : 4 * t + 4]), first=13 + t)
    finish(*copies[13:])


def receive_kernel(l0, l1, l2, l3, x0, x1, x2, x3, near_from, out_to, codes, packs, samples, matrix, near, out, sems):
    copies = begin(
        sems,
        *[(l, codes.at[k]) for k, l in enumerate((l0, l1, l2, l3))],
        *[(x, packs.at[k]) for k, x in enumerate((x0, x1, x2, x3))],
        (near_from, near),
    )
    finish(*copies[0:4])
    for k in range(4):
        values = value_of(codes[k, 0:512]) * unit_of(codes[k, 512:528])
        samples[:, :, :, sender(k)] = values.reshape(4, 8, 2, 8, 128)
    finish(*copies[4:9])
    units = [unit_of(packs[k, 1024:1040]) for k in range(4)]

    def body(p, carry):
        for j in range(4):
            b = 4 * p + j
            rows = pl.ds(pl.multiple_of(32 * b, 32), 32)
            for k in range(4):
                matrix[b, sender(k)] = value_of(packs[k, rows, :]) * units[k]
            left_high, left_low = halves(samples[j, p].reshape(64, 128))
            high, low = halves(matrix[b].reshape(128, 128))
            left = jnp.concatenate([left_high, left_low], axis=1)
            right = jnp.concatenate(
                [jnp.concatenate([high, low], axis=1), jnp.concatenate([high, jnp.zeros_like(low)], axis=1)], axis=0
            )
            both = rows_by_cols(left, right)
            total = near[b] + (both[:, :128] + both[:, 128:])
            turned = swap_half(total)
            out[b, 0] = (total[:32] - turned[32:])[:, :64]
            out[b, 1] = (total[32:] + turned[:32])[:, :64]
        return carry

    for t in range(4):
        lax.fori_loop(2 * t, 2 * t + 2, body, 0, unroll=2)
        part = slice(8 * t, 8 * t + 8)
        copies += begin(sems, (out.at[part], out_to.at[part]), first=9 + t)
    finish(*copies[9:])


def around(x, axis, peers, k):
    return lax.ppermute(x, axis, [(i, (i + k) % peers) for i in range(peers)])


def after_all(values, *tokens):
    return lax.optimization_barrier((*values, *tokens))[: len(values)]


def shards(
    currents,
    near_blocks,
    near_list,
    near_count,
    radiate,
    receive,
    phase_one,
    phase_two,
    interp_one,
    interp_two,
    trans_one,
    kind_one,
    list_one,
    trans_two,
    kind_two,
    list_two,
):
    n_space = lax.axis_size("space")
    n_dir = lax.axis_size("dir")
    up = [(i, i + 1) for i in range(n_space - 1)]
    down = [(i + 1, i) for i in range(n_space - 1)]

    flat = currents.reshape(32, 64, 256)
    before = lax.ppermute(flat, "space", up)
    after = lax.ppermute(flat, "space", down)

    leaf = call(
        leaf_kernel,
        [((248, 128), F32)] * 4,
        [currents, radiate, trans_one, trans_two],
        [
            pltpu.VMEM((32, 2, 32, 256), BF16),
            pltpu.VMEM((32, 2, 32, 256), BF16),
            pltpu.VMEM((40, 2, 128), F32),
            pltpu.VMEM((40, 2, 512), F32),
            pltpu.VMEM((4, 248, 128), F32),
        ],
        6,
        LARGE,
        "leaf",
    )
    own_leaf = leaf[0]
    leaf = [own_leaf] + [around(leaf[k], "dir", n_dir, k) for k in (1, 2, 3)]
    angle_room = [*[pltpu.VMEM((4, 512), F32)] * 2, *[pltpu.VMEM((4, 2048), F32)] * 2]
    packed = call(
        pack_kernel,
        [((1040, 128), I16)] * 4 + [((4, 512), F32)] * 2 + [((4, 2048), F32)] * 2,
        list(after_all((receive, phase_one, phase_two), own_leaf)),
        [
            pltpu.VMEM((32, 2, 32, 256), F32),
            pltpu.VMEM((4, 512), F32),
            pltpu.VMEM((4, 2048), F32),
            *angle_room,
            pltpu.VMEM((4, 1040, 128), I16),
        ],
        8,
        SMALL,
        "pack",
    )
    packed, angles = packed[:4], packed[4:]
    leaf, packed, before, after = lax.optimization_barrier((leaf, packed, before, after))
    packed = [packed[0]] + [around(packed[k], "dir", n_dir, k) for k in (1, 2, 3)]

    weight_room = [*[pltpu.VMEM((512, 128), BF16)] * 2, *[pltpu.VMEM((2048, 512), BF16)] * 2]

    parent, halo, message, *weights = call(
        lift_kernel,
        [((8, 2, 8, 512), F32), ((128, 512), BF16), ((32, 16, 128), F32)]
        + [((512, 128), BF16)] * 2
        + [((2048, 512), BF16)] * 2,
        leaf + [interp_one, interp_two] + list(angles),
        [
            pltpu.VMEM((512, 128), F32),
            pltpu.VMEM((2048, 512), F32),
            *angle_room,
            *weight_room,
            pltpu.VMEM((8, 2, 8, 512), F32),
            pltpu.VMEM((128, 512), BF16),
            pltpu.VMEM((32, 16, 128), F32),
            pltpu.VMEM((4, 128, 128), F32),
            pltpu.VMEM((2, 4, 2, 8, 2048), F32),
        ],
        26,
        LARGE,
        "lift",
        landed=(1, 2, 3),
    )
    top = lax.all_to_all(message, "space", 0, 0)
    parents_before = lax.ppermute(halo, "space", up)
    parents_after = lax.ppermute(halo, "space", down)

    (moved,) = call(
        top_kernel,
        [((64, 8, 128), F32)],
        [kind_two.T, list_two.T, top.reshape(64, 8, 128)] + leaf,
        [
            pltpu.SMEM((8, 64), I32),
            pltpu.SMEM((8, 64), I32),
            pltpu.VMEM((64, 8, 128), F32),
            pltpu.VMEM((4, 40, 128), F32),
            pltpu.VMEM((40, 128), F32),
            pltpu.VMEM((40, 128), F32),
            pltpu.VMEM((64, 8, 128), F32),
        ],
        7,
        LARGE,
        "translate_two",
        landed=(2, 4, 5, 6),
    )
    arrived = lax.all_to_all(moved.reshape(32, 16, 128), "space", 0, 0)

    packed, parents_before, parents_after = lax.optimization_barrier((packed, parents_before, parents_after))
    (near_one,) = call(
        parent_kernel,
        [((8, 2, 8, 512), F32)],
        [kind_one, list_one, parents_before, parent, parents_after] + leaf,
        [
            pltpu.SMEM((8, 8), I32),
            pltpu.SMEM((8, 8), I32),
            pltpu.VMEM((128, 512), BF16),
            pltpu.VMEM((128, 512), BF16),
            pltpu.VMEM((24, 2, 8, 512), F32),
            pltpu.VMEM((4, 80, 128), F32),
            pltpu.VMEM((8, 2, 8, 512), F32),
        ],
        9,
        SMALL,
        "translate_one",
        landed=(2, 4, 6, 7, 8),
    )

    (lowered,) = call(
        lower_kernel,
        [((528, 128), I16)],
        [arrived, near_one] + list(angles) + weights,
        [
            *angle_room,
            *weight_room,
            pltpu.VMEM((32, 16, 128), F32),
            pltpu.VMEM((8, 2, 8, 512), F32),
            pltpu.VMEM((128, 2048), BF16),
            pltpu.VMEM((128, 2048), BF16),
            pltpu.VMEM((512, 128), F32),
            pltpu.VMEM((528, 128), I16),
        ],
        16,
        LARGE,
        "lower",
        landed=(0,),
    )
    shared = [around(lowered, "dir", n_dir, k) for k in (1, 2, 3)]

    (near,) = call(
        near_kernel,
        [((32, 64, 128), F32)],
        [near_list.T, near_count, before, flat, after, near_blocks],
        [
            pltpu.SMEM((6, 32), I32),
            pltpu.SMEM((32,), I32),
            pltpu.VMEM((97, 64, 256), BF16),
            pltpu.VMEM((32, 6, 2, 64, 256), BF16),
            pltpu.VMEM((32, 64, 128), F32),
        ],
        21,
        SMALL,
        "near",
        landed=(2, 4),
    )
    (fields,) = call(
        receive_kernel,
        [((32, 2, 32, 64), F32)],
        [lowered] + shared + packed + [near],
        [
            pltpu.VMEM((4, 528, 128), I16),
            pltpu.VMEM((4, 1040, 128), I16),
            pltpu.VMEM((4, 8, 2, 4, 8, 128), F32),
            pltpu.VMEM((32, 4, 32, 128), F32),
            pltpu.VMEM((32, 64, 128), F32),
            pltpu.VMEM((32, 2, 32, 64), F32),
        ],
        13,
        LARGE,
        "receive",
        landed=(1, 2, 3, 5, 6, 7),
    )
    return fields


def solution(mesh):
    in_specs = (
        P("space", None, None, None),
        P("space", None, None, "dir", None),
        P("space", None),
        P("space"),
        P("space", None, "dir", None),
        P("space", None, "dir", None),
        P(),
        P(),
        P(),
        P(),
        P(None, None, "dir"),
        P("space", None),
        P("space", None),
        P(None, None, "dir"),
        P(),
        P(),
    )
    out_specs = P("space", None, None, "dir")
    return jax.shard_map(shards, mesh=mesh, in_specs=in_specs, out_specs=out_specs, check_vma=False)
```

```python
import jax
import jax.numpy as jnp
from jax import lax
from jax.experimental import pallas as pl
from jax.experimental.pallas import tpu as pltpu
from jax.sharding import PartitionSpec as P

F32 = jnp.float32
BF16 = jnp.bfloat16
I32 = jnp.int32
I16 = jnp.int16
IN_HBM = pl.BlockSpec(memory_space=pltpu.HBM)
ANYWHERE = pl.BlockSpec(memory_space=pl.ANY)
MIB = 1024 * 1024
SMALL = 2**12
LARGE = 2**36


def call(kernel, outs, operands, scratch, copies, cost, name, landed=(), limit=52):
    shapes = tuple(jax.ShapeDtypeStruct(shape, kind) for shape, kind in outs)
    return pl.pallas_call(
        kernel,
        out_shape=shapes,
        in_specs=[ANYWHERE if n in landed else IN_HBM for n in range(len(operands))],
        out_specs=tuple(IN_HBM for _ in outs),
        scratch_shapes=[*scratch, pltpu.SemaphoreType.DMA((copies,))],
        compiler_params=pltpu.CompilerParams(vmem_limit_bytes=limit * MIB),
        cost_estimate=pl.CostEstimate(flops=cost, bytes_accessed=cost, transcendentals=0),
        name=name,
    )(*operands)


def begin(sems, *pairs, first=0):
    copies = [pltpu.make_async_copy(source, target, sems.at[first + n]) for n, (source, target) in enumerate(pairs)]
    for copy in copies:
        copy.start()
    return copies


def finish(*copies):
    for copy in copies:
        copy.wait()


def rows_by_rows(a, b):
    return lax.dot_general(a, b, (((1,), (1,)), ((), ())), preferred_element_type=F32)


def rows_by_cols(a, b):
    return lax.dot_general(a, b, (((1,), (0,)), ((), ())), preferred_element_type=F32)


def halves(x):
    high = x.astype(BF16)
    return high, (x - high.astype(F32)).astype(BF16)


def product(dot, x, high, low):
    x_high, x_low = halves(x)
    return dot(x_high, high) + (dot(x_high, low) + dot(x_low, high))


def lanes_of(shape):
    return lax.broadcasted_iota(I32, shape, len(shape) - 1)


def swap_half(x):
    return pltpu.roll(x, 64, x.ndim - 1)


def sender(k):
    return lax.rem(lax.axis_index("dir") + 4 - k, 4)


def receiver(k):
    return lax.rem(lax.axis_index("dir") + k, 4)


def power_of(largest):
    return jnp.ceil(jnp.log2(jnp.maximum(largest, 2.0**-100)))


def code_of(scaled):
    return jnp.round(scaled).astype(I32).astype(I16)


def value_of(code):
    return code.astype(I32).astype(F32)


def scale_from(power):
    return jnp.exp2(-power) * 32767.0


def unit_from(power):
    return jnp.exp2(power) * (1.0 / 32767.0)


def unit_of(rows):
    return unit_from(value_of(rows)[0:1])


def leaf_kernel(cur_from, rad_from, one_from, two_from, out0, out1, out2, out3, cur, rad, one, trans, held, codes, sems):
    near_half, far_half = slice(0, 16), slice(16, 32)
    copies = begin(
        sems,
        (cur_from.at[near_half], cur.at[near_half]),
        (rad_from.at[near_half], rad.at[near_half]),
        (cur_from.at[far_half], cur.at[far_half]),
        (rad_from.at[far_half], rad.at[far_half]),
        (one_from, one),
        (two_from, trans),
    )
    lane = lanes_of((32, 128)) // 32
    for p in range(8):
        if p == 0:
            finish(*copies[0:2])
        if p == 4:
            finish(*copies[2:4])
        boxes = cur[4 * p : 4 * p + 4].reshape(256, 256)
        re_rows = rad[4 * p : 4 * p + 4, 0].reshape(128, 256)
        im_rows = rad[4 * p : 4 * p + 4, 1].reshape(128, 256)
        with_re = rows_by_rows(boxes, re_rows)
        with_im = rows_by_rows(boxes, im_rows)
        re = jnp.zeros((32, 128), F32)
        im = jnp.zeros((32, 128), F32)
        for j in range(4):
            a = with_re[64 * j : 64 * j + 64]
            b = with_im[64 * j : 64 * j + 64]
            re = jnp.where(lane == j, a[:32] - b[32:], re)
            im = jnp.where(lane == j, a[32:] + b[:32], im)
        for e in range(4):
            held[e, 16 * p : 16 * p + 8] = re[8 * e : 8 * e + 8]
            held[e, 16 * p + 8 : 16 * p + 16] = im[8 * e : 8 * e + 8]
    finish(*copies[4:6])
    part = lax.rem(lax.axis_index("space"), 8)
    at = pl.ds(pl.multiple_of(part // 2 * 128, 128), 128)
    odd = part % 2
    re = trans[:, 0, at]
    im = trans[:, 1, at]
    lane = lanes_of((40, 128)) < 64
    even_cut = jnp.where(lane, re, swap_half(im))
    odd_cut = jnp.where(lane, swap_half(re), im)
    cut = jnp.where(odd == 1, odd_cut, even_cut)
    cut = jnp.concatenate([cut, jnp.zeros((8, 128), F32)], axis=0)
    table = jnp.concatenate([one[:, 0, :], one[:, 1, :]], axis=0)
    row = lax.broadcasted_iota(I32, (16, 128), 0)
    powers = jnp.zeros((16, 128), F32)
    coded = []
    for n, values in enumerate((held[...], cut, table)):
        flat = jnp.abs(values).reshape(-1, 128)
        power = power_of(jnp.max(flat, keepdims=True))
        powers = jnp.where(row == n, power, powers)
        coded.append(code_of(values.reshape(-1, 128) * scale_from(power)))
    for e in range(4):
        codes[e, 0:128] = coded[0][128 * e : 128 * e + 128]
        codes[e, 128:176] = coded[1]
        codes[e, 176:256] = coded[2]
        codes[e, 256:272] = powers.astype(I32).astype(I16)
    finish(*begin(sems, *[(codes.at[receiver(k)], out) for k, out in enumerate((out0, out1, out2, out3))]))


def pack_kernel(rec_from, one_from, two_from, *refs):
    outs = refs[:4]
    angles_to = refs[4:8]
    rec, one, two, cos1, sin1, cos2, sin2, held, sems = refs[8:]
    copies = begin(
        sems, (one_from, one), (two_from, two), (rec_from.at[0:16], rec.at[0:16]), (rec_from.at[16:32], rec.at[16:32])
    )
    finish(*copies[0:2])
    cos1[...] = jnp.cos(one[...])
    sin1[...] = jnp.sin(one[...])
    cos2[...] = jnp.cos(two[...])
    sin2[...] = jnp.sin(two[...])
    angle_copies = begin(sems, *zip((cos1, sin1, cos2, sin2), angles_to), first=4)
    largest = jnp.zeros((32, 256), F32)
    for t in range(2):
        finish(copies[2 + t])

        def look(b, found):
            return jnp.maximum(found, jnp.maximum(jnp.abs(rec[b, 0]), jnp.abs(rec[b, 1])))

        largest = lax.fori_loop(16 * t, 16 * t + 16, look, largest, unroll=4)
    power = power_of(jnp.max(largest, keepdims=True))
    unit = scale_from(power)
    for e in range(4):
        held[e, 1024:1040] = jnp.broadcast_to(power, (16, 128)).astype(I32).astype(I16)
    lane = lanes_of((32, 128)) < 64

    def body(b, carry):
        rows = pl.ds(pl.multiple_of(b * 32, 32), 32)
        for m in range(2):
            re = rec[b, 0, :, 128 * m : 128 * m + 128] * unit
            im = rec[b, 1, :, 128 * m : 128 * m + 128] * unit
            held[2 * m, rows, :] = code_of(jnp.where(lane, re, swap_half(im)))
            held[2 * m + 1, rows, :] = code_of(jnp.where(lane, swap_half(re), im))
        return carry

    lax.fori_loop(0, 32, body, 0, unroll=4)
    finish(*begin(sems, *[(held.at[receiver(k)], out) for k, out in enumerate(outs)]), *angle_copies)


def lift_kernel(r0, r1, r2, r3, *refs):
    one_from, two_from, *angles_from = refs[:6]
    parent_to, halo_to, message_to = refs[6:9]
    one, two, cos1, sin1, cos2, sin2 = refs[9:15]
    parent, halo, message, codes, held, top, sems = refs[15:]
    copies = begin(
        sems,
        *[(r, codes.at[sender(k)]) for k, r in enumerate((r0, r1, r2, r3))],
        (one_from, one),
        *zip(angles_from, (cos1, sin1, cos2, sin2)),
        *[(two_from.at[512 * t : 512 * t + 512], two.at[512 * t : 512 * t + 512]) for t in range(4)],
    )
    finish(*copies[0:9])
    for e in range(4):
        held[e] = value_of(codes[e, 0:128]) * unit_of(codes[e, 256:272])
    w1h, w1l = halves(one[...])
    lane = lanes_of((128, 128)) // 32
    rows = []
    for j in range(4):
        x = jnp.zeros((128, 128), F32)
        for e in range(4):
            piece = held[e]
            shift = (32 * (e - j)) % 128
            if shift:
                piece = pltpu.roll(piece, shift, 1)
            x = jnp.where(lane == e, piece, x)
        rows.append(x)
    up = product(rows_by_rows, jnp.concatenate(rows, axis=0), w1h, w1l)
    up = up.reshape(4, 8, 2, 8, 512)
    re = jnp.zeros((8, 8, 512), F32)
    im = jnp.zeros((8, 8, 512), F32)
    for j in range(4):
        c = cos1[j : j + 1, :][None]
        s = sin1[j : j + 1, :][None]
        re = re + (c * up[j, :, 0] - s * up[j, :, 1])
        im = im + (c * up[j, :, 1] + s * up[j, :, 0])
    parent[:, 0] = re
    parent[:, 1] = im
    whole = parent[...].reshape(128, 512)
    halo[...] = whole.astype(BF16)
    copies += begin(sems, (parent, parent_to), (halo, halo_to), first=13)
    x_high, x_low = halves(whole)
    for t in range(4):
        finish(copies[9 + t])
        rows = slice(512 * t, 512 * t + 512)
        high, low = halves(two[rows, :])
        part = rows_by_rows(x_high, high) + (rows_by_rows(x_high, low) + rows_by_rows(x_low, high))
        top[:, :, :, :, rows] = part.reshape(2, 4, 2, 8, 512)
    lane = lanes_of((16, 128)) < 64
    for m in range(16):
        at = slice(128 * m, 128 * m + 128)
        re = jnp.zeros((2, 8, 128), F32)
        im = jnp.zeros((2, 8, 128), F32)
        for j in range(4):
            c = cos2[j : j + 1, at][None]
            s = sin2[j : j + 1, at][None]
            u_re = top[:, j, 0, :, at]
            u_im = top[:, j, 1, :, at]
            re = re + (c * u_re - s * u_im)
            im = im + (c * u_im + s * u_re)
        re = re.reshape(16, 128)
        im = im.reshape(16, 128)
        message[2 * m] = jnp.where(lane, re, swap_half(im))
        message[2 * m + 1] = jnp.where(lane, swap_half(re), im)
    copies += begin(sems, (message, message_to), first=15)
    finish(*copies[13:])


def top_kernel(kinds_from, lists_from, top_from, m0, m1, m2, m3, out_to, kinds, lists, top, cuts, first, second, out, sems):
    finish(
        *begin(
            sems,
            (kinds_from, kinds),
            (lists_from, lists),
            (top_from, top),
            *[(m.at[128:272], cuts.at[sender(k)]) for k, m in enumerate((m0, m1, m2, m3))],
        )
    )
    chosen = lax.axis_index("space") // 8
    unit = unit_from(value_of(cuts[chosen, 128:144])[1:2])
    table = (value_of(cuts[chosen, 0:48]) * unit)[0:40]
    lane = lanes_of((40, 128)) < 64
    turned = swap_half(table)
    first[...] = jnp.where(lane, table, turned)
    second[...] = jnp.where(lane, turned, -table)

    def body(g, carry):
        straight = jnp.zeros((8, 128), F32)
        crossed = jnp.zeros((8, 128), F32)
        for k in range(8):
            kind = kinds[k, g]
            value = top[lists[k, g]]
            straight = straight + first[pl.ds(kind, 1), :] * value
            crossed = crossed + second[pl.ds(kind, 1), :] * value
        out[g] = straight + swap_half(crossed)
        return carry

    lax.fori_loop(0, 64, body, 0, unroll=8)
    finish(*begin(sems, (out, out_to)))


def parent_kernel(
    kinds_from, lists_from, before_from, parent_from, after_from, m0, m1, m2, m3,
    out_to,
    kinds, lists, before, after, held, codes, table, out, sems,
):
    finish(
        *begin(
            sems,
            (kinds_from, kinds),
            (lists_from, lists),
            (before_from, before),
            (parent_from, held.at[8:16]),
            (after_from, after),
            *[(m.at[176:272], codes.at[sender(k)]) for k, m in enumerate((m0, m1, m2, m3))],
        )
    )
    base = lax.axis_index("space") * 8 - 8
    for e in range(4):
        table[e] = value_of(codes[e, 0:80]) * unit_from(value_of(codes[e, 80:96])[2:3])
    held[0:8] = before[...].astype(F32).reshape(8, 2, 8, 512)
    held[16:24] = after[...].astype(F32).reshape(8, 2, 8, 512)

    def body(p, carry):
        re = [jnp.zeros((8, 128), F32) for _ in range(4)]
        im = [jnp.zeros((8, 128), F32) for _ in range(4)]
        for k in range(8):
            kind = kinds[p, k]
            source = lists[p, k] - base
            for m in range(4):
                at = slice(128 * m, 128 * m + 128)
                s_re = held[source, 0, :, at]
                s_im = held[source, 1, :, at]
                c_re = table[m, pl.ds(kind, 1), :]
                c_im = table[m, pl.ds(kind + 40, 1), :]
                re[m] = re[m] + (c_re * s_re - c_im * s_im)
                im[m] = im[m] + (c_re * s_im + c_im * s_re)
        for m in range(4):
            at = slice(128 * m, 128 * m + 128)
            out[p, 0, :, at] = re[m]
            out[p, 1, :, at] = im[m]
        return carry

    lax.fori_loop(0, 8, body, 0)
    finish(*begin(sems, (out, out_to)))


def lower_kernel(arrived_from, near_one_from, *refs):
    sources = refs[:6]
    out_to = refs[6]
    cos1, sin1, cos2, sin2, one, two = refs[7:13]
    arrived, near_one, child_high, child_low, held, out, sems = refs[13:]
    copies = begin(
        sems,
        (arrived_from, arrived),
        (near_one_from, near_one),
        *zip(sources[:5], refs[7:12]),
        *[(sources[5].at[512 * t : 512 * t + 512], two.at[512 * t : 512 * t + 512]) for t in range(4)],
    )
    finish(copies[0], *copies[4:6])
    lane = lanes_of((16, 128)) < 64
    for m in range(16):
        at = slice(128 * m, 128 * m + 128)
        a = arrived[2 * m]
        b = arrived[2 * m + 1]
        re = jnp.where(lane, a, swap_half(b)).reshape(2, 8, 128)
        im = jnp.where(lane, swap_half(a), b).reshape(2, 8, 128)
        for j in range(4):
            c = cos2[j : j + 1, at][None]
            s = sin2[j : j + 1, at][None]
            both = jnp.concatenate([(c * re + s * im)[:, None], (c * im - s * re)[:, None]], axis=1)
            high, low = halves(both.reshape(2, 16, 128))
            for g in range(2):
                rows = slice(64 * g + 16 * j, 64 * g + 16 * j + 16)
                child_high[rows, at] = high[g]
                child_low[rows, at] = low[g]
    local = jnp.zeros((128, 512), F32)
    for t in range(4):
        finish(copies[7 + t])
        at = slice(512 * t, 512 * t + 512)
        high = child_high[:, at]
        w2h, w2l = halves(two[at, :])
        local = local + (rows_by_cols(high, w2h) + (rows_by_cols(high, w2l) + rows_by_cols(child_low[:, at], w2h)))
    finish(*copies[1:4], copies[6])
    w1h, w1l = halves(one[...])
    local = local.reshape(8, 2, 8, 512) + near_one[...]
    re = local[:, 0]
    im = local[:, 1]
    for j in range(4):
        c = cos1[j : j + 1, :][None]
        s = sin1[j : j + 1, :][None]
        both = jnp.concatenate([(c * re + s * im)[:, None], (c * im - s * re)[:, None]], axis=1)
        down = product(rows_by_cols, both.reshape(128, 512), w1h, w1l)
        held[128 * j : 128 * j + 128] = down
    largest = jnp.max(jnp.abs(held[...]), keepdims=True)
    power = power_of(largest)
    out[0:512] = code_of(held[...] * scale_from(power))
    out[512:528] = jnp.broadcast_to(power, (16, 128)).astype(I32).astype(I16)
    finish(*begin(sems, (out, out_to)))


def near_kernel(lists_from, counts_from, before, current, after, blocks_from, out_to, lists, counts, held, blocks, out, sems):
    copies = begin(
        sems,
        (lists_from, lists),
        (counts_from, counts),
        (before, held.at[0:32]),
        (current, held.at[32:64]),
        (after, held.at[64:96]),
        *[(blocks_from.at[4 * t : 4 * t + 4], blocks.at[4 * t : 4 * t + 4]) for t in range(8)],
    )
    held[96] = jnp.zeros((64, 256), BF16)
    finish(*copies[0:5])
    base = lax.axis_index("space") * 32 - 32

    for t in range(8):
        finish(copies[5 + t])

        def body(n, carry):
            for box in (4 * t + 2 * n, 4 * t + 2 * n + 1):
                total = jnp.zeros((64, 128), F32)
                for k in range(6):
                    source = jnp.where(k < counts[box], lists[k, box] - base, 96)
                    total = total + rows_by_rows(held[source], blocks[box, k].reshape(128, 256))
                out[box] = total
            return carry

        lax.fori_loop(0, 2, body, 0, unroll=2)
        copies += begin(sems, (out.at[4 * t : 4 * t + 4], out_to.at[4 * t : 4 * t + 4]), first=13 + t)
    finish(*copies[13:])


def receive_kernel(l0, l1, l2, l3, x0, x1, x2, x3, near_from, out_to, codes, packs, samples, matrix, near, out, sems):
    copies = begin(
        sems,
        *[(l, codes.at[k]) for k, l in enumerate((l0, l1, l2, l3))],
        *[(x, packs.at[k]) for k, x in enumerate((x0, x1, x2, x3))],
        (near_from, near),
    )
    finish(*copies[0:4])
    for k in range(4):
        values = value_of(codes[k, 0:512]) * unit_of(codes[k, 512:528])
        samples[:, :, :, sender(k)] = values.reshape(4, 8, 2, 8, 128)
    finish(*copies[4:9])
    units = [unit_of(packs[k, 1024:1040]) for k in range(4)]

    def body(p, carry):
        for j in range(4):
            b = 4 * p + j
            rows = pl.ds(pl.multiple_of(32 * b, 32), 32)
            for k in range(4):
                matrix[b, sender(k)] = value_of(packs[k, rows, :]) * units[k]
            left_high, left_low = halves(samples[j, p].reshape(64, 128))
            high, low = halves(matrix[b].reshape(128, 128))
            left = jnp.concatenate([left_high, left_low], axis=1)
            right = jnp.concatenate(
                [jnp.concatenate([high, low], axis=1), jnp.concatenate([high, jnp.zeros_like(low)], axis=1)], axis=0
            )
            both = rows_by_cols(left, right)
            total = near[b] + (both[:, :128] + both[:, 128:])
            turned = swap_half(total)
            out[b, 0] = (total[:32] - turned[32:])[:, :64]
            out[b, 1] = (total[32:] + turned[:32])[:, :64]
        return carry

    for t in range(4):
        lax.fori_loop(2 * t, 2 * t + 2, body, 0, unroll=2)
        part = slice(8 * t, 8 * t + 8)
        copies += begin(sems, (out.at[part], out_to.at[part]), first=9 + t)
    finish(*copies[9:])


def around(x, axis, peers, k):
    return lax.ppermute(x, axis, [(i, (i + k) % peers) for i in range(peers)])


def after_all(values, *tokens):
    return lax.optimization_barrier((*values, *tokens))[: len(values)]


def shards(
    currents,
    near_blocks,
    near_list,
    near_count,
    radiate,
    receive,
    phase_one,
    phase_two,
    interp_one,
    interp_two,
    trans_one,
    kind_one,
    list_one,
    trans_two,
    kind_two,
    list_two,
):
    n_space = lax.axis_size("space")
    n_dir = lax.axis_size("dir")
    up = [(i, i + 1) for i in range(n_space - 1)]
    down = [(i + 1, i) for i in range(n_space - 1)]

    flat = currents.reshape(32, 64, 256)
    before = lax.ppermute(flat, "space", up)
    after = lax.ppermute(flat, "space", down)

    leaf = call(
        leaf_kernel,
        [((272, 128), I16)] * 4,
        [currents, radiate, trans_one, trans_two],
        [
            pltpu.VMEM((32, 2, 32, 256), BF16),
            pltpu.VMEM((32, 2, 32, 256), BF16),
            pltpu.VMEM((40, 2, 128), F32),
            pltpu.VMEM((40, 2, 512), F32),
            pltpu.VMEM((4, 128, 128), F32),
            pltpu.VMEM((4, 272, 128), I16),
        ],
        6,
        LARGE,
        "leaf",
        limit=62,
    )
    own_leaf = leaf[0]
    leaf = [own_leaf] + [around(leaf[k], "dir", n_dir, k) for k in (1, 2, 3)]
    angle_room = [*[pltpu.VMEM((4, 512), F32)] * 2, *[pltpu.VMEM((4, 2048), F32)] * 2]
    packed = call(
        pack_kernel,
        [((1040, 128), I16)] * 4 + [((4, 512), F32)] * 2 + [((4, 2048), F32)] * 2,
        list(after_all((receive, phase_one, phase_two), own_leaf)),
        [
            pltpu.VMEM((32, 2, 32, 256), F32),
            pltpu.VMEM((4, 512), F32),
            pltpu.VMEM((4, 2048), F32),
            *angle_room,
            pltpu.VMEM((4, 1040, 128), I16),
        ],
        8,
        SMALL,
        "pack",
    )
    packed, angles = packed[:4], packed[4:]
    leaf, packed, before, after = lax.optimization_barrier((leaf, packed, before, after))
    packed = [packed[0]] + [around(packed[k], "dir", n_dir, k) for k in (1, 2, 3)]


    parent, halo, message = call(
        lift_kernel,
        [((8, 2, 8, 512), F32), ((128, 512), BF16), ((32, 16, 128), F32)],
        leaf + [interp_one, interp_two] + list(angles),
        [
            pltpu.VMEM((512, 128), F32),
            pltpu.VMEM((2048, 512), F32),
            *angle_room,
            pltpu.VMEM((8, 2, 8, 512), F32),
            pltpu.VMEM((128, 512), BF16),
            pltpu.VMEM((32, 16, 128), F32),
            pltpu.VMEM((4, 272, 128), I16),
            pltpu.VMEM((4, 128, 128), F32),
            pltpu.VMEM((2, 4, 2, 8, 2048), F32),
        ],
        16,
        LARGE,
        "lift",
        landed=(1, 2, 3),
    )
    top = lax.all_to_all(message, "space", 0, 0)
    parents_before = lax.ppermute(halo, "space", up)
    parents_after = lax.ppermute(halo, "space", down)

    (moved,) = call(
        top_kernel,
        [((64, 8, 128), F32)],
        [kind_two.T, list_two.T, top.reshape(64, 8, 128)] + leaf,
        [
            pltpu.SMEM((8, 64), I32),
            pltpu.SMEM((8, 64), I32),
            pltpu.VMEM((64, 8, 128), F32),
            pltpu.VMEM((4, 144, 128), I16),
            pltpu.VMEM((40, 128), F32),
            pltpu.VMEM((40, 128), F32),
            pltpu.VMEM((64, 8, 128), F32),
        ],
        7,
        LARGE,
        "translate_two",
        landed=(2, 4, 5, 6),
    )
    arrived = lax.all_to_all(moved.reshape(32, 16, 128), "space", 0, 0)

    packed, parents_before, parents_after = lax.optimization_barrier((packed, parents_before, parents_after))
    (near_one,) = call(
        parent_kernel,
        [((8, 2, 8, 512), F32)],
        [kind_one, list_one, parents_before, parent, parents_after] + leaf,
        [
            pltpu.SMEM((8, 8), I32),
            pltpu.SMEM((8, 8), I32),
            pltpu.VMEM((128, 512), BF16),
            pltpu.VMEM((128, 512), BF16),
            pltpu.VMEM((24, 2, 8, 512), F32),
            pltpu.VMEM((4, 96, 128), I16),
            pltpu.VMEM((4, 80, 128), F32),
            pltpu.VMEM((8, 2, 8, 512), F32),
        ],
        9,
        SMALL,
        "translate_one",
        landed=(2, 4, 6, 7, 8),
    )

    (lowered,) = call(
        lower_kernel,
        [((528, 128), I16)],
        [arrived, near_one] + list(angles) + [interp_one, interp_two],
        [
            *angle_room,
            pltpu.VMEM((512, 128), F32),
            pltpu.VMEM((2048, 512), F32),
            pltpu.VMEM((32, 16, 128), F32),
            pltpu.VMEM((8, 2, 8, 512), F32),
            pltpu.VMEM((128, 2048), BF16),
            pltpu.VMEM((128, 2048), BF16),
            pltpu.VMEM((512, 128), F32),
            pltpu.VMEM((528, 128), I16),
        ],
        11,
        LARGE,
        "lower",
        landed=(0,),
    )
    shared = [around(lowered, "dir", n_dir, k) for k in (1, 2, 3)]

    (near,) = call(
        near_kernel,
        [((32, 64, 128), F32)],
        [near_list.T, near_count, before, flat, after, near_blocks],
        [
            pltpu.SMEM((6, 32), I32),
            pltpu.SMEM((32,), I32),
            pltpu.VMEM((97, 64, 256), BF16),
            pltpu.VMEM((32, 6, 2, 64, 256), BF16),
            pltpu.VMEM((32, 64, 128), F32),
        ],
        21,
        SMALL,
        "near",
        limit=62,
        landed=(2, 4),
    )
    (fields,) = call(
        receive_kernel,
        [((32, 2, 32, 64), F32)],
        [lowered] + shared + packed + [near],
        [
            pltpu.VMEM((4, 528, 128), I16),
            pltpu.VMEM((4, 1040, 128), I16),
            pltpu.VMEM((4, 8, 2, 4, 8, 128), F32),
            pltpu.VMEM((32, 4, 32, 128), F32),
            pltpu.VMEM((32, 64, 128), F32),
            pltpu.VMEM((32, 2, 32, 64), F32),
        ],
        13,
        LARGE,
        "receive",
        landed=(1, 2, 3, 5, 6, 7),
    )
    return fields


def solution(mesh):
    in_specs = (
        P("space", None, None, None),
        P("space", None, None, "dir", None),
        P("space", None),
        P("space"),
        P("space", None, "dir", None),
        P("space", None, "dir", None),
        P(),
        P(),
        P(),
        P(),
        P(None, None, "dir"),
        P("space", None),
        P("space", None),
        P(None, None, "dir"),
        P(),
        P(),
    )
    out_specs = P("space", None, None, "dir")
    return jax.shard_map(shards, mesh=mesh, in_specs=in_specs, out_specs=out_specs, check_vma=False)
```

```python
import functools

import jax
import jax.numpy as jnp
from jax import lax
from jax.experimental import pallas as pl
from jax.experimental.pallas import tpu as pltpu
from jax.sharding import PartitionSpec as P

F32 = jnp.float32
BF16 = jnp.bfloat16
I32 = jnp.int32
I16 = jnp.int16
IN_HBM = pl.BlockSpec(memory_space=pltpu.HBM)
IN_VMEM = pl.BlockSpec(memory_space=pltpu.VMEM)
ANYWHERE = pl.BlockSpec(memory_space=pl.ANY)
MIB = 1024 * 1024
SMALL = 2**12
LARGE = 2**36


def call(kernel, outs, operands, scratch, copies, cost, name, landed=(), limit=52, kept=()):
    shapes = tuple(jax.ShapeDtypeStruct(shape, kind) for shape, kind in outs)
    return pl.pallas_call(
        kernel,
        out_shape=shapes,
        in_specs=[ANYWHERE if n in landed else IN_HBM for n in range(len(operands))],
        out_specs=tuple(IN_VMEM if n in kept else IN_HBM for n in range(len(outs))),
        scratch_shapes=[*scratch, pltpu.SemaphoreType.DMA((copies,))],
        compiler_params=pltpu.CompilerParams(vmem_limit_bytes=limit * MIB),
        cost_estimate=pl.CostEstimate(flops=cost, bytes_accessed=cost, transcendentals=0),
        name=name,
    )(*operands)


def begin(sems, *pairs, first=0):
    copies = [pltpu.make_async_copy(source, target, sems.at[first + n]) for n, (source, target) in enumerate(pairs)]
    for copy in copies:
        copy.start()
    return copies


def finish(*copies):
    for copy in copies:
        copy.wait()


def rows_by_rows(a, b):
    return lax.dot_general(a, b, (((1,), (1,)), ((), ())), preferred_element_type=F32)


def rows_by_cols(a, b):
    return lax.dot_general(a, b, (((1,), (0,)), ((), ())), preferred_element_type=F32)


def halves(x):
    high = x.astype(BF16)
    return high, (x - high.astype(F32)).astype(BF16)


def product(dot, x, high, low):
    x_high, x_low = halves(x)
    return dot(x_high, high) + (dot(x_high, low) + dot(x_low, high))


def lanes_of(shape):
    return lax.broadcasted_iota(I32, shape, len(shape) - 1)


def swap_half(x):
    return pltpu.roll(x, 64, x.ndim - 1)


def sender(k):
    return lax.rem(lax.axis_index("dir") + 4 - k, 4)


def receiver(k):
    return lax.rem(lax.axis_index("dir") + k, 4)


def power_of(largest):
    return jnp.ceil(jnp.log2(jnp.maximum(largest, 2.0**-100)))


def code_of(scaled):
    return jnp.round(scaled).astype(I32).astype(I16)


def value_of(code):
    return code.astype(I32).astype(F32)


def scale_from(power):
    return jnp.exp2(-power) * 32767.0


def unit_from(power):
    return jnp.exp2(power) * (1.0 / 32767.0)


def unit_of(rows):
    return unit_from(value_of(rows)[0:1])


def leaf_kernel(cur_from, rad_from, one_from, two_from, out0, out1, out2, out3, cur, rad, one, trans, held, codes, sems):
    near_half, far_half = slice(0, 16), slice(16, 32)
    copies = begin(
        sems,
        (cur_from.at[near_half], cur.at[near_half]),
        (rad_from.at[near_half], rad.at[near_half]),
        (cur_from.at[far_half], cur.at[far_half]),
        (rad_from.at[far_half], rad.at[far_half]),
        (one_from, one),
        (two_from, trans),
    )
    lane = lanes_of((32, 128)) // 32
    for p in range(8):
        if p == 0:
            finish(*copies[0:2])
        if p == 4:
            finish(*copies[2:4])
        boxes = cur[4 * p : 4 * p + 4].reshape(256, 256)
        re_rows = rad[4 * p : 4 * p + 4, 0].reshape(128, 256)
        im_rows = rad[4 * p : 4 * p + 4, 1].reshape(128, 256)
        with_re = rows_by_rows(boxes, re_rows)
        with_im = rows_by_rows(boxes, im_rows)
        re = jnp.zeros((32, 128), F32)
        im = jnp.zeros((32, 128), F32)
        for j in range(4):
            a = with_re[64 * j : 64 * j + 64]
            b = with_im[64 * j : 64 * j + 64]
            re = jnp.where(lane == j, a[:32] - b[32:], re)
            im = jnp.where(lane == j, a[32:] + b[:32], im)
        for e in range(4):
            held[e, 16 * p : 16 * p + 8] = re[8 * e : 8 * e + 8]
            held[e, 16 * p + 8 : 16 * p + 16] = im[8 * e : 8 * e + 8]
    finish(*copies[4:6])
    part = lax.rem(lax.axis_index("space"), 8)
    at = pl.ds(pl.multiple_of(part // 2 * 128, 128), 128)
    odd = part % 2
    re = trans[:, 0, at]
    im = trans[:, 1, at]
    lane = lanes_of((40, 128)) < 64
    even_cut = jnp.where(lane, re, swap_half(im))
    odd_cut = jnp.where(lane, swap_half(re), im)
    cut = jnp.where(odd == 1, odd_cut, even_cut)
    cut = jnp.concatenate([cut, jnp.zeros((8, 128), F32)], axis=0)
    table = jnp.concatenate([one[:, 0, :], one[:, 1, :]], axis=0)
    row = lax.broadcasted_iota(I32, (16, 128), 0)
    powers = jnp.zeros((16, 128), F32)
    coded = []
    for n, values in enumerate((held[...], cut, table)):
        flat = jnp.abs(values).reshape(-1, 128)
        power = power_of(jnp.max(flat, keepdims=True))
        powers = jnp.where(row == n, power, powers)
        coded.append(code_of(values.reshape(-1, 128) * scale_from(power)))
    for e in range(4):
        codes[e, 0:128] = coded[0][128 * e : 128 * e + 128]
        codes[e, 128:176] = coded[1]
        codes[e, 176:256] = coded[2]
        codes[e, 256:272] = powers.astype(I32).astype(I16)
    finish(*begin(sems, *[(codes.at[receiver(k)], out) for k, out in enumerate((out0, out1, out2, out3))]))


def pack_kernel(rec_from, one_from, two_from, *refs):
    outs = refs[:4]
    angles_to = refs[4:8]
    rec, one, two, cos1, sin1, cos2, sin2, held, sems = refs[8:]
    copies = begin(
        sems, (one_from, one), (two_from, two), (rec_from.at[0:16], rec.at[0:16]), (rec_from.at[16:32], rec.at[16:32])
    )
    finish(*copies[0:2])
    cos1[...] = jnp.cos(one[...])
    sin1[...] = jnp.sin(one[...])
    cos2[...] = jnp.cos(two[...])
    sin2[...] = jnp.sin(two[...])
    angle_copies = begin(sems, *zip((cos1, sin1, cos2, sin2), angles_to), first=4)
    largest = jnp.zeros((32, 256), F32)
    for t in range(2):
        finish(copies[2 + t])

        def look(b, found):
            return jnp.maximum(found, jnp.maximum(jnp.abs(rec[b, 0]), jnp.abs(rec[b, 1])))

        largest = lax.fori_loop(16 * t, 16 * t + 16, look, largest, unroll=4)
    power = power_of(jnp.max(largest, keepdims=True))
    unit = scale_from(power)
    for e in range(4):
        held[e, 1024:1040] = jnp.broadcast_to(power, (16, 128)).astype(I32).astype(I16)
    lane = lanes_of((32, 128)) < 64

    def body(b, carry):
        rows = pl.ds(pl.multiple_of(b * 32, 32), 32)
        for m in range(2):
            re = rec[b, 0, :, 128 * m : 128 * m + 128] * unit
            im = rec[b, 1, :, 128 * m : 128 * m + 128] * unit
            held[2 * m, rows, :] = code_of(jnp.where(lane, re, swap_half(im)))
            held[2 * m + 1, rows, :] = code_of(jnp.where(lane, swap_half(re), im))
        return carry

    lax.fori_loop(0, 32, body, 0, unroll=4)
    finish(*begin(sems, *[(held.at[receiver(k)], out) for k, out in enumerate(outs)]), *angle_copies)


def lift_kernel(r0, r1, r2, r3, *refs):
    one_from, two_from, *angles_from = refs[:6]
    parent_to, halo_to, message_to = refs[6:9]
    one, two, cos1, sin1, cos2, sin2 = refs[9:15]
    parent, halo, message, codes, held, top, sems = refs[15:]
    copies = begin(
        sems,
        *[(r, codes.at[sender(k)]) for k, r in enumerate((r0, r1, r2, r3))],
        (one_from, one),
        *zip(angles_from, (cos1, sin1, cos2, sin2)),
        *[(two_from.at[512 * t : 512 * t + 512], two.at[512 * t : 512 * t + 512]) for t in range(4)],
    )
    finish(*copies[0:9])
    for e in range(4):
        held[e] = value_of(codes[e, 0:128]) * unit_of(codes[e, 256:272])
    w1h, w1l = halves(one[...])
    lane = lanes_of((128, 128)) // 32
    rows = []
    for j in range(4):
        x = jnp.zeros((128, 128), F32)
        for e in range(4):
            piece = held[e]
            shift = (32 * (e - j)) % 128
            if shift:
                piece = pltpu.roll(piece, shift, 1)
            x = jnp.where(lane == e, piece, x)
        rows.append(x)
    up = product(rows_by_rows, jnp.concatenate(rows, axis=0), w1h, w1l)
    up = up.reshape(4, 8, 2, 8, 512)
    re = jnp.zeros((8, 8, 512), F32)
    im = jnp.zeros((8, 8, 512), F32)
    for j in range(4):
        c = cos1[j : j + 1, :][None]
        s = sin1[j : j + 1, :][None]
        re = re + (c * up[j, :, 0] - s * up[j, :, 1])
        im = im + (c * up[j, :, 1] + s * up[j, :, 0])
    parent[:, 0] = re
    parent[:, 1] = im
    whole = parent[...].reshape(128, 512)
    halo[...] = whole.astype(BF16)
    copies += begin(sems, (parent, parent_to), (halo, halo_to), first=13)
    x_high, x_low = halves(whole)
    for t in range(4):
        finish(copies[9 + t])
        rows = slice(512 * t, 512 * t + 512)
        high, low = halves(two[rows, :])
        part = rows_by_rows(x_high, high) + (rows_by_rows(x_high, low) + rows_by_rows(x_low, high))
        top[:, :, :, :, rows] = part.reshape(2, 4, 2, 8, 512)
    lane = lanes_of((16, 128)) < 64
    for m in range(16):
        at = slice(128 * m, 128 * m + 128)
        re = jnp.zeros((2, 8, 128), F32)
        im = jnp.zeros((2, 8, 128), F32)
        for j in range(4):
            c = cos2[j : j + 1, at][None]
            s = sin2[j : j + 1, at][None]
            u_re = top[:, j, 0, :, at]
            u_im = top[:, j, 1, :, at]
            re = re + (c * u_re - s * u_im)
            im = im + (c * u_im + s * u_re)
        re = re.reshape(16, 128)
        im = im.reshape(16, 128)
        message[2 * m] = jnp.where(lane, re, swap_half(im))
        message[2 * m + 1] = jnp.where(lane, swap_half(re), im)
    copies += begin(sems, (message, message_to), first=15)
    finish(*copies[13:])


def top_kernel(kinds_from, lists_from, top_from, m0, m1, m2, m3, out_to, kinds, lists, top, cuts, first, second, out, sems):
    finish(
        *begin(
            sems,
            (kinds_from, kinds),
            (lists_from, lists),
            (top_from, top),
            *[(m.at[128:272], cuts.at[sender(k)]) for k, m in enumerate((m0, m1, m2, m3))],
        )
    )
    chosen = lax.axis_index("space") // 8
    unit = unit_from(value_of(cuts[chosen, 128:144])[1:2])
    table = (value_of(cuts[chosen, 0:48]) * unit)[0:40]
    lane = lanes_of((40, 128)) < 64
    turned = swap_half(table)
    first[...] = jnp.where(lane, table, turned)
    second[...] = jnp.where(lane, turned, -table)

    def body(g, carry):
        straight = jnp.zeros((8, 128), F32)
        crossed = jnp.zeros((8, 128), F32)
        for k in range(8):
            kind = kinds[k, g]
            value = top[lists[k, g]]
            straight = straight + first[pl.ds(kind, 1), :] * value
            crossed = crossed + second[pl.ds(kind, 1), :] * value
        out[g] = straight + swap_half(crossed)
        return carry

    lax.fori_loop(0, 64, body, 0, unroll=8)
    finish(*begin(sems, (out, out_to)))


def parent_kernel(
    kinds_from, lists_from, before_from, parent_from, after_from, m0, m1, m2, m3,
    out_to,
    kinds, lists, before, after, held, codes, table, out, sems,
):
    finish(
        *begin(
            sems,
            (kinds_from, kinds),
            (lists_from, lists),
            (before_from, before),
            (parent_from, held.at[8:16]),
            (after_from, after),
            *[(m.at[176:272], codes.at[sender(k)]) for k, m in enumerate((m0, m1, m2, m3))],
        )
    )
    base = lax.axis_index("space") * 8 - 8
    for e in range(4):
        table[e] = value_of(codes[e, 0:80]) * unit_from(value_of(codes[e, 80:96])[2:3])
    held[0:8] = before[...].astype(F32).reshape(8, 2, 8, 512)
    held[16:24] = after[...].astype(F32).reshape(8, 2, 8, 512)

    def body(p, carry):
        re = [jnp.zeros((8, 128), F32) for _ in range(4)]
        im = [jnp.zeros((8, 128), F32) for _ in range(4)]
        for k in range(8):
            kind = kinds[p, k]
            source = lists[p, k] - base
            for m in range(4):
                at = slice(128 * m, 128 * m + 128)
                s_re = held[source, 0, :, at]
                s_im = held[source, 1, :, at]
                c_re = table[m, pl.ds(kind, 1), :]
                c_im = table[m, pl.ds(kind + 40, 1), :]
                re[m] = re[m] + (c_re * s_re - c_im * s_im)
                im[m] = im[m] + (c_re * s_im + c_im * s_re)
        for m in range(4):
            at = slice(128 * m, 128 * m + 128)
            out[p, 0, :, at] = re[m]
            out[p, 1, :, at] = im[m]
        return carry

    lax.fori_loop(0, 8, body, 0)
    finish(*begin(sems, (out, out_to)))


def lower_kernel(arrived_from, near_one_from, *refs):
    sources = refs[:6]
    out_to = refs[6]
    cos1, sin1, cos2, sin2, one, two = refs[7:13]
    arrived, near_one, child_high, child_low, held, out, sems = refs[13:]
    copies = begin(
        sems,
        (arrived_from, arrived),
        (near_one_from, near_one),
        *zip(sources[:5], refs[7:12]),
        *[(sources[5].at[512 * t : 512 * t + 512], two.at[512 * t : 512 * t + 512]) for t in range(4)],
    )
    finish(copies[0], *copies[4:6])
    lane = lanes_of((16, 128)) < 64
    for m in range(16):
        at = slice(128 * m, 128 * m + 128)
        a = arrived[2 * m]
        b = arrived[2 * m + 1]
        re = jnp.where(lane, a, swap_half(b)).reshape(2, 8, 128)
        im = jnp.where(lane, swap_half(a), b).reshape(2, 8, 128)
        for j in range(4):
            c = cos2[j : j + 1, at][None]
            s = sin2[j : j + 1, at][None]
            both = jnp.concatenate([(c * re + s * im)[:, None], (c * im - s * re)[:, None]], axis=1)
            high, low = halves(both.reshape(2, 16, 128))
            for g in range(2):
                rows = slice(64 * g + 16 * j, 64 * g + 16 * j + 16)
                child_high[rows, at] = high[g]
                child_low[rows, at] = low[g]
    local = jnp.zeros((128, 512), F32)
    for t in range(4):
        finish(copies[7 + t])
        at = slice(512 * t, 512 * t + 512)
        high = child_high[:, at]
        w2h, w2l = halves(two[at, :])
        local = local + (rows_by_cols(high, w2h) + (rows_by_cols(high, w2l) + rows_by_cols(child_low[:, at], w2h)))
    finish(*copies[1:4], copies[6])
    w1h, w1l = halves(one[...])
    local = local.reshape(8, 2, 8, 512) + near_one[...]
    re = local[:, 0]
    im = local[:, 1]
    for j in range(4):
        c = cos1[j : j + 1, :][None]
        s = sin1[j : j + 1, :][None]
        both = jnp.concatenate([(c * re + s * im)[:, None], (c * im - s * re)[:, None]], axis=1)
        down = product(rows_by_cols, both.reshape(128, 512), w1h, w1l)
        held[128 * j : 128 * j + 128] = down
    largest = jnp.max(jnp.abs(held[...]), keepdims=True)
    power = power_of(largest)
    out[0:512] = code_of(held[...] * scale_from(power))
    out[512:528] = jnp.broadcast_to(power, (16, 128)).astype(I32).astype(I16)
    finish(*begin(sems, (out, out_to)))


def near_kernel(half, lists_from, counts_from, before, current, after, blocks_from, out_to, lists, counts, held, blocks, out, sems):
    if half == 0:
        sources = [(before, held.at[0:32]), (after.at[0:16], held.at[64:80])]
    else:
        sources = [(before.at[16:32], held.at[16:32]), (after, held.at[64:96])]
    copies = begin(
        sems,
        (lists_from, lists),
        (counts_from, counts),
        (current, held.at[32:64]),
        *sources,
        *[
            (blocks_from.at[16 * half + 4 * t : 16 * half + 4 * t + 4], blocks.at[4 * t : 4 * t + 4])
            for t in range(4)
        ],
    )
    held[96] = jnp.zeros((64, 256), BF16)
    finish(*copies[0:5])
    base = lax.axis_index("space") * 32 - 32

    for t in range(4):
        finish(copies[5 + t])

        def body(n, carry):
            for row in (4 * t + 2 * n, 4 * t + 2 * n + 1):
                box = 16 * half + row
                total = jnp.zeros((64, 128), F32)
                for k in range(6):
                    source = jnp.where(k < counts[box], lists[k, box] - base, 96)
                    total = total + rows_by_rows(held[source], blocks[row, k].reshape(128, 256))
                out[row] = total
            return carry

        lax.fori_loop(0, 2, body, 0, unroll=2)
        copies += begin(sems, (out.at[4 * t : 4 * t + 4], out_to.at[4 * t : 4 * t + 4]), first=9 + t)
    finish(*copies[9:])


def receive_kernel(l0, l1, l2, l3, x0, x1, x2, x3, near_first, near_second, out_to, codes, packs, samples, matrix, near, out, sems):
    copies = begin(
        sems,
        *[(l, codes.at[k]) for k, l in enumerate((l0, l1, l2, l3))],
        *[(x, packs.at[k]) for k, x in enumerate((x0, x1, x2, x3))],
        (near_first, near.at[0:16]),
        (near_second, near.at[16:32]),
    )
    finish(*copies[0:4])
    for k in range(4):
        values = value_of(codes[k, 0:512]) * unit_of(codes[k, 512:528])
        samples[:, :, :, sender(k)] = values.reshape(4, 8, 2, 8, 128)
    finish(*copies[4:10])
    units = [unit_of(packs[k, 1024:1040]) for k in range(4)]

    def body(p, carry):
        for j in range(4):
            b = 4 * p + j
            rows = pl.ds(pl.multiple_of(32 * b, 32), 32)
            for k in range(4):
                matrix[b, sender(k)] = value_of(packs[k, rows, :]) * units[k]
            left_high, left_low = halves(samples[j, p].reshape(64, 128))
            high, low = halves(matrix[b].reshape(128, 128))
            left = jnp.concatenate([left_high, left_low], axis=1)
            right = jnp.concatenate(
                [jnp.concatenate([high, low], axis=1), jnp.concatenate([high, jnp.zeros_like(low)], axis=1)], axis=0
            )
            both = rows_by_cols(left, right)
            total = near[b] + (both[:, :128] + both[:, 128:])
            turned = swap_half(total)
            out[b, 0] = (total[:32] - turned[32:])[:, :64]
            out[b, 1] = (total[32:] + turned[:32])[:, :64]
        return carry

    for t in range(4):
        lax.fori_loop(2 * t, 2 * t + 2, body, 0, unroll=2)
        part = slice(8 * t, 8 * t + 8)
        copies += begin(sems, (out.at[part], out_to.at[part]), first=10 + t)
    finish(*copies[10:])


def near_half(half, *operands):
    return call(
        functools.partial(near_kernel, half),
        [((16, 64, 128), F32)],
        list(operands),
        [
            pltpu.SMEM((6, 32), I32),
            pltpu.SMEM((32,), I32),
            pltpu.VMEM((97, 64, 256), BF16),
            pltpu.VMEM((16, 6, 2, 64, 256), BF16),
            pltpu.VMEM((16, 64, 128), F32),
        ],
        13,
        SMALL,
        "near",
        limit=60,
        landed=(2, 4),
    )[0]


def around(x, axis, peers, k):
    return lax.ppermute(x, axis, [(i, (i + k) % peers) for i in range(peers)])


def after_all(values, *tokens):
    return lax.optimization_barrier((*values, *tokens))[: len(values)]


def shards(
    currents,
    near_blocks,
    near_list,
    near_count,
    radiate,
    receive,
    phase_one,
    phase_two,
    interp_one,
    interp_two,
    trans_one,
    kind_one,
    list_one,
    trans_two,
    kind_two,
    list_two,
):
    n_space = lax.axis_size("space")
    n_dir = lax.axis_size("dir")
    up = [(i, i + 1) for i in range(n_space - 1)]
    down = [(i + 1, i) for i in range(n_space - 1)]

    flat = currents.reshape(32, 64, 256)
    before = lax.ppermute(flat, "space", up)
    after = lax.ppermute(flat, "space", down)

    leaf = call(
        leaf_kernel,
        [((272, 128), I16)] * 4,
        [currents, radiate, trans_one, trans_two],
        [
            pltpu.VMEM((32, 2, 32, 256), BF16),
            pltpu.VMEM((32, 2, 32, 256), BF16),
            pltpu.VMEM((40, 2, 128), F32),
            pltpu.VMEM((40, 2, 512), F32),
            pltpu.VMEM((4, 128, 128), F32),
            pltpu.VMEM((4, 272, 128), I16),
        ],
        6,
        LARGE,
        "leaf",
        limit=60,
        kept=(0,),
    )
    own_leaf = leaf[0]
    leaf = [own_leaf] + [around(leaf[k], "dir", n_dir, k) for k in (1, 2, 3)]
    angle_room = [*[pltpu.VMEM((4, 512), F32)] * 2, *[pltpu.VMEM((4, 2048), F32)] * 2]
    packed = call(
        pack_kernel,
        [((1040, 128), I16)] * 4 + [((4, 512), F32)] * 2 + [((4, 2048), F32)] * 2,
        list(after_all((receive, phase_one, phase_two), own_leaf)),
        [
            pltpu.VMEM((32, 2, 32, 256), F32),
            pltpu.VMEM((4, 512), F32),
            pltpu.VMEM((4, 2048), F32),
            *angle_room,
            pltpu.VMEM((4, 1040, 128), I16),
        ],
        8,
        SMALL,
        "pack",
    )
    packed, angles = packed[:4], packed[4:]
    leaf, packed, before, after = lax.optimization_barrier((leaf, packed, before, after))
    packed = [packed[0]] + [around(packed[k], "dir", n_dir, k) for k in (1, 2, 3)]


    parent, halo, message = call(
        lift_kernel,
        [((8, 2, 8, 512), F32), ((128, 512), BF16), ((32, 16, 128), F32)],
        leaf + [interp_one, interp_two] + list(angles),
        [
            pltpu.VMEM((512, 128), F32),
            pltpu.VMEM((2048, 512), F32),
            *angle_room,
            pltpu.VMEM((8, 2, 8, 512), F32),
            pltpu.VMEM((128, 512), BF16),
            pltpu.VMEM((32, 16, 128), F32),
            pltpu.VMEM((4, 272, 128), I16),
            pltpu.VMEM((4, 128, 128), F32),
            pltpu.VMEM((2, 4, 2, 8, 2048), F32),
        ],
        16,
        LARGE,
        "lift",
        landed=(0, 1, 2, 3),
    )
    top = lax.all_to_all(message, "space", 0, 0)
    parents_before = lax.ppermute(halo, "space", up)
    parents_after = lax.ppermute(halo, "space", down)

    top, parents_before, parents_after = lax.optimization_barrier((top, parents_before, parents_after))
    (moved,) = call(
        top_kernel,
        [((64, 8, 128), F32)],
        [kind_two.T, list_two.T, top.reshape(64, 8, 128)] + leaf,
        [
            pltpu.SMEM((8, 64), I32),
            pltpu.SMEM((8, 64), I32),
            pltpu.VMEM((64, 8, 128), F32),
            pltpu.VMEM((4, 144, 128), I16),
            pltpu.VMEM((40, 128), F32),
            pltpu.VMEM((40, 128), F32),
            pltpu.VMEM((64, 8, 128), F32),
        ],
        7,
        LARGE,
        "translate_two",
        landed=(2, 3, 4, 5, 6),
    )
    arrived = lax.all_to_all(moved.reshape(32, 16, 128), "space", 0, 0)

    near_parts = [near_half(half, near_list.T, near_count, before, flat, after, near_blocks) for half in (0, 1)]
    (near_one,) = call(
        parent_kernel,
        [((8, 2, 8, 512), F32)],
        [kind_one, list_one, parents_before, parent, parents_after] + leaf,
        [
            pltpu.SMEM((8, 8), I32),
            pltpu.SMEM((8, 8), I32),
            pltpu.VMEM((128, 512), BF16),
            pltpu.VMEM((128, 512), BF16),
            pltpu.VMEM((24, 2, 8, 512), F32),
            pltpu.VMEM((4, 96, 128), I16),
            pltpu.VMEM((4, 80, 128), F32),
            pltpu.VMEM((8, 2, 8, 512), F32),
        ],
        9,
        SMALL,
        "translate_one",
        landed=(2, 4, 5, 6, 7, 8),
    )

    arrived, near_one, near_parts[0] = lax.optimization_barrier((arrived, near_one, near_parts[0]))
    (lowered,) = call(
        lower_kernel,
        [((528, 128), I16)],
        [arrived, near_one] + list(angles) + [interp_one, interp_two],
        [
            *angle_room,
            pltpu.VMEM((512, 128), F32),
            pltpu.VMEM((2048, 512), F32),
            pltpu.VMEM((32, 16, 128), F32),
            pltpu.VMEM((8, 2, 8, 512), F32),
            pltpu.VMEM((128, 2048), BF16),
            pltpu.VMEM((128, 2048), BF16),
            pltpu.VMEM((512, 128), F32),
            pltpu.VMEM((528, 128), I16),
        ],
        11,
        LARGE,
        "lower",
        landed=(0,),
    )
    shared = [around(lowered, "dir", n_dir, k) for k in (1, 2, 3)]

    (fields,) = call(
        receive_kernel,
        [((32, 2, 32, 64), F32)],
        [lowered] + shared + packed + near_parts,
        [
            pltpu.VMEM((4, 528, 128), I16),
            pltpu.VMEM((4, 1040, 128), I16),
            pltpu.VMEM((4, 8, 2, 4, 8, 128), F32),
            pltpu.VMEM((32, 4, 32, 128), F32),
            pltpu.VMEM((32, 64, 128), F32),
            pltpu.VMEM((32, 2, 32, 64), F32),
        ],
        14,
        LARGE,
        "receive",
        landed=(1, 2, 3, 5, 6, 7),
    )
    return fields


def solution(mesh):
    in_specs = (
        P("space", None, None, None),
        P("space", None, None, "dir", None),
        P("space", None),
        P("space"),
        P("space", None, "dir", None),
        P("space", None, "dir", None),
        P(),
        P(),
        P(),
        P(),
        P(None, None, "dir"),
        P("space", None),
        P("space", None),
        P(None, None, "dir"),
        P(),
        P(),
    )
    out_specs = P("space", None, None, "dir")
    return jax.shard_map(shards, mesh=mesh, in_specs=in_specs, out_specs=out_specs, check_vma=False)
```

```python
import jax
import jax.numpy as jnp
from jax import lax
from jax.experimental import pallas as pl
from jax.experimental.pallas import tpu as pltpu
from jax.sharding import PartitionSpec as P

F32 = jnp.float32
BF16 = jnp.bfloat16
I32 = jnp.int32
I16 = jnp.int16
IN_HBM = pl.BlockSpec(memory_space=pltpu.HBM)
ANYWHERE = pl.BlockSpec(memory_space=pl.ANY)
MIB = 1024 * 1024
SMALL = 2**12
LARGE = 2**36


def call(kernel, outs, operands, scratch, copies, cost, name, landed=(), limit=52):
    shapes = tuple(jax.ShapeDtypeStruct(shape, kind) for shape, kind in outs)
    return pl.pallas_call(
        kernel,
        out_shape=shapes,
        in_specs=[ANYWHERE if n in landed else IN_HBM for n in range(len(operands))],
        out_specs=tuple(IN_HBM for _ in outs),
        scratch_shapes=[*scratch, pltpu.SemaphoreType.DMA((copies,))],
        compiler_params=pltpu.CompilerParams(vmem_limit_bytes=limit * MIB),
        cost_estimate=pl.CostEstimate(flops=cost, bytes_accessed=cost, transcendentals=0),
        name=name,
    )(*operands)


def begin(sems, *pairs, first=0):
    copies = [pltpu.make_async_copy(source, target, sems.at[first + n]) for n, (source, target) in enumerate(pairs)]
    for copy in copies:
        copy.start()
    return copies


def finish(*copies):
    for copy in copies:
        copy.wait()


def rows_by_rows(a, b):
    return lax.dot_general(a, b, (((1,), (1,)), ((), ())), preferred_element_type=F32)


def rows_by_cols(a, b):
    return lax.dot_general(a, b, (((1,), (0,)), ((), ())), preferred_element_type=F32)


def halves(x):
    high = x.astype(BF16)
    return high, (x - high.astype(F32)).astype(BF16)


def product(dot, x, high, low):
    x_high, x_low = halves(x)
    return dot(x_high, high) + (dot(x_high, low) + dot(x_low, high))


def lanes_of(shape):
    return lax.broadcasted_iota(I32, shape, len(shape) - 1)


def swap_half(x):
    return pltpu.roll(x, 64, x.ndim - 1)


def sender(k):
    return lax.rem(lax.axis_index("dir") + 4 - k, 4)


def receiver(k):
    return lax.rem(lax.axis_index("dir") + k, 4)


def power_of(largest):
    return jnp.ceil(jnp.log2(jnp.maximum(largest, 2.0**-100)))


def code_of(scaled):
    return jnp.round(scaled).astype(I32).astype(I16)


def value_of(code):
    return code.astype(I32).astype(F32)


def scale_from(power):
    return jnp.exp2(-power) * 32767.0


def unit_from(power):
    return jnp.exp2(power) * (1.0 / 32767.0)


def unit_of(rows):
    return unit_from(value_of(rows)[0:1])


def leaf_kernel(cur_from, rad_from, one_from, two_from, out0, out1, out2, out3, cur, rad, one, trans, held, codes, sems):
    near_half, far_half = slice(0, 16), slice(16, 32)
    copies = begin(
        sems,
        (cur_from.at[near_half], cur.at[near_half]),
        (rad_from.at[near_half], rad.at[near_half]),
        (cur_from.at[far_half], cur.at[far_half]),
        (rad_from.at[far_half], rad.at[far_half]),
        (one_from, one),
        (two_from, trans),
    )
    lane = lanes_of((32, 128)) // 32
    for p in range(8):
        if p == 0:
            finish(*copies[0:2])
        if p == 4:
            finish(*copies[2:4])
        boxes = cur[4 * p : 4 * p + 4].reshape(256, 256)
        re_rows = rad[4 * p : 4 * p + 4, 0].reshape(128, 256)
        im_rows = rad[4 * p : 4 * p + 4, 1].reshape(128, 256)
        with_re = rows_by_rows(boxes, re_rows)
        with_im = rows_by_rows(boxes, im_rows)
        re = jnp.zeros((32, 128), F32)
        im = jnp.zeros((32, 128), F32)
        for j in range(4):
            a = with_re[64 * j : 64 * j + 64]
            b = with_im[64 * j : 64 * j + 64]
            re = jnp.where(lane == j, a[:32] - b[32:], re)
            im = jnp.where(lane == j, a[32:] + b[:32], im)
        for e in range(4):
            held[e, 16 * p : 16 * p + 8] = re[8 * e : 8 * e + 8]
            held[e, 16 * p + 8 : 16 * p + 16] = im[8 * e : 8 * e + 8]
    finish(*copies[4:6])
    part = lax.rem(lax.axis_index("space"), 8)
    at = pl.ds(pl.multiple_of(part // 2 * 128, 128), 128)
    odd = part % 2
    re = trans[:, 0, at]
    im = trans[:, 1, at]
    lane = lanes_of((40, 128)) < 64
    even_cut = jnp.where(lane, re, swap_half(im))
    odd_cut = jnp.where(lane, swap_half(re), im)
    cut = jnp.where(odd == 1, odd_cut, even_cut)
    cut = jnp.concatenate([cut, jnp.zeros((8, 128), F32)], axis=0)
    table = jnp.concatenate([one[:, 0, :], one[:, 1, :]], axis=0)
    row = lax.broadcasted_iota(I32, (16, 128), 0)
    powers = jnp.zeros((16, 128), F32)
    coded = []
    for n, values in enumerate((held[...], cut, table)):
        flat = jnp.abs(values).reshape(-1, 128)
        power = power_of(jnp.max(flat, keepdims=True))
        powers = jnp.where(row == n, power, powers)
        coded.append(code_of(values.reshape(-1, 128) * scale_from(power)))
    for e in range(4):
        codes[e, 0:128] = coded[0][128 * e : 128 * e + 128]
        codes[e, 128:176] = coded[1]
        codes[e, 176:256] = coded[2]
        codes[e, 256:272] = powers.astype(I32).astype(I16)
    finish(*begin(sems, *[(codes.at[receiver(k)], out) for k, out in enumerate((out0, out1, out2, out3))]))


def pack_kernel(rec_from, one_from, two_from, *refs):
    outs = refs[:4]
    angles_to = refs[4:8]
    rec, one, two, cos1, sin1, cos2, sin2, held, sems = refs[8:]
    copies = begin(
        sems, (one_from, one), (two_from, two), (rec_from.at[0:16], rec.at[0:16]), (rec_from.at[16:32], rec.at[16:32])
    )
    finish(*copies[0:2])
    cos1[...] = jnp.cos(one[...])
    sin1[...] = jnp.sin(one[...])
    cos2[...] = jnp.cos(two[...])
    sin2[...] = jnp.sin(two[...])
    angle_copies = begin(sems, *zip((cos1, sin1, cos2, sin2), angles_to), first=4)
    largest = jnp.zeros((32, 256), F32)
    for t in range(2):
        finish(copies[2 + t])

        def look(b, found):
            return jnp.maximum(found, jnp.maximum(jnp.abs(rec[b, 0]), jnp.abs(rec[b, 1])))

        largest = lax.fori_loop(16 * t, 16 * t + 16, look, largest, unroll=4)
    power = power_of(jnp.max(largest, keepdims=True))
    unit = scale_from(power)
    for e in range(4):
        held[e, 1024:1040] = jnp.broadcast_to(power, (16, 128)).astype(I32).astype(I16)
    lane = lanes_of((32, 128)) < 64

    def body(b, carry):
        rows = pl.ds(pl.multiple_of(b * 32, 32), 32)
        for m in range(2):
            re = rec[b, 0, :, 128 * m : 128 * m + 128] * unit
            im = rec[b, 1, :, 128 * m : 128 * m + 128] * unit
            held[2 * m, rows, :] = code_of(jnp.where(lane, re, swap_half(im)))
            held[2 * m + 1, rows, :] = code_of(jnp.where(lane, swap_half(re), im))
        return carry

    lax.fori_loop(0, 32, body, 0, unroll=4)
    finish(*begin(sems, *[(held.at[receiver(k)], out) for k, out in enumerate(outs)]), *angle_copies)


def lift_kernel(r0, r1, r2, r3, *refs):
    one_from, two_from, *angles_from = refs[:6]
    parent_to, halo_to, message_to = refs[6:9]
    one, two, cos1, sin1, cos2, sin2 = refs[9:15]
    parent, halo, message, codes, held, top, sems = refs[15:]
    copies = begin(
        sems,
        *[(r, codes.at[sender(k)]) for k, r in enumerate((r0, r1, r2, r3))],
        (one_from, one),
        *zip(angles_from, (cos1, sin1, cos2, sin2)),
        *[(two_from.at[512 * t : 512 * t + 512], two.at[512 * t : 512 * t + 512]) for t in range(4)],
    )
    finish(*copies[0:9])
    for e in range(4):
        held[e] = value_of(codes[e, 0:128]) * unit_of(codes[e, 256:272])
    w1h, w1l = halves(one[...])
    lane = lanes_of((128, 128)) // 32
    rows = []
    for j in range(4):
        x = jnp.zeros((128, 128), F32)
        for e in range(4):
            piece = held[e]
            shift = (32 * (e - j)) % 128
            if shift:
                piece = pltpu.roll(piece, shift, 1)
            x = jnp.where(lane == e, piece, x)
        rows.append(x)
    up = product(rows_by_rows, jnp.concatenate(rows, axis=0), w1h, w1l)
    up = up.reshape(4, 8, 2, 8, 512)
    re = jnp.zeros((8, 8, 512), F32)
    im = jnp.zeros((8, 8, 512), F32)
    for j in range(4):
        c = cos1[j : j + 1, :][None]
        s = sin1[j : j + 1, :][None]
        re = re + (c * up[j, :, 0] - s * up[j, :, 1])
        im = im + (c * up[j, :, 1] + s * up[j, :, 0])
    parent[:, 0] = re
    parent[:, 1] = im
    whole = parent[...].reshape(128, 512)
    halo[...] = whole.astype(BF16)
    copies += begin(sems, (parent, parent_to), (halo, halo_to), first=13)
    x_high, x_low = halves(whole)
    for t in range(4):
        finish(copies[9 + t])
        rows = slice(512 * t, 512 * t + 512)
        high, low = halves(two[rows, :])
        part = rows_by_rows(x_high, high) + (rows_by_rows(x_high, low) + rows_by_rows(x_low, high))
        top[:, :, :, :, rows] = part.reshape(2, 4, 2, 8, 512)
    lane = lanes_of((16, 128)) < 64
    for m in range(16):
        at = slice(128 * m, 128 * m + 128)
        re = jnp.zeros((2, 8, 128), F32)
        im = jnp.zeros((2, 8, 128), F32)
        for j in range(4):
            c = cos2[j : j + 1, at][None]
            s = sin2[j : j + 1, at][None]
            u_re = top[:, j, 0, :, at]
            u_im = top[:, j, 1, :, at]
            re = re + (c * u_re - s * u_im)
            im = im + (c * u_im + s * u_re)
        re = re.reshape(16, 128)
        im = im.reshape(16, 128)
        message[2 * m] = jnp.where(lane, re, swap_half(im))
        message[2 * m + 1] = jnp.where(lane, swap_half(re), im)
    copies += begin(sems, (message, message_to), first=15)
    finish(*copies[13:])


def top_kernel(kinds_from, lists_from, top_from, m0, m1, m2, m3, out_to, kinds, lists, top, cuts, first, second, out, sems):
    finish(
        *begin(
            sems,
            (kinds_from, kinds),
            (lists_from, lists),
            (top_from, top),
            *[(m.at[128:272], cuts.at[sender(k)]) for k, m in enumerate((m0, m1, m2, m3))],
        )
    )
    chosen = lax.axis_index("space") // 8
    unit = unit_from(value_of(cuts[chosen, 128:144])[1:2])
    table = (value_of(cuts[chosen, 0:48]) * unit)[0:40]
    lane = lanes_of((40, 128)) < 64
    turned = swap_half(table)
    first[...] = jnp.where(lane, table, turned)
    second[...] = jnp.where(lane, turned, -table)

    def body(g, carry):
        straight = jnp.zeros((8, 128), F32)
        crossed = jnp.zeros((8, 128), F32)
        for k in range(8):
            kind = kinds[k, g]
            value = top[lists[k, g]]
            straight = straight + first[pl.ds(kind, 1), :] * value
            crossed = crossed + second[pl.ds(kind, 1), :] * value
        out[g] = straight + swap_half(crossed)
        return carry

    lax.fori_loop(0, 64, body, 0, unroll=8)
    finish(*begin(sems, (out, out_to)))


def parent_kernel(
    kinds_from, lists_from, inner_from, parent_from, outer_from, m0, m1, m2, m3,
    out_to,
    kinds, lists, inner, outer, held, codes, table, out, sems,
):
    finish(
        *begin(
            sems,
            (kinds_from, kinds),
            (lists_from, lists),
            (inner_from, inner),
            (parent_from, held.at[8:16]),
            (outer_from, outer),
            *[(m.at[176:272], codes.at[sender(k)]) for k, m in enumerate((m0, m1, m2, m3))],
        )
    )
    base = lax.axis_index("space") * 8 - 8
    for e in range(4):
        table[e] = value_of(codes[e, 0:80]) * unit_from(value_of(codes[e, 80:96])[2:3])
    odd = lax.rem(lax.axis_index("space"), 2)
    held[pl.ds(16 - 16 * odd, 8)] = inner[...].astype(F32).reshape(8, 2, 8, 512)
    held[pl.ds(16 * odd, 8)] = outer[...].astype(F32).reshape(8, 2, 8, 512)

    def body(p, carry):
        re = [jnp.zeros((8, 128), F32) for _ in range(4)]
        im = [jnp.zeros((8, 128), F32) for _ in range(4)]
        for k in range(8):
            kind = kinds[p, k]
            source = lists[p, k] - base
            for m in range(4):
                at = slice(128 * m, 128 * m + 128)
                s_re = held[source, 0, :, at]
                s_im = held[source, 1, :, at]
                c_re = table[m, pl.ds(kind, 1), :]
                c_im = table[m, pl.ds(kind + 40, 1), :]
                re[m] = re[m] + (c_re * s_re - c_im * s_im)
                im[m] = im[m] + (c_re * s_im + c_im * s_re)
        for m in range(4):
            at = slice(128 * m, 128 * m + 128)
            out[p, 0, :, at] = re[m]
            out[p, 1, :, at] = im[m]
        return carry

    lax.fori_loop(0, 8, body, 0)
    finish(*begin(sems, (out, out_to)))


def lower_kernel(arrived_from, near_one_from, *refs):
    sources = refs[:6]
    out_to = refs[6]
    cos1, sin1, cos2, sin2, one, two = refs[7:13]
    arrived, near_one, child_high, child_low, held, out, sems = refs[13:]
    copies = begin(
        sems,
        (arrived_from, arrived),
        (near_one_from, near_one),
        *zip(sources[:5], refs[7:12]),
        *[(sources[5].at[512 * t : 512 * t + 512], two.at[512 * t : 512 * t + 512]) for t in range(4)],
    )
    finish(copies[0], *copies[4:6])
    lane = lanes_of((16, 128)) < 64
    for m in range(16):
        at = slice(128 * m, 128 * m + 128)
        a = arrived[2 * m]
        b = arrived[2 * m + 1]
        re = jnp.where(lane, a, swap_half(b)).reshape(2, 8, 128)
        im = jnp.where(lane, swap_half(a), b).reshape(2, 8, 128)
        for j in range(4):
            c = cos2[j : j + 1, at][None]
            s = sin2[j : j + 1, at][None]
            both = jnp.concatenate([(c * re + s * im)[:, None], (c * im - s * re)[:, None]], axis=1)
            high, low = halves(both.reshape(2, 16, 128))
            for g in range(2):
                rows = slice(64 * g + 16 * j, 64 * g + 16 * j + 16)
                child_high[rows, at] = high[g]
                child_low[rows, at] = low[g]
    local = jnp.zeros((128, 512), F32)
    for t in range(4):
        finish(copies[7 + t])
        at = slice(512 * t, 512 * t + 512)
        high = child_high[:, at]
        w2h, w2l = halves(two[at, :])
        local = local + (rows_by_cols(high, w2h) + (rows_by_cols(high, w2l) + rows_by_cols(child_low[:, at], w2h)))
    finish(*copies[1:4], copies[6])
    w1h, w1l = halves(one[...])
    local = local.reshape(8, 2, 8, 512) + near_one[...]
    re = local[:, 0]
    im = local[:, 1]
    for j in range(4):
        c = cos1[j : j + 1, :][None]
        s = sin1[j : j + 1, :][None]
        both = jnp.concatenate([(c * re + s * im)[:, None], (c * im - s * re)[:, None]], axis=1)
        down = product(rows_by_cols, both.reshape(128, 512), w1h, w1l)
        held[128 * j : 128 * j + 128] = down
    largest = jnp.max(jnp.abs(held[...]), keepdims=True)
    power = power_of(largest)
    out[0:512] = code_of(held[...] * scale_from(power))
    out[512:528] = jnp.broadcast_to(power, (16, 128)).astype(I32).astype(I16)
    finish(*begin(sems, (out, out_to)))


def near_kernel(lists_from, counts_from, inner, current, outer, blocks_from, out_to, lists, counts, held, blocks, out, sems):
    odd = lax.rem(lax.axis_index("space"), 2)
    copies = begin(
        sems,
        (lists_from, lists),
        (counts_from, counts),
        (inner, held.at[pl.ds(64 - 64 * odd, 32)]),
        (current, held.at[32:64]),
        (outer, held.at[pl.ds(64 * odd, 32)]),
        *[(blocks_from.at[4 * t : 4 * t + 4], blocks.at[4 * t : 4 * t + 4]) for t in range(8)],
    )
    held[96] = jnp.zeros((64, 256), BF16)
    finish(*copies[0:5])
    base = lax.axis_index("space") * 32 - 32

    for t in range(8):
        finish(copies[5 + t])

        def body(n, carry):
            for box in (4 * t + 2 * n, 4 * t + 2 * n + 1):
                total = jnp.zeros((64, 128), F32)
                for k in range(6):
                    source = jnp.where(k < counts[box], lists[k, box] - base, 96)
                    total = total + rows_by_rows(held[source], blocks[box, k].reshape(128, 256))
                out[box] = total
            return carry

        lax.fori_loop(0, 2, body, 0, unroll=2)
        copies += begin(sems, (out.at[4 * t : 4 * t + 4], out_to.at[4 * t : 4 * t + 4]), first=13 + t)
    finish(*copies[13:])


def receive_kernel(l0, l1, l2, l3, x0, x1, x2, x3, near_from, out_to, codes, packs, samples, matrix, near, out, sems):
    copies = begin(
        sems,
        *[(l, codes.at[k]) for k, l in enumerate((l0, l1, l2, l3))],
        *[(x, packs.at[k]) for k, x in enumerate((x0, x1, x2, x3))],
        (near_from, near),
    )
    finish(*copies[0:4])
    for k in range(4):
        values = value_of(codes[k, 0:512]) * unit_of(codes[k, 512:528])
        samples[:, :, :, sender(k)] = values.reshape(4, 8, 2, 8, 128)
    finish(*copies[4:9])
    units = [unit_of(packs[k, 1024:1040]) for k in range(4)]

    def body(p, carry):
        for j in range(4):
            b = 4 * p + j
            rows = pl.ds(pl.multiple_of(32 * b, 32), 32)
            for k in range(4):
                matrix[b, sender(k)] = value_of(packs[k, rows, :]) * units[k]
            left_high, left_low = halves(samples[j, p].reshape(64, 128))
            high, low = halves(matrix[b].reshape(128, 128))
            left = jnp.concatenate([left_high, left_low], axis=1)
            right = jnp.concatenate(
                [jnp.concatenate([high, low], axis=1), jnp.concatenate([high, jnp.zeros_like(low)], axis=1)], axis=0
            )
            both = rows_by_cols(left, right)
            total = near[b] + (both[:, :128] + both[:, 128:])
            turned = swap_half(total)
            out[b, 0] = (total[:32] - turned[32:])[:, :64]
            out[b, 1] = (total[32:] + turned[:32])[:, :64]
        return carry

    for t in range(4):
        lax.fori_loop(2 * t, 2 * t + 2, body, 0, unroll=2)
        part = slice(8 * t, 8 * t + 8)
        copies += begin(sems, (out.at[part], out_to.at[part]), first=9 + t)
    finish(*copies[9:])


def around(x, axis, peers, k):
    return lax.ppermute(x, axis, [(i, (i + k) % peers) for i in range(peers)])


def after_all(values, *tokens):
    return lax.optimization_barrier((*values, *tokens))[: len(values)]


def shards(
    currents,
    near_blocks,
    near_list,
    near_count,
    radiate,
    receive,
    phase_one,
    phase_two,
    interp_one,
    interp_two,
    trans_one,
    kind_one,
    list_one,
    trans_two,
    kind_two,
    list_two,
):
    n_space = lax.axis_size("space")
    n_dir = lax.axis_size("dir")
    first_swap = [(i ^ 1, i) for i in range(n_space)]
    second_swap = [(i, j) for k in range(1, n_space - 1, 2) for i, j in ((k, k + 1), (k + 1, k))]

    flat = currents.reshape(32, 64, 256)
    inner = lax.ppermute(flat, "space", first_swap)
    outer = lax.ppermute(flat, "space", second_swap)

    leaf = call(
        leaf_kernel,
        [((272, 128), I16)] * 4,
        [currents, radiate, trans_one, trans_two],
        [
            pltpu.VMEM((32, 2, 32, 256), BF16),
            pltpu.VMEM((32, 2, 32, 256), BF16),
            pltpu.VMEM((40, 2, 128), F32),
            pltpu.VMEM((40, 2, 512), F32),
            pltpu.VMEM((4, 128, 128), F32),
            pltpu.VMEM((4, 272, 128), I16),
        ],
        6,
        LARGE,
        "leaf",
        limit=62,
    )
    own_leaf = leaf[0]
    leaf = [own_leaf] + [around(leaf[k], "dir", n_dir, k) for k in (1, 2, 3)]
    angle_room = [*[pltpu.VMEM((4, 512), F32)] * 2, *[pltpu.VMEM((4, 2048), F32)] * 2]
    packed = call(
        pack_kernel,
        [((1040, 128), I16)] * 4 + [((4, 512), F32)] * 2 + [((4, 2048), F32)] * 2,
        list(after_all((receive, phase_one, phase_two), own_leaf)),
        [
            pltpu.VMEM((32, 2, 32, 256), F32),
            pltpu.VMEM((4, 512), F32),
            pltpu.VMEM((4, 2048), F32),
            *angle_room,
            pltpu.VMEM((4, 1040, 128), I16),
        ],
        8,
        SMALL,
        "pack",
    )
    packed, angles = packed[:4], packed[4:]
    leaf, packed = lax.optimization_barrier((leaf, packed))
    packed = [packed[0]] + [around(packed[k], "dir", n_dir, k) for k in (1, 2, 3)]


    parent, halo, message = call(
        lift_kernel,
        [((8, 2, 8, 512), F32), ((128, 512), BF16), ((32, 16, 128), F32)],
        leaf + [interp_one, interp_two] + list(angles),
        [
            pltpu.VMEM((512, 128), F32),
            pltpu.VMEM((2048, 512), F32),
            *angle_room,
            pltpu.VMEM((8, 2, 8, 512), F32),
            pltpu.VMEM((128, 512), BF16),
            pltpu.VMEM((32, 16, 128), F32),
            pltpu.VMEM((4, 272, 128), I16),
            pltpu.VMEM((4, 128, 128), F32),
            pltpu.VMEM((2, 4, 2, 8, 2048), F32),
        ],
        16,
        LARGE,
        "lift",
        landed=(1, 2, 3),
    )
    top = lax.all_to_all(message, "space", 0, 0)
    parents_inner = lax.ppermute(halo, "space", first_swap)
    parents_outer = lax.ppermute(halo, "space", second_swap)

    top, inner, outer = lax.optimization_barrier((top, inner, outer))
    (moved,) = call(
        top_kernel,
        [((64, 8, 128), F32)],
        [kind_two.T, list_two.T, top.reshape(64, 8, 128)] + leaf,
        [
            pltpu.SMEM((8, 64), I32),
            pltpu.SMEM((8, 64), I32),
            pltpu.VMEM((64, 8, 128), F32),
            pltpu.VMEM((4, 144, 128), I16),
            pltpu.VMEM((40, 128), F32),
            pltpu.VMEM((40, 128), F32),
            pltpu.VMEM((64, 8, 128), F32),
        ],
        7,
        LARGE,
        "translate_two",
        landed=(2, 4, 5, 6),
    )
    arrived = lax.all_to_all(moved.reshape(32, 16, 128), "space", 0, 0)

    packed, parents_inner, parents_outer = lax.optimization_barrier((packed, parents_inner, parents_outer))
    (near_one,) = call(
        parent_kernel,
        [((8, 2, 8, 512), F32)],
        [kind_one, list_one, parents_inner, parent, parents_outer] + leaf,
        [
            pltpu.SMEM((8, 8), I32),
            pltpu.SMEM((8, 8), I32),
            pltpu.VMEM((128, 512), BF16),
            pltpu.VMEM((128, 512), BF16),
            pltpu.VMEM((24, 2, 8, 512), F32),
            pltpu.VMEM((4, 96, 128), I16),
            pltpu.VMEM((4, 80, 128), F32),
            pltpu.VMEM((8, 2, 8, 512), F32),
        ],
        9,
        SMALL,
        "translate_one",
        landed=(2, 4, 6, 7, 8),
    )

    (lowered,) = call(
        lower_kernel,
        [((528, 128), I16)],
        [arrived, near_one] + list(angles) + [interp_one, interp_two],
        [
            *angle_room,
            pltpu.VMEM((512, 128), F32),
            pltpu.VMEM((2048, 512), F32),
            pltpu.VMEM((32, 16, 128), F32),
            pltpu.VMEM((8, 2, 8, 512), F32),
            pltpu.VMEM((128, 2048), BF16),
            pltpu.VMEM((128, 2048), BF16),
            pltpu.VMEM((512, 128), F32),
            pltpu.VMEM((528, 128), I16),
        ],
        11,
        LARGE,
        "lower",
        landed=(0,),
    )
    shared = [around(lowered, "dir", n_dir, k) for k in (1, 2, 3)]

    (near,) = call(
        near_kernel,
        [((32, 64, 128), F32)],
        [near_list.T, near_count, inner, flat, outer, near_blocks],
        [
            pltpu.SMEM((6, 32), I32),
            pltpu.SMEM((32,), I32),
            pltpu.VMEM((97, 64, 256), BF16),
            pltpu.VMEM((32, 6, 2, 64, 256), BF16),
            pltpu.VMEM((32, 64, 128), F32),
        ],
        21,
        SMALL,
        "near",
        limit=62,
        landed=(2, 4),
    )
    (fields,) = call(
        receive_kernel,
        [((32, 2, 32, 64), F32)],
        [lowered] + shared + packed + [near],
        [
            pltpu.VMEM((4, 528, 128), I16),
            pltpu.VMEM((4, 1040, 128), I16),
            pltpu.VMEM((4, 8, 2, 4, 8, 128), F32),
            pltpu.VMEM((32, 4, 32, 128), F32),
            pltpu.VMEM((32, 64, 128), F32),
            pltpu.VMEM((32, 2, 32, 64), F32),
        ],
        13,
        LARGE,
        "receive",
        landed=(1, 2, 3, 5, 6, 7),
    )
    return fields


def solution(mesh):
    in_specs = (
        P("space", None, None, None),
        P("space", None, None, "dir", None),
        P("space", None),
        P("space"),
        P("space", None, "dir", None),
        P("space", None, "dir", None),
        P(),
        P(),
        P(),
        P(),
        P(None, None, "dir"),
        P("space", None),
        P("space", None),
        P(None, None, "dir"),
        P(),
        P(),
    )
    out_specs = P("space", None, None, "dir")
    return jax.shard_map(shards, mesh=mesh, in_specs=in_specs, out_specs=out_specs, check_vma=False)
```

```python
import functools

import jax
import jax.numpy as jnp
from jax import lax
from jax.experimental import pallas as pl
from jax.experimental.pallas import tpu as pltpu
from jax.sharding import PartitionSpec as P

F32 = jnp.float32
BF16 = jnp.bfloat16
I32 = jnp.int32
I16 = jnp.int16
IN_HBM = pl.BlockSpec(memory_space=pltpu.HBM)
ANYWHERE = pl.BlockSpec(memory_space=pl.ANY)
MIB = 1024 * 1024
SMALL = 2**12
LARGE = 2**36


def call(kernel, outs, operands, scratch, copies, cost, name, landed=(), limit=52):
    shapes = tuple(jax.ShapeDtypeStruct(shape, kind) for shape, kind in outs)
    return pl.pallas_call(
        kernel,
        out_shape=shapes,
        in_specs=[ANYWHERE if n in landed else IN_HBM for n in range(len(operands))],
        out_specs=tuple(IN_HBM for _ in outs),
        scratch_shapes=[*scratch, pltpu.SemaphoreType.DMA((copies,))],
        compiler_params=pltpu.CompilerParams(vmem_limit_bytes=limit * MIB),
        cost_estimate=pl.CostEstimate(flops=cost, bytes_accessed=cost, transcendentals=0),
        name=name,
    )(*operands)


def begin(sems, *pairs, first=0):
    copies = [pltpu.make_async_copy(source, target, sems.at[first + n]) for n, (source, target) in enumerate(pairs)]
    for copy in copies:
        copy.start()
    return copies


def finish(*copies):
    for copy in copies:
        copy.wait()


def rows_by_rows(a, b):
    return lax.dot_general(a, b, (((1,), (1,)), ((), ())), preferred_element_type=F32)


def rows_by_cols(a, b):
    return lax.dot_general(a, b, (((1,), (0,)), ((), ())), preferred_element_type=F32)


def halves(x):
    high = x.astype(BF16)
    return high, (x - high.astype(F32)).astype(BF16)


def product(dot, x, high, low):
    x_high, x_low = halves(x)
    return dot(x_high, high) + (dot(x_high, low) + dot(x_low, high))


def lanes_of(shape):
    return lax.broadcasted_iota(I32, shape, len(shape) - 1)


def swap_half(x):
    return pltpu.roll(x, 64, x.ndim - 1)


def sender(k):
    return lax.rem(lax.axis_index("dir") + 4 - k, 4)


def receiver(k):
    return lax.rem(lax.axis_index("dir") + k, 4)


def power_of(largest):
    return jnp.ceil(jnp.log2(jnp.maximum(largest, 2.0**-100)))


def code_of(scaled):
    return jnp.round(scaled).astype(I32).astype(I16)


def value_of(code):
    return code.astype(I32).astype(F32)


def scale_from(power):
    return jnp.exp2(-power) * 32767.0


def unit_from(power):
    return jnp.exp2(power) * (1.0 / 32767.0)


def unit_of(rows):
    return unit_from(value_of(rows)[0:1])


def leaf_kernel(cur_from, rad_from, one_from, two_from, out0, out1, out2, out3, cur, rad, one, trans, held, codes, sems):
    near_half, far_half = slice(0, 16), slice(16, 32)
    copies = begin(
        sems,
        (cur_from.at[near_half], cur.at[near_half]),
        (rad_from.at[near_half], rad.at[near_half]),
        (cur_from.at[far_half], cur.at[far_half]),
        (rad_from.at[far_half], rad.at[far_half]),
        (one_from, one),
        (two_from, trans),
    )
    lane = lanes_of((32, 128)) // 32
    for p in range(8):
        if p == 0:
            finish(*copies[0:2])
        if p == 4:
            finish(*copies[2:4])
        boxes = cur[4 * p : 4 * p + 4].reshape(256, 256)
        re_rows = rad[4 * p : 4 * p + 4, 0].reshape(128, 256)
        im_rows = rad[4 * p : 4 * p + 4, 1].reshape(128, 256)
        with_re = rows_by_rows(boxes, re_rows)
        with_im = rows_by_rows(boxes, im_rows)
        re = jnp.zeros((32, 128), F32)
        im = jnp.zeros((32, 128), F32)
        for j in range(4):
            a = with_re[64 * j : 64 * j + 64]
            b = with_im[64 * j : 64 * j + 64]
            re = jnp.where(lane == j, a[:32] - b[32:], re)
            im = jnp.where(lane == j, a[32:] + b[:32], im)
        for e in range(4):
            held[e, 16 * p : 16 * p + 8] = re[8 * e : 8 * e + 8]
            held[e, 16 * p + 8 : 16 * p + 16] = im[8 * e : 8 * e + 8]
    finish(*copies[4:6])
    part = lax.rem(lax.axis_index("space"), 8)
    at = pl.ds(pl.multiple_of(part // 2 * 128, 128), 128)
    odd = part % 2
    re = trans[:, 0, at]
    im = trans[:, 1, at]
    lane = lanes_of((40, 128)) < 64
    even_cut = jnp.where(lane, re, swap_half(im))
    odd_cut = jnp.where(lane, swap_half(re), im)
    cut = jnp.where(odd == 1, odd_cut, even_cut)
    cut = jnp.concatenate([cut, jnp.zeros((8, 128), F32)], axis=0)
    table = jnp.concatenate([one[:, 0, :], one[:, 1, :]], axis=0)
    row = lax.broadcasted_iota(I32, (16, 128), 0)
    powers = jnp.zeros((16, 128), F32)
    coded = []
    for n, values in enumerate((held[...], cut, table)):
        flat = jnp.abs(values).reshape(-1, 128)
        power = power_of(jnp.max(flat, keepdims=True))
        powers = jnp.where(row == n, power, powers)
        coded.append(code_of(values.reshape(-1, 128) * scale_from(power)))
    for e in range(4):
        codes[e, 0:128] = coded[0][128 * e : 128 * e + 128]
        codes[e, 128:176] = coded[1]
        codes[e, 176:256] = coded[2]
        codes[e, 256:272] = powers.astype(I32).astype(I16)
    finish(*begin(sems, *[(codes.at[receiver(k)], out) for k, out in enumerate((out0, out1, out2, out3))]))


def pack_kernel(rec_from, one_from, two_from, *refs):
    outs = refs[:4]
    angles_to = refs[4:8]
    rec, one, two, cos1, sin1, cos2, sin2, held, sems = refs[8:]
    copies = begin(
        sems, (one_from, one), (two_from, two), (rec_from.at[0:16], rec.at[0:16]), (rec_from.at[16:32], rec.at[16:32])
    )
    finish(*copies[0:2])
    cos1[...] = jnp.cos(one[...])
    sin1[...] = jnp.sin(one[...])
    cos2[...] = jnp.cos(two[...])
    sin2[...] = jnp.sin(two[...])
    angle_copies = begin(sems, *zip((cos1, sin1, cos2, sin2), angles_to), first=4)
    largest = jnp.zeros((32, 256), F32)
    for t in range(2):
        finish(copies[2 + t])

        def look(b, found):
            return jnp.maximum(found, jnp.maximum(jnp.abs(rec[b, 0]), jnp.abs(rec[b, 1])))

        largest = lax.fori_loop(16 * t, 16 * t + 16, look, largest, unroll=4)
    power = power_of(jnp.max(largest, keepdims=True))
    unit = scale_from(power)
    for e in range(4):
        held[e, 1024:1040] = jnp.broadcast_to(power, (16, 128)).astype(I32).astype(I16)
    lane = lanes_of((32, 128)) < 64

    def body(b, carry):
        rows = pl.ds(pl.multiple_of(b * 32, 32), 32)
        for m in range(2):
            re = rec[b, 0, :, 128 * m : 128 * m + 128] * unit
            im = rec[b, 1, :, 128 * m : 128 * m + 128] * unit
            held[2 * m, rows, :] = code_of(jnp.where(lane, re, swap_half(im)))
            held[2 * m + 1, rows, :] = code_of(jnp.where(lane, swap_half(re), im))
        return carry

    lax.fori_loop(0, 32, body, 0, unroll=4)
    finish(*begin(sems, *[(held.at[receiver(k)], out) for k, out in enumerate(outs)]), *angle_copies)


def lift_kernel(r0, r1, r2, r3, *refs):
    one_from, two_from, *angles_from = refs[:6]
    parent_to, halo_to, message_to = refs[6:9]
    one, two, cos1, sin1, cos2, sin2 = refs[9:15]
    parent, halo, message, codes, held, top, sems = refs[15:]
    copies = begin(
        sems,
        *[(r, codes.at[sender(k)]) for k, r in enumerate((r0, r1, r2, r3))],
        (one_from, one),
        *zip(angles_from, (cos1, sin1, cos2, sin2)),
        *[(two_from.at[512 * t : 512 * t + 512], two.at[512 * t : 512 * t + 512]) for t in range(4)],
    )
    finish(*copies[0:9])
    for e in range(4):
        held[e] = value_of(codes[e, 0:128]) * unit_of(codes[e, 256:272])
    w1h, w1l = halves(one[...])
    lane = lanes_of((128, 128)) // 32
    rows = []
    for j in range(4):
        x = jnp.zeros((128, 128), F32)
        for e in range(4):
            piece = held[e]
            shift = (32 * (e - j)) % 128
            if shift:
                piece = pltpu.roll(piece, shift, 1)
            x = jnp.where(lane == e, piece, x)
        rows.append(x)
    up = product(rows_by_rows, jnp.concatenate(rows, axis=0), w1h, w1l)
    up = up.reshape(4, 8, 2, 8, 512)
    re = jnp.zeros((8, 8, 512), F32)
    im = jnp.zeros((8, 8, 512), F32)
    for j in range(4):
        c = cos1[j : j + 1, :][None]
        s = sin1[j : j + 1, :][None]
        re = re + (c * up[j, :, 0] - s * up[j, :, 1])
        im = im + (c * up[j, :, 1] + s * up[j, :, 0])
    parent[:, 0] = re
    parent[:, 1] = im
    whole = parent[...].reshape(128, 512)
    halo[...] = whole.astype(BF16)
    copies += begin(sems, (parent, parent_to), (halo, halo_to), first=13)
    x_high, x_low = halves(whole)
    for t in range(4):
        finish(copies[9 + t])
        rows = slice(512 * t, 512 * t + 512)
        high, low = halves(two[rows, :])
        part = rows_by_rows(x_high, high) + (rows_by_rows(x_high, low) + rows_by_rows(x_low, high))
        top[:, :, :, :, rows] = part.reshape(2, 4, 2, 8, 512)
    lane = lanes_of((16, 128)) < 64
    for m in range(16):
        at = slice(128 * m, 128 * m + 128)
        re = jnp.zeros((2, 8, 128), F32)
        im = jnp.zeros((2, 8, 128), F32)
        for j in range(4):
            c = cos2[j : j + 1, at][None]
            s = sin2[j : j + 1, at][None]
            u_re = top[:, j, 0, :, at]
            u_im = top[:, j, 1, :, at]
            re = re + (c * u_re - s * u_im)
            im = im + (c * u_im + s * u_re)
        re = re.reshape(16, 128)
        im = im.reshape(16, 128)
        message[2 * m] = jnp.where(lane, re, swap_half(im))
        message[2 * m + 1] = jnp.where(lane, swap_half(re), im)
    copies += begin(sems, (message, message_to), first=15)
    finish(*copies[13:])


def top_kernel(kinds_from, lists_from, top_from, m0, m1, m2, m3, out_to, kinds, lists, top, cuts, first, second, out, sems):
    finish(
        *begin(
            sems,
            (kinds_from, kinds),
            (lists_from, lists),
            (top_from, top),
            *[(m.at[128:272], cuts.at[sender(k)]) for k, m in enumerate((m0, m1, m2, m3))],
        )
    )
    chosen = lax.axis_index("space") // 8
    unit = unit_from(value_of(cuts[chosen, 128:144])[1:2])
    table = (value_of(cuts[chosen, 0:48]) * unit)[0:40]
    lane = lanes_of((40, 128)) < 64
    turned = swap_half(table)
    first[...] = jnp.where(lane, table, turned)
    second[...] = jnp.where(lane, turned, -table)

    def body(g, carry):
        straight = jnp.zeros((8, 128), F32)
        crossed = jnp.zeros((8, 128), F32)
        for k in range(8):
            kind = kinds[k, g]
            value = top[lists[k, g]]
            straight = straight + first[pl.ds(kind, 1), :] * value
            crossed = crossed + second[pl.ds(kind, 1), :] * value
        out[g] = straight + swap_half(crossed)
        return carry

    lax.fori_loop(0, 64, body, 0, unroll=8)
    finish(*begin(sems, (out, out_to)))


def parent_kernel(
    kinds_from, lists_from, inner_from, parent_from, outer_from, m0, m1, m2, m3,
    out_to,
    kinds, lists, inner, outer, held, codes, table, out, sems,
):
    finish(
        *begin(
            sems,
            (kinds_from, kinds),
            (lists_from, lists),
            (inner_from, inner),
            (parent_from, held.at[8:16]),
            (outer_from, outer),
            *[(m.at[176:272], codes.at[sender(k)]) for k, m in enumerate((m0, m1, m2, m3))],
        )
    )
    base = lax.axis_index("space") * 8 - 8
    for e in range(4):
        table[e] = value_of(codes[e, 0:80]) * unit_from(value_of(codes[e, 80:96])[2:3])
    odd = lax.rem(lax.axis_index("space"), 2)
    held[pl.ds(16 - 16 * odd, 8)] = inner[...].astype(F32).reshape(8, 2, 8, 512)
    held[pl.ds(16 * odd, 8)] = outer[...].astype(F32).reshape(8, 2, 8, 512)

    def body(p, carry):
        re = [jnp.zeros((8, 128), F32) for _ in range(4)]
        im = [jnp.zeros((8, 128), F32) for _ in range(4)]
        for k in range(8):
            kind = kinds[p, k]
            source = lists[p, k] - base
            for m in range(4):
                at = slice(128 * m, 128 * m + 128)
                s_re = held[source, 0, :, at]
                s_im = held[source, 1, :, at]
                c_re = table[m, pl.ds(kind, 1), :]
                c_im = table[m, pl.ds(kind + 40, 1), :]
                re[m] = re[m] + (c_re * s_re - c_im * s_im)
                im[m] = im[m] + (c_re * s_im + c_im * s_re)
        for m in range(4):
            at = slice(128 * m, 128 * m + 128)
            out[p, 0, :, at] = re[m]
            out[p, 1, :, at] = im[m]
        return carry

    lax.fori_loop(0, 8, body, 0)
    finish(*begin(sems, (out, out_to)))


def lower_kernel(arrived_from, near_one_from, *refs):
    sources = refs[:6]
    out_to = refs[6]
    cos1, sin1, cos2, sin2, one, two = refs[7:13]
    arrived, near_one, child_high, child_low, held, out, sems = refs[13:]
    copies = begin(
        sems,
        (arrived_from, arrived),
        (near_one_from, near_one),
        *zip(sources[:5], refs[7:12]),
        *[(sources[5].at[512 * t : 512 * t + 512], two.at[512 * t : 512 * t + 512]) for t in range(4)],
    )
    finish(copies[0], *copies[4:6])
    lane = lanes_of((16, 128)) < 64
    for m in range(16):
        at = slice(128 * m, 128 * m + 128)
        a = arrived[2 * m]
        b = arrived[2 * m + 1]
        re = jnp.where(lane, a, swap_half(b)).reshape(2, 8, 128)
        im = jnp.where(lane, swap_half(a), b).reshape(2, 8, 128)
        for j in range(4):
            c = cos2[j : j + 1, at][None]
            s = sin2[j : j + 1, at][None]
            both = jnp.concatenate([(c * re + s * im)[:, None], (c * im - s * re)[:, None]], axis=1)
            high, low = halves(both.reshape(2, 16, 128))
            for g in range(2):
                rows = slice(64 * g + 16 * j, 64 * g + 16 * j + 16)
                child_high[rows, at] = high[g]
                child_low[rows, at] = low[g]
    local = jnp.zeros((128, 512), F32)
    for t in range(4):
        finish(copies[7 + t])
        at = slice(512 * t, 512 * t + 512)
        high = child_high[:, at]
        w2h, w2l = halves(two[at, :])
        local = local + (rows_by_cols(high, w2h) + (rows_by_cols(high, w2l) + rows_by_cols(child_low[:, at], w2h)))
    finish(*copies[1:4], copies[6])
    w1h, w1l = halves(one[...])
    local = local.reshape(8, 2, 8, 512) + near_one[...]
    re = local[:, 0]
    im = local[:, 1]
    for j in range(4):
        c = cos1[j : j + 1, :][None]
        s = sin1[j : j + 1, :][None]
        both = jnp.concatenate([(c * re + s * im)[:, None], (c * im - s * re)[:, None]], axis=1)
        down = product(rows_by_cols, both.reshape(128, 512), w1h, w1l)
        held[128 * j : 128 * j + 128] = down
    largest = jnp.max(jnp.abs(held[...]), keepdims=True)
    power = power_of(largest)
    out[0:512] = code_of(held[...] * scale_from(power))
    out[512:528] = jnp.broadcast_to(power, (16, 128)).astype(I32).astype(I16)
    finish(*begin(sems, (out, out_to)))


def near_kernel(half, lists_from, counts_from, inner, current, outer, blocks_from, out_to, lists, counts, held, blocks, out, sems):
    odd = lax.rem(lax.axis_index("space"), 2)
    copies = begin(
        sems,
        (lists_from, lists),
        (counts_from, counts),
        (inner, held.at[pl.ds(64 - 64 * odd, 32)]),
        (current, held.at[32:64]),
        (outer, held.at[pl.ds(64 * odd, 32)]),
        *[
            (blocks_from.at[16 * half + 4 * t : 16 * half + 4 * t + 4], blocks.at[4 * t : 4 * t + 4])
            for t in range(4)
        ],
    )
    held[96] = jnp.zeros((64, 256), BF16)
    finish(*copies[0:5])
    base = lax.axis_index("space") * 32 - 32

    for t in range(4):
        finish(copies[5 + t])

        def body(n, carry):
            for row in (4 * t + 2 * n, 4 * t + 2 * n + 1):
                box = 16 * half + row
                total = jnp.zeros((64, 128), F32)
                for k in range(6):
                    source = jnp.where(k < counts[box], lists[k, box] - base, 96)
                    total = total + rows_by_rows(held[source], blocks[row, k].reshape(128, 256))
                out[row] = total
            return carry

        lax.fori_loop(0, 2, body, 0, unroll=2)
        copies += begin(sems, (out.at[4 * t : 4 * t + 4], out_to.at[4 * t : 4 * t + 4]), first=9 + t)
    finish(*copies[9:])


def receive_kernel(l0, l1, l2, l3, x0, x1, x2, x3, near_first, near_second, out_to, codes, packs, samples, matrix, near, out, sems):
    copies = begin(
        sems,
        *[(l, codes.at[k]) for k, l in enumerate((l0, l1, l2, l3))],
        *[(x, packs.at[k]) for k, x in enumerate((x0, x1, x2, x3))],
        (near_first, near.at[0:16]),
        (near_second, near.at[16:32]),
    )
    finish(*copies[0:4])
    for k in range(4):
        values = value_of(codes[k, 0:512]) * unit_of(codes[k, 512:528])
        samples[:, :, :, sender(k)] = values.reshape(4, 8, 2, 8, 128)
    finish(*copies[4:10])
    units = [unit_of(packs[k, 1024:1040]) for k in range(4)]

    def body(p, carry):
        for j in range(4):
            b = 4 * p + j
            rows = pl.ds(pl.multiple_of(32 * b, 32), 32)
            for k in range(4):
                matrix[b, sender(k)] = value_of(packs[k, rows, :]) * units[k]
            left_high, left_low = halves(samples[j, p].reshape(64, 128))
            high, low = halves(matrix[b].reshape(128, 128))
            left = jnp.concatenate([left_high, left_low], axis=1)
            right = jnp.concatenate(
                [jnp.concatenate([high, low], axis=1), jnp.concatenate([high, jnp.zeros_like(low)], axis=1)], axis=0
            )
            both = rows_by_cols(left, right)
            total = near[b] + (both[:, :128] + both[:, 128:])
            turned = swap_half(total)
            out[b, 0] = (total[:32] - turned[32:])[:, :64]
            out[b, 1] = (total[32:] + turned[:32])[:, :64]
        return carry

    for t in range(4):
        lax.fori_loop(2 * t, 2 * t + 2, body, 0, unroll=2)
        part = slice(8 * t, 8 * t + 8)
        copies += begin(sems, (out.at[part], out_to.at[part]), first=10 + t)
    finish(*copies[10:])


def near_half(half, *operands):
    return call(
        functools.partial(near_kernel, half),
        [((16, 64, 128), F32)],
        list(operands),
        [
            pltpu.SMEM((6, 32), I32),
            pltpu.SMEM((32,), I32),
            pltpu.VMEM((97, 64, 256), BF16),
            pltpu.VMEM((16, 6, 2, 64, 256), BF16),
            pltpu.VMEM((16, 64, 128), F32),
        ],
        13,
        SMALL,
        "near",
        limit=60,
        landed=(2, 4),
    )[0]


def around(x, axis, peers, k):
    return lax.ppermute(x, axis, [(i, (i + k) % peers) for i in range(peers)])


def after_all(values, *tokens):
    return lax.optimization_barrier((*values, *tokens))[: len(values)]


def shards(
    currents,
    near_blocks,
    near_list,
    near_count,
    radiate,
    receive,
    phase_one,
    phase_two,
    interp_one,
    interp_two,
    trans_one,
    kind_one,
    list_one,
    trans_two,
    kind_two,
    list_two,
):
    n_space = lax.axis_size("space")
    n_dir = lax.axis_size("dir")
    first_swap = [(i ^ 1, i) for i in range(n_space)]
    second_swap = [(i, j) for k in range(1, n_space - 1, 2) for i, j in ((k, k + 1), (k + 1, k))]

    flat = currents.reshape(32, 64, 256)
    inner = lax.ppermute(flat, "space", first_swap)
    outer = lax.ppermute(flat, "space", second_swap)

    leaf = call(
        leaf_kernel,
        [((272, 128), I16)] * 4,
        [currents, radiate, trans_one, trans_two],
        [
            pltpu.VMEM((32, 2, 32, 256), BF16),
            pltpu.VMEM((32, 2, 32, 256), BF16),
            pltpu.VMEM((40, 2, 128), F32),
            pltpu.VMEM((40, 2, 512), F32),
            pltpu.VMEM((4, 128, 128), F32),
            pltpu.VMEM((4, 272, 128), I16),
        ],
        6,
        LARGE,
        "leaf",
        limit=62,
    )
    own_leaf = leaf[0]
    leaf = [own_leaf] + [around(leaf[k], "dir", n_dir, k) for k in (1, 2, 3)]
    angle_room = [*[pltpu.VMEM((4, 512), F32)] * 2, *[pltpu.VMEM((4, 2048), F32)] * 2]
    packed = call(
        pack_kernel,
        [((1040, 128), I16)] * 4 + [((4, 512), F32)] * 2 + [((4, 2048), F32)] * 2,
        list(after_all((receive, phase_one, phase_two), own_leaf)),
        [
            pltpu.VMEM((32, 2, 32, 256), F32),
            pltpu.VMEM((4, 512), F32),
            pltpu.VMEM((4, 2048), F32),
            *angle_room,
            pltpu.VMEM((4, 1040, 128), I16),
        ],
        8,
        SMALL,
        "pack",
    )
    packed, angles = packed[:4], packed[4:]
    leaf, packed = lax.optimization_barrier((leaf, packed))
    packed = [packed[0]] + [around(packed[k], "dir", n_dir, k) for k in (1, 2, 3)]


    parent, halo, message = call(
        lift_kernel,
        [((8, 2, 8, 512), F32), ((128, 512), BF16), ((32, 16, 128), F32)],
        leaf + [interp_one, interp_two] + list(angles),
        [
            pltpu.VMEM((512, 128), F32),
            pltpu.VMEM((2048, 512), F32),
            *angle_room,
            pltpu.VMEM((8, 2, 8, 512), F32),
            pltpu.VMEM((128, 512), BF16),
            pltpu.VMEM((32, 16, 128), F32),
            pltpu.VMEM((4, 272, 128), I16),
            pltpu.VMEM((4, 128, 128), F32),
            pltpu.VMEM((2, 4, 2, 8, 2048), F32),
        ],
        16,
        LARGE,
        "lift",
        landed=(1, 2, 3),
    )
    top = lax.all_to_all(message, "space", 0, 0)
    parents_inner = lax.ppermute(halo, "space", first_swap)
    parents_outer = lax.ppermute(halo, "space", second_swap)

    top, inner, outer = lax.optimization_barrier((top, inner, outer))
    (moved,) = call(
        top_kernel,
        [((64, 8, 128), F32)],
        [kind_two.T, list_two.T, top.reshape(64, 8, 128)] + leaf,
        [
            pltpu.SMEM((8, 64), I32),
            pltpu.SMEM((8, 64), I32),
            pltpu.VMEM((64, 8, 128), F32),
            pltpu.VMEM((4, 144, 128), I16),
            pltpu.VMEM((40, 128), F32),
            pltpu.VMEM((40, 128), F32),
            pltpu.VMEM((64, 8, 128), F32),
        ],
        7,
        LARGE,
        "translate_two",
        landed=(2, 4, 5, 6),
    )
    moved, parents_inner, parents_outer = lax.optimization_barrier((moved, parents_inner, parents_outer))
    arrived = lax.all_to_all(moved.reshape(32, 16, 128), "space", 0, 0)

    packed, parents_inner, parents_outer = lax.optimization_barrier((packed, parents_inner, parents_outer))
    near_parts = [near_half(half, near_list.T, near_count, inner, flat, outer, near_blocks) for half in (0, 1)]
    (near_one,) = call(
        parent_kernel,
        [((8, 2, 8, 512), F32)],
        [kind_one, list_one, parents_inner, parent, parents_outer] + leaf,
        [
            pltpu.SMEM((8, 8), I32),
            pltpu.SMEM((8, 8), I32),
            pltpu.VMEM((128, 512), BF16),
            pltpu.VMEM((128, 512), BF16),
            pltpu.VMEM((24, 2, 8, 512), F32),
            pltpu.VMEM((4, 96, 128), I16),
            pltpu.VMEM((4, 80, 128), F32),
            pltpu.VMEM((8, 2, 8, 512), F32),
        ],
        9,
        SMALL,
        "translate_one",
        landed=(2, 4, 6, 7, 8),
    )

    arrived, near_one, near_parts[0] = lax.optimization_barrier((arrived, near_one, near_parts[0]))
    (lowered,) = call(
        lower_kernel,
        [((528, 128), I16)],
        [arrived, near_one] + list(angles) + [interp_one, interp_two],
        [
            *angle_room,
            pltpu.VMEM((512, 128), F32),
            pltpu.VMEM((2048, 512), F32),
            pltpu.VMEM((32, 16, 128), F32),
            pltpu.VMEM((8, 2, 8, 512), F32),
            pltpu.VMEM((128, 2048), BF16),
            pltpu.VMEM((128, 2048), BF16),
            pltpu.VMEM((512, 128), F32),
            pltpu.VMEM((528, 128), I16),
        ],
        11,
        LARGE,
        "lower",
        landed=(0,),
    )
    shared = [around(lowered, "dir", n_dir, k) for k in (1, 2, 3)]

    (fields,) = call(
        receive_kernel,
        [((32, 2, 32, 64), F32)],
        [lowered] + shared + packed + near_parts,
        [
            pltpu.VMEM((4, 528, 128), I16),
            pltpu.VMEM((4, 1040, 128), I16),
            pltpu.VMEM((4, 8, 2, 4, 8, 128), F32),
            pltpu.VMEM((32, 4, 32, 128), F32),
            pltpu.VMEM((32, 64, 128), F32),
            pltpu.VMEM((32, 2, 32, 64), F32),
        ],
        14,
        LARGE,
        "receive",
        landed=(1, 2, 3, 5, 6, 7),
    )
    return fields


def solution(mesh):
    in_specs = (
        P("space", None, None, None),
        P("space", None, None, "dir", None),
        P("space", None),
        P("space"),
        P("space", None, "dir", None),
        P("space", None, "dir", None),
        P(),
        P(),
        P(),
        P(),
        P(None, None, "dir"),
        P("space", None),
        P("space", None),
        P(None, None, "dir"),
        P(),
        P(),
    )
    out_specs = P("space", None, None, "dir")
    return jax.shard_map(shards, mesh=mesh, in_specs=in_specs, out_specs=out_specs, check_vma=False)
```

```python
import functools

import jax
import jax.numpy as jnp
from jax import lax
from jax.experimental import pallas as pl
from jax.experimental.pallas import tpu as pltpu
from jax.sharding import PartitionSpec as P

F32 = jnp.float32
BF16 = jnp.bfloat16
I32 = jnp.int32
I16 = jnp.int16
IN_HBM = pl.BlockSpec(memory_space=pltpu.HBM)
ANYWHERE = pl.BlockSpec(memory_space=pl.ANY)
MIB = 1024 * 1024
SMALL = 2**12
LARGE = 2**36


def call(kernel, outs, operands, scratch, copies, cost, name, landed=(), limit=52):
    shapes = tuple(jax.ShapeDtypeStruct(shape, kind) for shape, kind in outs)
    return pl.pallas_call(
        kernel,
        out_shape=shapes,
        in_specs=[ANYWHERE if n in landed else IN_HBM for n in range(len(operands))],
        out_specs=tuple(IN_HBM for _ in outs),
        scratch_shapes=[*scratch, pltpu.SemaphoreType.DMA((copies,))],
        compiler_params=pltpu.CompilerParams(vmem_limit_bytes=limit * MIB),
        cost_estimate=pl.CostEstimate(flops=cost, bytes_accessed=cost, transcendentals=0),
        name=name,
    )(*operands)


def begin(sems, *pairs, first=0):
    copies = [pltpu.make_async_copy(source, target, sems.at[first + n]) for n, (source, target) in enumerate(pairs)]
    for copy in copies:
        copy.start()
    return copies


def finish(*copies):
    for copy in copies:
        copy.wait()


def rows_by_rows(a, b):
    return lax.dot_general(a, b, (((1,), (1,)), ((), ())), preferred_element_type=F32)


def rows_by_cols(a, b):
    return lax.dot_general(a, b, (((1,), (0,)), ((), ())), preferred_element_type=F32)


def halves(x):
    high = x.astype(BF16)
    return high, (x - high.astype(F32)).astype(BF16)


def product(dot, x, high, low):
    x_high, x_low = halves(x)
    return dot(x_high, high) + (dot(x_high, low) + dot(x_low, high))


def lanes_of(shape):
    return lax.broadcasted_iota(I32, shape, len(shape) - 1)


def swap_half(x):
    return pltpu.roll(x, 64, x.ndim - 1)


def sender(k):
    return lax.rem(lax.axis_index("dir") + 4 - k, 4)


def receiver(k):
    return lax.rem(lax.axis_index("dir") + k, 4)


def power_of(largest):
    return jnp.ceil(jnp.log2(jnp.maximum(largest, 2.0**-100)))


def code_of(scaled):
    return jnp.round(scaled).astype(I32).astype(I16)


def value_of(code):
    return code.astype(I32).astype(F32)


def scale_from(power):
    return jnp.exp2(-power) * 32767.0


def unit_from(power):
    return jnp.exp2(power) * (1.0 / 32767.0)


def unit_of(rows):
    return unit_from(value_of(rows)[0:1])


def leaf_kernel(cur_from, rad_from, one_from, two_from, out0, out1, out2, out3, cur, rad, one, trans, held, codes, sems):
    near_half, far_half = slice(0, 16), slice(16, 32)
    copies = begin(
        sems,
        (cur_from.at[near_half], cur.at[near_half]),
        (rad_from.at[near_half], rad.at[near_half]),
        (cur_from.at[far_half], cur.at[far_half]),
        (rad_from.at[far_half], rad.at[far_half]),
        (one_from, one),
        (two_from, trans),
    )
    lane = lanes_of((32, 128)) // 32
    for p in range(8):
        if p == 0:
            finish(*copies[0:2])
        if p == 4:
            finish(*copies[2:4])
        boxes = cur[4 * p : 4 * p + 4].reshape(256, 256)
        re_rows = rad[4 * p : 4 * p + 4, 0].reshape(128, 256)
        im_rows = rad[4 * p : 4 * p + 4, 1].reshape(128, 256)
        with_re = rows_by_rows(boxes, re_rows)
        with_im = rows_by_rows(boxes, im_rows)
        re = jnp.zeros((32, 128), F32)
        im = jnp.zeros((32, 128), F32)
        for j in range(4):
            a = with_re[64 * j : 64 * j + 64]
            b = with_im[64 * j : 64 * j + 64]
            re = jnp.where(lane == j, a[:32] - b[32:], re)
            im = jnp.where(lane == j, a[32:] + b[:32], im)
        for e in range(4):
            held[e, 16 * p : 16 * p + 8] = re[8 * e : 8 * e + 8]
            held[e, 16 * p + 8 : 16 * p + 16] = im[8 * e : 8 * e + 8]
    finish(*copies[4:6])
    part = lax.rem(lax.axis_index("space"), 8)
    at = pl.ds(pl.multiple_of(part // 2 * 128, 128), 128)
    odd = part % 2
    re = trans[:, 0, at]
    im = trans[:, 1, at]
    lane = lanes_of((40, 128)) < 64
    even_cut = jnp.where(lane, re, swap_half(im))
    odd_cut = jnp.where(lane, swap_half(re), im)
    cut = jnp.where(odd == 1, odd_cut, even_cut)
    cut = jnp.concatenate([cut, jnp.zeros((8, 128), F32)], axis=0)
    table = jnp.concatenate([one[:, 0, :], one[:, 1, :]], axis=0)
    row = lax.broadcasted_iota(I32, (16, 128), 0)
    powers = jnp.zeros((16, 128), F32)
    coded = []
    for n, values in enumerate((held[...], cut, table)):
        flat = jnp.abs(values).reshape(-1, 128)
        power = power_of(jnp.max(flat, keepdims=True))
        powers = jnp.where(row == n, power, powers)
        coded.append(code_of(values.reshape(-1, 128) * scale_from(power)))
    for e in range(4):
        codes[e, 0:128] = coded[0][128 * e : 128 * e + 128]
        codes[e, 128:176] = coded[1]
        codes[e, 176:256] = coded[2]
        codes[e, 256:272] = powers.astype(I32).astype(I16)
    finish(*begin(sems, *[(codes.at[receiver(k)], out) for k, out in enumerate((out0, out1, out2, out3))]))


def pack_kernel(rec_from, one_from, two_from, *refs):
    outs = refs[:4]
    angles_to = refs[4:8]
    rec, one, two, cos1, sin1, cos2, sin2, held, sems = refs[8:]
    copies = begin(
        sems, (one_from, one), (two_from, two), (rec_from.at[0:16], rec.at[0:16]), (rec_from.at[16:32], rec.at[16:32])
    )
    finish(*copies[0:2])
    cos1[...] = jnp.cos(one[...])
    sin1[...] = jnp.sin(one[...])
    cos2[...] = jnp.cos(two[...])
    sin2[...] = jnp.sin(two[...])
    angle_copies = begin(sems, *zip((cos1, sin1, cos2, sin2), angles_to), first=4)
    largest = jnp.zeros((32, 256), F32)
    for t in range(2):
        finish(copies[2 + t])

        def look(b, found):
            return jnp.maximum(found, jnp.maximum(jnp.abs(rec[b, 0]), jnp.abs(rec[b, 1])))

        largest = lax.fori_loop(16 * t, 16 * t + 16, look, largest, unroll=4)
    power = power_of(jnp.max(largest, keepdims=True))
    unit = scale_from(power)
    for e in range(4):
        held[e, 1024:1040] = jnp.broadcast_to(power, (16, 128)).astype(I32).astype(I16)
    lane = lanes_of((32, 128)) < 64

    def body(b, carry):
        rows = pl.ds(pl.multiple_of(b * 32, 32), 32)
        for m in range(2):
            re = rec[b, 0, :, 128 * m : 128 * m + 128] * unit
            im = rec[b, 1, :, 128 * m : 128 * m + 128] * unit
            held[2 * m, rows, :] = code_of(jnp.where(lane, re, swap_half(im)))
            held[2 * m + 1, rows, :] = code_of(jnp.where(lane, swap_half(re), im))
        return carry

    lax.fori_loop(0, 32, body, 0, unroll=4)
    finish(*begin(sems, *[(held.at[receiver(k)], out) for k, out in enumerate(outs)]), *angle_copies)


def lift_kernel(r0, r1, r2, r3, *refs):
    one_from, two_from, *angles_from = refs[:6]
    parent_to, halo_to, message_to = refs[6:9]
    one, two, cos1, sin1, cos2, sin2 = refs[9:15]
    parent, halo, message, codes, held, top, sems = refs[15:]
    copies = begin(
        sems,
        *[(r, codes.at[sender(k)]) for k, r in enumerate((r0, r1, r2, r3))],
        (one_from, one),
        *zip(angles_from, (cos1, sin1, cos2, sin2)),
        *[(two_from.at[512 * t : 512 * t + 512], two.at[512 * t : 512 * t + 512]) for t in range(4)],
    )
    finish(*copies[0:9])
    for e in range(4):
        held[e] = value_of(codes[e, 0:128]) * unit_of(codes[e, 256:272])
    w1h, w1l = halves(one[...])
    lane = lanes_of((128, 128)) // 32
    rows = []
    for j in range(4):
        x = jnp.zeros((128, 128), F32)
        for e in range(4):
            piece = held[e]
            shift = (32 * (e - j)) % 128
            if shift:
                piece = pltpu.roll(piece, shift, 1)
            x = jnp.where(lane == e, piece, x)
        rows.append(x)
    up = product(rows_by_rows, jnp.concatenate(rows, axis=0), w1h, w1l)
    up = up.reshape(4, 8, 2, 8, 512)
    re = jnp.zeros((8, 8, 512), F32)
    im = jnp.zeros((8, 8, 512), F32)
    for j in range(4):
        c = cos1[j : j + 1, :][None]
        s = sin1[j : j + 1, :][None]
        re = re + (c * up[j, :, 0] - s * up[j, :, 1])
        im = im + (c * up[j, :, 1] + s * up[j, :, 0])
    parent[:, 0] = re
    parent[:, 1] = im
    whole = parent[...].reshape(128, 512)
    halo[...] = whole.astype(BF16)
    copies += begin(sems, (parent, parent_to), (halo, halo_to), first=13)
    x_high, x_low = halves(whole)
    for t in range(4):
        finish(copies[9 + t])
        rows = slice(512 * t, 512 * t + 512)
        high, low = halves(two[rows, :])
        part = rows_by_rows(x_high, high) + (rows_by_rows(x_high, low) + rows_by_rows(x_low, high))
        top[:, :, :, :, rows] = part.reshape(2, 4, 2, 8, 512)
    lane = lanes_of((16, 128)) < 64
    for m in range(16):
        at = slice(128 * m, 128 * m + 128)
        re = jnp.zeros((2, 8, 128), F32)
        im = jnp.zeros((2, 8, 128), F32)
        for j in range(4):
            c = cos2[j : j + 1, at][None]
            s = sin2[j : j + 1, at][None]
            u_re = top[:, j, 0, :, at]
            u_im = top[:, j, 1, :, at]
            re = re + (c * u_re - s * u_im)
            im = im + (c * u_im + s * u_re)
        re = re.reshape(16, 128)
        im = im.reshape(16, 128)
        message[2 * m] = jnp.where(lane, re, swap_half(im))
        message[2 * m + 1] = jnp.where(lane, swap_half(re), im)
    copies += begin(sems, (message, message_to), first=15)
    finish(*copies[13:])


def top_kernel(kinds_from, lists_from, top_from, m0, m1, m2, m3, out_to, kinds, lists, top, cuts, first, second, out, sems):
    finish(
        *begin(
            sems,
            (kinds_from, kinds),
            (lists_from, lists),
            (top_from, top),
            *[(m.at[128:272], cuts.at[sender(k)]) for k, m in enumerate((m0, m1, m2, m3))],
        )
    )
    chosen = lax.axis_index("space") // 8
    unit = unit_from(value_of(cuts[chosen, 128:144])[1:2])
    table = (value_of(cuts[chosen, 0:48]) * unit)[0:40]
    lane = lanes_of((40, 128)) < 64
    turned = swap_half(table)
    first[...] = jnp.where(lane, table, turned)
    second[...] = jnp.where(lane, turned, -table)

    def body(g, carry):
        straight = jnp.zeros((8, 128), F32)
        crossed = jnp.zeros((8, 128), F32)
        for k in range(8):
            kind = kinds[k, g]
            value = top[lists[k, g]]
            straight = straight + first[pl.ds(kind, 1), :] * value
            crossed = crossed + second[pl.ds(kind, 1), :] * value
        out[g] = straight + swap_half(crossed)
        return carry

    lax.fori_loop(0, 64, body, 0, unroll=8)
    finish(*begin(sems, (out, out_to)))


def parent_kernel(
    kinds_from, lists_from, inner_from, parent_from, outer_from, m0, m1, m2, m3,
    out_to,
    kinds, lists, inner, outer, held, codes, table, out, sems,
):
    finish(
        *begin(
            sems,
            (kinds_from, kinds),
            (lists_from, lists),
            (inner_from, inner),
            (parent_from, held.at[8:16]),
            (outer_from, outer),
            *[(m.at[176:272], codes.at[sender(k)]) for k, m in enumerate((m0, m1, m2, m3))],
        )
    )
    base = lax.axis_index("space") * 8 - 8
    for e in range(4):
        table[e] = value_of(codes[e, 0:80]) * unit_from(value_of(codes[e, 80:96])[2:3])
    odd = lax.rem(lax.axis_index("space"), 2)
    held[pl.ds(16 - 16 * odd, 8)] = inner[...].astype(F32).reshape(8, 2, 8, 512)
    held[pl.ds(16 * odd, 8)] = outer[...].astype(F32).reshape(8, 2, 8, 512)

    def body(p, carry):
        re = [jnp.zeros((8, 128), F32) for _ in range(4)]
        im = [jnp.zeros((8, 128), F32) for _ in range(4)]
        for k in range(8):
            kind = kinds[p, k]
            source = lists[p, k] - base
            for m in range(4):
                at = slice(128 * m, 128 * m + 128)
                s_re = held[source, 0, :, at]
                s_im = held[source, 1, :, at]
                c_re = table[m, pl.ds(kind, 1), :]
                c_im = table[m, pl.ds(kind + 40, 1), :]
                re[m] = re[m] + (c_re * s_re - c_im * s_im)
                im[m] = im[m] + (c_re * s_im + c_im * s_re)
        for m in range(4):
            at = slice(128 * m, 128 * m + 128)
            out[p, 0, :, at] = re[m]
            out[p, 1, :, at] = im[m]
        return carry

    lax.fori_loop(0, 8, body, 0)
    finish(*begin(sems, (out, out_to)))


def lower_kernel(arrived_from, near_one_from, *refs):
    sources = refs[:6]
    out_to = refs[6]
    cos1, sin1, cos2, sin2, one, two = refs[7:13]
    arrived, near_one, child_high, child_low, held, out, sems = refs[13:]
    copies = begin(
        sems,
        (arrived_from, arrived),
        (near_one_from, near_one),
        *zip(sources[:5], refs[7:12]),
        *[(sources[5].at[512 * t : 512 * t + 512], two.at[512 * t : 512 * t + 512]) for t in range(4)],
    )
    finish(copies[0], *copies[4:6])
    lane = lanes_of((16, 128)) < 64
    for m in range(16):
        at = slice(128 * m, 128 * m + 128)
        a = arrived[2 * m]
        b = arrived[2 * m + 1]
        re = jnp.where(lane, a, swap_half(b)).reshape(2, 8, 128)
        im = jnp.where(lane, swap_half(a), b).reshape(2, 8, 128)
        for j in range(4):
            c = cos2[j : j + 1, at][None]
            s = sin2[j : j + 1, at][None]
            both = jnp.concatenate([(c * re + s * im)[:, None], (c * im - s * re)[:, None]], axis=1)
            high, low = halves(both.reshape(2, 16, 128))
            for g in range(2):
                rows = slice(64 * g + 16 * j, 64 * g + 16 * j + 16)
                child_high[rows, at] = high[g]
                child_low[rows, at] = low[g]
    local = jnp.zeros((128, 512), F32)
    for t in range(4):
        finish(copies[7 + t])
        at = slice(512 * t, 512 * t + 512)
        high = child_high[:, at]
        w2h, w2l = halves(two[at, :])
        local = local + (rows_by_cols(high, w2h) + (rows_by_cols(high, w2l) + rows_by_cols(child_low[:, at], w2h)))
    finish(*copies[1:4], copies[6])
    w1h, w1l = halves(one[...])
    local = local.reshape(8, 2, 8, 512) + near_one[...]
    re = local[:, 0]
    im = local[:, 1]
    for j in range(4):
        c = cos1[j : j + 1, :][None]
        s = sin1[j : j + 1, :][None]
        both = jnp.concatenate([(c * re + s * im)[:, None], (c * im - s * re)[:, None]], axis=1)
        down = product(rows_by_cols, both.reshape(128, 512), w1h, w1l)
        held[128 * j : 128 * j + 128] = down
    largest = jnp.max(jnp.abs(held[...]), keepdims=True)
    power = power_of(largest)
    out[0:512] = code_of(held[...] * scale_from(power))
    out[512:528] = jnp.broadcast_to(power, (16, 128)).astype(I32).astype(I16)
    finish(*begin(sems, (out, out_to)))


def near_kernel(half, lists_from, counts_from, inner, current, outer, blocks_from, out_to, lists, counts, held, blocks, out, sems):
    odd = lax.rem(lax.axis_index("space"), 2)
    copies = begin(
        sems,
        (lists_from, lists),
        (counts_from, counts),
        (inner, held.at[pl.ds(64 - 64 * odd, 32)]),
        (current, held.at[32:64]),
        (outer, held.at[pl.ds(64 * odd, 32)]),
        *[
            (blocks_from.at[16 * half + 4 * t : 16 * half + 4 * t + 4], blocks.at[4 * t : 4 * t + 4])
            for t in range(4)
        ],
    )
    held[96] = jnp.zeros((64, 256), BF16)
    finish(*copies[0:5])
    base = lax.axis_index("space") * 32 - 32

    for t in range(4):
        finish(copies[5 + t])

        def body(n, carry):
            for row in (4 * t + 2 * n, 4 * t + 2 * n + 1):
                box = 16 * half + row
                total = jnp.zeros((64, 128), F32)
                for k in range(6):
                    source = jnp.where(k < counts[box], lists[k, box] - base, 96)
                    total = total + rows_by_rows(held[source], blocks[row, k].reshape(128, 256))
                out[row] = total
            return carry

        lax.fori_loop(0, 2, body, 0, unroll=2)
        copies += begin(sems, (out.at[4 * t : 4 * t + 4], out_to.at[4 * t : 4 * t + 4]), first=9 + t)
    finish(*copies[9:])


def receive_kernel(l0, l1, l2, l3, x0, x1, x2, x3, near_first, near_second, out_to, codes, packs, samples, matrix, near, out, sems):
    copies = begin(
        sems,
        *[(l, codes.at[k]) for k, l in enumerate((l0, l1, l2, l3))],
        *[(x, packs.at[k]) for k, x in enumerate((x0, x1, x2, x3))],
        (near_first, near.at[0:16]),
        (near_second, near.at[16:32]),
    )
    finish(*copies[0:4])
    for k in range(4):
        values = value_of(codes[k, 0:512]) * unit_of(codes[k, 512:528])
        samples[:, :, :, sender(k)] = values.reshape(4, 8, 2, 8, 128)
    finish(*copies[4:10])
    units = [unit_of(packs[k, 1024:1040]) for k in range(4)]

    def body(p, carry):
        for j in range(4):
            b = 4 * p + j
            rows = pl.ds(pl.multiple_of(32 * b, 32), 32)
            for k in range(4):
                matrix[b, sender(k)] = value_of(packs[k, rows, :]) * units[k]
            left_high, left_low = halves(samples[j, p].reshape(64, 128))
            high, low = halves(matrix[b].reshape(128, 128))
            left = jnp.concatenate([left_high, left_low], axis=1)
            right = jnp.concatenate(
                [jnp.concatenate([high, low], axis=1), jnp.concatenate([high, jnp.zeros_like(low)], axis=1)], axis=0
            )
            both = rows_by_cols(left, right)
            total = near[b] + (both[:, :128] + both[:, 128:])
            turned = swap_half(total)
            out[b, 0] = (total[:32] - turned[32:])[:, :64]
            out[b, 1] = (total[32:] + turned[:32])[:, :64]
        return carry

    for t in range(4):
        lax.fori_loop(2 * t, 2 * t + 2, body, 0, unroll=2)
        part = slice(8 * t, 8 * t + 8)
        copies += begin(sems, (out.at[part], out_to.at[part]), first=10 + t)
    finish(*copies[10:])


def near_half(half, *operands):
    return call(
        functools.partial(near_kernel, half),
        [((16, 64, 128), F32)],
        list(operands),
        [
            pltpu.SMEM((6, 32), I32),
            pltpu.SMEM((32,), I32),
            pltpu.VMEM((97, 64, 256), BF16),
            pltpu.VMEM((16, 6, 2, 64, 256), BF16),
            pltpu.VMEM((16, 64, 128), F32),
        ],
        13,
        SMALL,
        "near",
        limit=60,
        landed=(2, 4),
    )[0]


def around(x, axis, peers, k):
    return lax.ppermute(x, axis, [(i, (i + k) % peers) for i in range(peers)])


def after_all(values, *tokens):
    return lax.optimization_barrier((*values, *tokens))[: len(values)]


def shards(
    currents,
    near_blocks,
    near_list,
    near_count,
    radiate,
    receive,
    phase_one,
    phase_two,
    interp_one,
    interp_two,
    trans_one,
    kind_one,
    list_one,
    trans_two,
    kind_two,
    list_two,
):
    n_space = lax.axis_size("space")
    n_dir = lax.axis_size("dir")
    first_swap = [(i ^ 1, i) for i in range(n_space)]
    second_swap = [(i, j) for k in range(1, n_space - 1, 2) for i, j in ((k, k + 1), (k + 1, k))]

    flat = currents.reshape(32, 64, 256)
    inner = lax.ppermute(flat, "space", first_swap)
    outer = lax.ppermute(flat, "space", second_swap)

    leaf = call(
        leaf_kernel,
        [((272, 128), I16)] * 4,
        [currents, radiate, trans_one, trans_two],
        [
            pltpu.VMEM((32, 2, 32, 256), BF16),
            pltpu.VMEM((32, 2, 32, 256), BF16),
            pltpu.VMEM((40, 2, 128), F32),
            pltpu.VMEM((40, 2, 512), F32),
            pltpu.VMEM((4, 128, 128), F32),
            pltpu.VMEM((4, 272, 128), I16),
        ],
        6,
        LARGE,
        "leaf",
        limit=62,
    )
    own_leaf = leaf[0]
    leaf = [own_leaf] + [around(leaf[k], "dir", n_dir, k) for k in (1, 2, 3)]
    angle_room = [*[pltpu.VMEM((4, 512), F32)] * 2, *[pltpu.VMEM((4, 2048), F32)] * 2]
    packed = call(
        pack_kernel,
        [((1040, 128), I16)] * 4 + [((4, 512), F32)] * 2 + [((4, 2048), F32)] * 2,
        list(after_all((receive, phase_one, phase_two), own_leaf)),
        [
            pltpu.VMEM((32, 2, 32, 256), F32),
            pltpu.VMEM((4, 512), F32),
            pltpu.VMEM((4, 2048), F32),
            *angle_room,
            pltpu.VMEM((4, 1040, 128), I16),
        ],
        8,
        SMALL,
        "pack",
    )
    packed, angles = packed[:4], packed[4:]
    leaf, packed = lax.optimization_barrier((leaf, packed))
    packed = [packed[0]] + [around(packed[k], "dir", n_dir, k) for k in (1, 2, 3)]


    parent, halo, message = call(
        lift_kernel,
        [((8, 2, 8, 512), F32), ((128, 512), BF16), ((32, 16, 128), F32)],
        leaf + [interp_one, interp_two] + list(angles),
        [
            pltpu.VMEM((512, 128), F32),
            pltpu.VMEM((2048, 512), F32),
            *angle_room,
            pltpu.VMEM((8, 2, 8, 512), F32),
            pltpu.VMEM((128, 512), BF16),
            pltpu.VMEM((32, 16, 128), F32),
            pltpu.VMEM((4, 272, 128), I16),
            pltpu.VMEM((4, 128, 128), F32),
            pltpu.VMEM((2, 4, 2, 8, 2048), F32),
        ],
        16,
        LARGE,
        "lift",
        landed=(1, 2, 3),
    )
    top = lax.all_to_all(message, "space", 0, 0)
    parents_inner = lax.ppermute(halo, "space", first_swap)
    parents_outer = lax.ppermute(halo, "space", second_swap)

    top, inner, outer = lax.optimization_barrier((top, inner, outer))
    (moved,) = call(
        top_kernel,
        [((64, 8, 128), F32)],
        [kind_two.T, list_two.T, top.reshape(64, 8, 128)] + leaf,
        [
            pltpu.SMEM((8, 64), I32),
            pltpu.SMEM((8, 64), I32),
            pltpu.VMEM((64, 8, 128), F32),
            pltpu.VMEM((4, 144, 128), I16),
            pltpu.VMEM((40, 128), F32),
            pltpu.VMEM((40, 128), F32),
            pltpu.VMEM((64, 8, 128), F32),
        ],
        7,
        LARGE,
        "translate_two",
        landed=(2, 4, 5, 6),
    )
    moved, parents_inner, parents_outer = lax.optimization_barrier((moved, parents_inner, parents_outer))
    arrived = lax.all_to_all(moved.reshape(32, 16, 128), "space", 0, 0)

    near_parts = [near_half(half, near_list.T, near_count, inner, flat, outer, near_blocks) for half in (0, 1)]
    (near_one,) = call(
        parent_kernel,
        [((8, 2, 8, 512), F32)],
        [kind_one, list_one, parents_inner, parent, parents_outer] + leaf,
        [
            pltpu.SMEM((8, 8), I32),
            pltpu.SMEM((8, 8), I32),
            pltpu.VMEM((128, 512), BF16),
            pltpu.VMEM((128, 512), BF16),
            pltpu.VMEM((24, 2, 8, 512), F32),
            pltpu.VMEM((4, 96, 128), I16),
            pltpu.VMEM((4, 80, 128), F32),
            pltpu.VMEM((8, 2, 8, 512), F32),
        ],
        9,
        SMALL,
        "translate_one",
        landed=(2, 4, 6, 7, 8),
    )

    arrived, near_one, near_parts[0], packed = lax.optimization_barrier((arrived, near_one, near_parts[0], packed))
    (lowered,) = call(
        lower_kernel,
        [((528, 128), I16)],
        [arrived, near_one] + list(angles) + [interp_one, interp_two],
        [
            *angle_room,
            pltpu.VMEM((512, 128), F32),
            pltpu.VMEM((2048, 512), F32),
            pltpu.VMEM((32, 16, 128), F32),
            pltpu.VMEM((8, 2, 8, 512), F32),
            pltpu.VMEM((128, 2048), BF16),
            pltpu.VMEM((128, 2048), BF16),
            pltpu.VMEM((512, 128), F32),
            pltpu.VMEM((528, 128), I16),
        ],
        11,
        LARGE,
        "lower",
        landed=(0,),
    )
    shared = [around(lowered, "dir", n_dir, k) for k in (1, 2, 3)]

    (fields,) = call(
        receive_kernel,
        [((32, 2, 32, 64), F32)],
        [lowered] + shared + packed + near_parts,
        [
            pltpu.VMEM((4, 528, 128), I16),
            pltpu.VMEM((4, 1040, 128), I16),
            pltpu.VMEM((4, 8, 2, 4, 8, 128), F32),
            pltpu.VMEM((32, 4, 32, 128), F32),
            pltpu.VMEM((32, 64, 128), F32),
            pltpu.VMEM((32, 2, 32, 64), F32),
        ],
        14,
        LARGE,
        "receive",
        landed=(1, 2, 3, 5, 6, 7),
    )
    return fields


def solution(mesh):
    in_specs = (
        P("space", None, None, None),
        P("space", None, None, "dir", None),
        P("space", None),
        P("space"),
        P("space", None, "dir", None),
        P("space", None, "dir", None),
        P(),
        P(),
        P(),
        P(),
        P(None, None, "dir"),
        P("space", None),
        P("space", None),
        P(None, None, "dir"),
        P(),
        P(),
    )
    out_specs = P("space", None, None, "dir")
    return jax.shard_map(shards, mesh=mesh, in_specs=in_specs, out_specs=out_specs, check_vma=False)
```

```python
import functools

import jax
import jax.numpy as jnp
from jax import lax
from jax.experimental import pallas as pl
from jax.experimental.pallas import tpu as pltpu
from jax.sharding import PartitionSpec as P

F32 = jnp.float32
BF16 = jnp.bfloat16
I32 = jnp.int32
I16 = jnp.int16
IN_HBM = pl.BlockSpec(memory_space=pltpu.HBM)
ANYWHERE = pl.BlockSpec(memory_space=pl.ANY)
NEAR_FIRST = 12
MIB = 1024 * 1024
SMALL = 2**12
LARGE = 2**36


def call(kernel, outs, operands, scratch, copies, cost, name, landed=(), limit=52):
    shapes = tuple(jax.ShapeDtypeStruct(shape, kind) for shape, kind in outs)
    return pl.pallas_call(
        kernel,
        out_shape=shapes,
        in_specs=[ANYWHERE if n in landed else IN_HBM for n in range(len(operands))],
        out_specs=tuple(IN_HBM for _ in outs),
        scratch_shapes=[*scratch, pltpu.SemaphoreType.DMA((copies,))],
        compiler_params=pltpu.CompilerParams(vmem_limit_bytes=limit * MIB),
        cost_estimate=pl.CostEstimate(flops=cost, bytes_accessed=cost, transcendentals=0),
        name=name,
    )(*operands)


def begin(sems, *pairs, first=0):
    copies = [pltpu.make_async_copy(source, target, sems.at[first + n]) for n, (source, target) in enumerate(pairs)]
    for copy in copies:
        copy.start()
    return copies


def finish(*copies):
    for copy in copies:
        copy.wait()


def rows_by_rows(a, b):
    return lax.dot_general(a, b, (((1,), (1,)), ((), ())), preferred_element_type=F32)


def rows_by_cols(a, b):
    return lax.dot_general(a, b, (((1,), (0,)), ((), ())), preferred_element_type=F32)


def halves(x):
    high = x.astype(BF16)
    return high, (x - high.astype(F32)).astype(BF16)


def product(dot, x, high, low):
    x_high, x_low = halves(x)
    return dot(x_high, high) + (dot(x_high, low) + dot(x_low, high))


def lanes_of(shape):
    return lax.broadcasted_iota(I32, shape, len(shape) - 1)


def swap_half(x):
    return pltpu.roll(x, 64, x.ndim - 1)


def sender(k):
    return lax.rem(lax.axis_index("dir") + 4 - k, 4)


def receiver(k):
    return lax.rem(lax.axis_index("dir") + k, 4)


def power_of(largest):
    return jnp.ceil(jnp.log2(jnp.maximum(largest, 2.0**-100)))


def code_of(scaled):
    return jnp.round(scaled).astype(I32).astype(I16)


def value_of(code):
    return code.astype(I32).astype(F32)


def scale_from(power):
    return jnp.exp2(-power) * 32767.0


def unit_from(power):
    return jnp.exp2(power) * (1.0 / 32767.0)


def unit_of(rows):
    return unit_from(value_of(rows)[0:1])


def leaf_kernel(cur_from, rad_from, one_from, two_from, out0, out1, out2, out3, cur, rad, one, trans, held, codes, sems):
    near_half, far_half = slice(0, 16), slice(16, 32)
    copies = begin(
        sems,
        (cur_from.at[near_half], cur.at[near_half]),
        (rad_from.at[near_half], rad.at[near_half]),
        (cur_from.at[far_half], cur.at[far_half]),
        (rad_from.at[far_half], rad.at[far_half]),
        (one_from, one),
        (two_from, trans),
    )
    lane = lanes_of((32, 128)) // 32
    for p in range(8):
        if p == 0:
            finish(*copies[0:2])
        if p == 4:
            finish(*copies[2:4])
        boxes = cur[4 * p : 4 * p + 4].reshape(256, 256)
        re_rows = rad[4 * p : 4 * p + 4, 0].reshape(128, 256)
        im_rows = rad[4 * p : 4 * p + 4, 1].reshape(128, 256)
        with_re = rows_by_rows(boxes, re_rows)
        with_im = rows_by_rows(boxes, im_rows)
        re = jnp.zeros((32, 128), F32)
        im = jnp.zeros((32, 128), F32)
        for j in range(4):
            a = with_re[64 * j : 64 * j + 64]
            b = with_im[64 * j : 64 * j + 64]
            re = jnp.where(lane == j, a[:32] - b[32:], re)
            im = jnp.where(lane == j, a[32:] + b[:32], im)
        for e in range(4):
            held[e, 16 * p : 16 * p + 8] = re[8 * e : 8 * e + 8]
            held[e, 16 * p + 8 : 16 * p + 16] = im[8 * e : 8 * e + 8]
    finish(*copies[4:6])
    part = lax.rem(lax.axis_index("space"), 8)
    at = pl.ds(pl.multiple_of(part // 2 * 128, 128), 128)
    odd = part % 2
    re = trans[:, 0, at]
    im = trans[:, 1, at]
    lane = lanes_of((40, 128)) < 64
    even_cut = jnp.where(lane, re, swap_half(im))
    odd_cut = jnp.where(lane, swap_half(re), im)
    cut = jnp.where(odd == 1, odd_cut, even_cut)
    cut = jnp.concatenate([cut, jnp.zeros((8, 128), F32)], axis=0)
    table = jnp.concatenate([one[:, 0, :], one[:, 1, :]], axis=0)
    row = lax.broadcasted_iota(I32, (16, 128), 0)
    powers = jnp.zeros((16, 128), F32)
    coded = []
    for n, values in enumerate((held[...], cut, table)):
        flat = jnp.abs(values).reshape(-1, 128)
        power = power_of(jnp.max(flat, keepdims=True))
        powers = jnp.where(row == n, power, powers)
        coded.append(code_of(values.reshape(-1, 128) * scale_from(power)))
    for e in range(4):
        codes[e, 0:128] = coded[0][128 * e : 128 * e + 128]
        codes[e, 128:176] = coded[1]
        codes[e, 176:256] = coded[2]
        codes[e, 256:272] = powers.astype(I32).astype(I16)
    finish(*begin(sems, *[(codes.at[receiver(k)], out) for k, out in enumerate((out0, out1, out2, out3))]))


def pack_kernel(rec_from, one_from, two_from, *refs):
    outs = refs[:4]
    angles_to = refs[4:8]
    rec, one, two, cos1, sin1, cos2, sin2, held, sems = refs[8:]
    copies = begin(
        sems, (one_from, one), (two_from, two), (rec_from.at[0:16], rec.at[0:16]), (rec_from.at[16:32], rec.at[16:32])
    )
    finish(*copies[0:2])
    cos1[...] = jnp.cos(one[...])
    sin1[...] = jnp.sin(one[...])
    cos2[...] = jnp.cos(two[...])
    sin2[...] = jnp.sin(two[...])
    angle_copies = begin(sems, *zip((cos1, sin1, cos2, sin2), angles_to), first=4)
    largest = jnp.zeros((32, 256), F32)
    for t in range(2):
        finish(copies[2 + t])

        def look(b, found):
            return jnp.maximum(found, jnp.maximum(jnp.abs(rec[b, 0]), jnp.abs(rec[b, 1])))

        largest = lax.fori_loop(16 * t, 16 * t + 16, look, largest, unroll=4)
    power = power_of(jnp.max(largest, keepdims=True))
    unit = scale_from(power)
    for e in range(4):
        held[e, 1024:1040] = jnp.broadcast_to(power, (16, 128)).astype(I32).astype(I16)
    lane = lanes_of((32, 128)) < 64

    def body(b, carry):
        rows = pl.ds(pl.multiple_of(b * 32, 32), 32)
        for m in range(2):
            re = rec[b, 0, :, 128 * m : 128 * m + 128] * unit
            im = rec[b, 1, :, 128 * m : 128 * m + 128] * unit
            held[2 * m, rows, :] = code_of(jnp.where(lane, re, swap_half(im)))
            held[2 * m + 1, rows, :] = code_of(jnp.where(lane, swap_half(re), im))
        return carry

    lax.fori_loop(0, 32, body, 0, unroll=4)
    finish(*begin(sems, *[(held.at[receiver(k)], out) for k, out in enumerate(outs)]), *angle_copies)


def lift_kernel(r0, r1, r2, r3, *refs):
    one_from, two_from, *angles_from = refs[:6]
    parent_to, halo_to, message_to = refs[6:9]
    one, two, cos1, sin1, cos2, sin2 = refs[9:15]
    parent, halo, message, codes, held, top, sems = refs[15:]
    copies = begin(
        sems,
        *[(r, codes.at[sender(k)]) for k, r in enumerate((r0, r1, r2, r3))],
        (one_from, one),
        *zip(angles_from, (cos1, sin1, cos2, sin2)),
        *[(two_from.at[512 * t : 512 * t + 512], two.at[512 * t : 512 * t + 512]) for t in range(4)],
    )
    finish(*copies[0:9])
    for e in range(4):
        held[e] = value_of(codes[e, 0:128]) * unit_of(codes[e, 256:272])
    w1h, w1l = halves(one[...])
    lane = lanes_of((128, 128)) // 32
    rows = []
    for j in range(4):
        x = jnp.zeros((128, 128), F32)
        for e in range(4):
            piece = held[e]
            shift = (32 * (e - j)) % 128
            if shift:
                piece = pltpu.roll(piece, shift, 1)
            x = jnp.where(lane == e, piece, x)
        rows.append(x)
    up = product(rows_by_rows, jnp.concatenate(rows, axis=0), w1h, w1l)
    up = up.reshape(4, 8, 2, 8, 512)
    re = jnp.zeros((8, 8, 512), F32)
    im = jnp.zeros((8, 8, 512), F32)
    for j in range(4):
        c = cos1[j : j + 1, :][None]
        s = sin1[j : j + 1, :][None]
        re = re + (c * up[j, :, 0] - s * up[j, :, 1])
        im = im + (c * up[j, :, 1] + s * up[j, :, 0])
    parent[:, 0] = re
    parent[:, 1] = im
    whole = parent[...].reshape(128, 512)
    halo[...] = whole.astype(BF16)
    copies += begin(sems, (parent, parent_to), (halo, halo_to), first=13)
    x_high, x_low = halves(whole)
    lane = lanes_of((16, 128)) < 64
    for t in range(4):
        finish(copies[9 + t])
        rows = slice(512 * t, 512 * t + 512)
        high, low = halves(two[rows, :])
        part = rows_by_rows(x_high, high) + (rows_by_rows(x_high, low) + rows_by_rows(x_low, high))
        top[t] = part.reshape(2, 4, 2, 8, 512)
        for n in range(4):
            m = 4 * t + n
            at = slice(128 * m, 128 * m + 128)
            here = slice(128 * n, 128 * n + 128)
            re = jnp.zeros((2, 8, 128), F32)
            im = jnp.zeros((2, 8, 128), F32)
            for j in range(4):
                c = cos2[j : j + 1, at][None]
                s = sin2[j : j + 1, at][None]
                u_re = top[t, :, j, 0, :, here]
                u_im = top[t, :, j, 1, :, here]
                re = re + (c * u_re - s * u_im)
                im = im + (c * u_im + s * u_re)
            re = re.reshape(16, 128)
            im = im.reshape(16, 128)
            message[2 * m] = jnp.where(lane, re, swap_half(im))
            message[2 * m + 1] = jnp.where(lane, swap_half(re), im)
        done = slice(8 * t, 8 * t + 8)
        copies += begin(sems, (message.at[done], message_to.at[done]), first=15 + t)
    finish(*copies[13:])


def top_kernel(kinds_from, lists_from, top_from, m0, m1, m2, m3, out_to, kinds, lists, top, cuts, first, second, out, sems):
    finish(
        *begin(
            sems,
            (kinds_from, kinds),
            (lists_from, lists),
            (top_from, top),
            *[(m.at[128:272], cuts.at[sender(k)]) for k, m in enumerate((m0, m1, m2, m3))],
        )
    )
    chosen = lax.axis_index("space") // 8
    unit = unit_from(value_of(cuts[chosen, 128:144])[1:2])
    table = (value_of(cuts[chosen, 0:48]) * unit)[0:40]
    lane = lanes_of((40, 128)) < 64
    turned = swap_half(table)
    first[...] = jnp.where(lane, table, turned)
    second[...] = jnp.where(lane, turned, -table)

    def body(g, carry):
        straight = jnp.zeros((8, 128), F32)
        crossed = jnp.zeros((8, 128), F32)
        for k in range(8):
            kind = kinds[k, g]
            value = top[lists[k, g]]
            straight = straight + first[pl.ds(kind, 1), :] * value
            crossed = crossed + second[pl.ds(kind, 1), :] * value
        out[g] = straight + swap_half(crossed)
        return carry

    lax.fori_loop(0, 64, body, 0, unroll=8)
    finish(*begin(sems, (out, out_to)))


def parent_kernel(
    kinds_from, lists_from, inner_from, parent_from, outer_from, m0, m1, m2, m3,
    out_to,
    kinds, lists, inner, outer, held, codes, table, out, sems,
):
    finish(
        *begin(
            sems,
            (kinds_from, kinds),
            (lists_from, lists),
            (inner_from, inner),
            (parent_from, held.at[8:16]),
            (outer_from, outer),
            *[(m.at[176:272], codes.at[sender(k)]) for k, m in enumerate((m0, m1, m2, m3))],
        )
    )
    base = lax.axis_index("space") * 8 - 8
    for e in range(4):
        table[e] = value_of(codes[e, 0:80]) * unit_from(value_of(codes[e, 80:96])[2:3])
    odd = lax.rem(lax.axis_index("space"), 2)
    held[pl.ds(16 - 16 * odd, 8)] = inner[...].astype(F32).reshape(8, 2, 8, 512)
    held[pl.ds(16 * odd, 8)] = outer[...].astype(F32).reshape(8, 2, 8, 512)

    def body(p, carry):
        re = [jnp.zeros((8, 128), F32) for _ in range(4)]
        im = [jnp.zeros((8, 128), F32) for _ in range(4)]
        for k in range(8):
            kind = kinds[p, k]
            source = lists[p, k] - base
            for m in range(4):
                at = slice(128 * m, 128 * m + 128)
                s_re = held[source, 0, :, at]
                s_im = held[source, 1, :, at]
                c_re = table[m, pl.ds(kind, 1), :]
                c_im = table[m, pl.ds(kind + 40, 1), :]
                re[m] = re[m] + (c_re * s_re - c_im * s_im)
                im[m] = im[m] + (c_re * s_im + c_im * s_re)
        for m in range(4):
            at = slice(128 * m, 128 * m + 128)
            out[p, 0, :, at] = re[m]
            out[p, 1, :, at] = im[m]
        return carry

    lax.fori_loop(0, 8, body, 0)
    finish(*begin(sems, (out, out_to)))


def lower_kernel(arrived_from, near_one_from, *refs):
    sources = refs[:6]
    out_to = refs[6]
    cos1, sin1, cos2, sin2, one, two = refs[7:13]
    arrived, near_one, child_high, child_low, held, out, sems = refs[13:]
    copies = begin(
        sems,
        (arrived_from, arrived),
        (near_one_from, near_one),
        *zip(sources[:5], refs[7:12]),
        *[(sources[5].at[512 * t : 512 * t + 512], two.at[512 * t : 512 * t + 512]) for t in range(4)],
    )
    finish(copies[0], *copies[4:6])
    lane = lanes_of((16, 128)) < 64
    for m in range(16):
        at = slice(128 * m, 128 * m + 128)
        a = arrived[2 * m]
        b = arrived[2 * m + 1]
        re = jnp.where(lane, a, swap_half(b)).reshape(2, 8, 128)
        im = jnp.where(lane, swap_half(a), b).reshape(2, 8, 128)
        for j in range(4):
            c = cos2[j : j + 1, at][None]
            s = sin2[j : j + 1, at][None]
            both = jnp.concatenate([(c * re + s * im)[:, None], (c * im - s * re)[:, None]], axis=1)
            high, low = halves(both.reshape(2, 16, 128))
            for g in range(2):
                rows = slice(64 * g + 16 * j, 64 * g + 16 * j + 16)
                child_high[rows, at] = high[g]
                child_low[rows, at] = low[g]
    local = jnp.zeros((128, 512), F32)
    for t in range(4):
        finish(copies[7 + t])
        at = slice(512 * t, 512 * t + 512)
        high = child_high[:, at]
        w2h, w2l = halves(two[at, :])
        local = local + (rows_by_cols(high, w2h) + (rows_by_cols(high, w2l) + rows_by_cols(child_low[:, at], w2h)))
    finish(*copies[1:4], copies[6])
    w1h, w1l = halves(one[...])
    local = local.reshape(8, 2, 8, 512) + near_one[...]
    re = local[:, 0]
    im = local[:, 1]
    for j in range(4):
        c = cos1[j : j + 1, :][None]
        s = sin1[j : j + 1, :][None]
        both = jnp.concatenate([(c * re + s * im)[:, None], (c * im - s * re)[:, None]], axis=1)
        down = product(rows_by_cols, both.reshape(128, 512), w1h, w1l)
        held[128 * j : 128 * j + 128] = down
    largest = jnp.max(jnp.abs(held[...]), keepdims=True)
    power = power_of(largest)
    out[0:512] = code_of(held[...] * scale_from(power))
    out[512:528] = jnp.broadcast_to(power, (16, 128)).astype(I32).astype(I16)
    finish(*begin(sems, (out, out_to)))


def near_kernel(start, groups, lists_from, counts_from, inner, current, outer, blocks_from, out_to, lists, counts, held, blocks, out, sems):
    odd = lax.rem(lax.axis_index("space"), 2)
    copies = begin(
        sems,
        (lists_from, lists),
        (counts_from, counts),
        (inner, held.at[pl.ds(64 - 64 * odd, 32)]),
        (current, held.at[32:64]),
        (outer, held.at[pl.ds(64 * odd, 32)]),
        *[
            (blocks_from.at[start + 4 * t : start + 4 * t + 4], blocks.at[4 * t : 4 * t + 4])
            for t in range(groups)
        ],
    )
    held[96] = jnp.zeros((64, 256), BF16)
    finish(*copies[0:5])
    base = lax.axis_index("space") * 32 - 32

    for t in range(groups):
        finish(copies[5 + t])

        def body(n, carry):
            for row in (4 * t + 2 * n, 4 * t + 2 * n + 1):
                box = start + row
                total = jnp.zeros((64, 128), F32)
                for k in range(6):
                    source = jnp.where(k < counts[box], lists[k, box] - base, 96)
                    total = total + rows_by_rows(held[source], blocks[row, k].reshape(128, 256))
                out[row] = total
            return carry

        lax.fori_loop(0, 2, body, 0, unroll=2)
        copies += begin(sems, (out.at[4 * t : 4 * t + 4], out_to.at[4 * t : 4 * t + 4]), first=5 + groups + t)
    finish(*copies[5 + groups :])


def receive_kernel(l0, l1, l2, l3, x0, x1, x2, x3, near_first, near_second, out_to, codes, packs, samples, matrix, near, out, sems):
    copies = begin(
        sems,
        *[(l, codes.at[k]) for k, l in enumerate((l0, l1, l2, l3))],
        *[(x, packs.at[k]) for k, x in enumerate((x0, x1, x2, x3))],
        (near_first, near.at[0:NEAR_FIRST]),
        (near_second, near.at[NEAR_FIRST:32]),
    )
    finish(*copies[0:4])
    for k in range(4):
        values = value_of(codes[k, 0:512]) * unit_of(codes[k, 512:528])
        samples[:, :, :, sender(k)] = values.reshape(4, 8, 2, 8, 128)
    finish(*copies[4:10])
    units = [unit_of(packs[k, 1024:1040]) for k in range(4)]

    def body(p, carry):
        for j in range(4):
            b = 4 * p + j
            rows = pl.ds(pl.multiple_of(32 * b, 32), 32)
            for k in range(4):
                matrix[b, sender(k)] = value_of(packs[k, rows, :]) * units[k]
            left_high, left_low = halves(samples[j, p].reshape(64, 128))
            high, low = halves(matrix[b].reshape(128, 128))
            left = jnp.concatenate([left_high, left_low], axis=1)
            right = jnp.concatenate(
                [jnp.concatenate([high, low], axis=1), jnp.concatenate([high, jnp.zeros_like(low)], axis=1)], axis=0
            )
            both = rows_by_cols(left, right)
            total = near[b] + (both[:, :128] + both[:, 128:])
            turned = swap_half(total)
            out[b, 0] = (total[:32] - turned[32:])[:, :64]
            out[b, 1] = (total[32:] + turned[:32])[:, :64]
        return carry

    for t in range(4):
        lax.fori_loop(2 * t, 2 * t + 2, body, 0, unroll=2)
        part = slice(8 * t, 8 * t + 8)
        copies += begin(sems, (out.at[part], out_to.at[part]), first=10 + t)
    finish(*copies[10:])


def near_part(start, boxes, *operands):
    return call(
        functools.partial(near_kernel, start, boxes // 4),
        [((boxes, 64, 128), F32)],
        list(operands),
        [
            pltpu.SMEM((6, 32), I32),
            pltpu.SMEM((32,), I32),
            pltpu.VMEM((97, 64, 256), BF16),
            pltpu.VMEM((boxes, 6, 2, 64, 256), BF16),
            pltpu.VMEM((boxes, 64, 128), F32),
        ],
        5 + boxes // 2,
        SMALL,
        "near",
        limit=60,
        landed=(2, 4),
    )[0]


def around(x, axis, peers, k):
    return lax.ppermute(x, axis, [(i, (i + k) % peers) for i in range(peers)])


def after_all(values, *tokens):
    return lax.optimization_barrier((*values, *tokens))[: len(values)]


def shards(
    currents,
    near_blocks,
    near_list,
    near_count,
    radiate,
    receive,
    phase_one,
    phase_two,
    interp_one,
    interp_two,
    trans_one,
    kind_one,
    list_one,
    trans_two,
    kind_two,
    list_two,
):
    n_space = lax.axis_size("space")
    n_dir = lax.axis_size("dir")
    first_swap = [(i ^ 1, i) for i in range(n_space)]
    second_swap = [(i, j) for k in range(1, n_space - 1, 2) for i, j in ((k, k + 1), (k + 1, k))]

    flat = currents.reshape(32, 64, 256)
    inner = lax.ppermute(flat, "space", first_swap)
    outer = lax.ppermute(flat, "space", second_swap)

    leaf = call(
        leaf_kernel,
        [((272, 128), I16)] * 4,
        [currents, radiate, trans_one, trans_two],
        [
            pltpu.VMEM((32, 2, 32, 256), BF16),
            pltpu.VMEM((32, 2, 32, 256), BF16),
            pltpu.VMEM((40, 2, 128), F32),
            pltpu.VMEM((40, 2, 512), F32),
            pltpu.VMEM((4, 128, 128), F32),
            pltpu.VMEM((4, 272, 128), I16),
        ],
        6,
        LARGE,
        "leaf",
        limit=62,
    )
    own_leaf = leaf[0]
    leaf = [own_leaf] + [around(leaf[k], "dir", n_dir, k) for k in (1, 2, 3)]
    angle_room = [*[pltpu.VMEM((4, 512), F32)] * 2, *[pltpu.VMEM((4, 2048), F32)] * 2]
    packed = call(
        pack_kernel,
        [((1040, 128), I16)] * 4 + [((4, 512), F32)] * 2 + [((4, 2048), F32)] * 2,
        list(after_all((receive, phase_one, phase_two), own_leaf)),
        [
            pltpu.VMEM((32, 2, 32, 256), F32),
            pltpu.VMEM((4, 512), F32),
            pltpu.VMEM((4, 2048), F32),
            *angle_room,
            pltpu.VMEM((4, 1040, 128), I16),
        ],
        8,
        SMALL,
        "pack",
    )
    packed, angles = packed[:4], packed[4:]
    leaf, packed = lax.optimization_barrier((leaf, packed))
    packed = [packed[0]] + [around(packed[k], "dir", n_dir, k) for k in (1, 2, 3)]


    parent, halo, message = call(
        lift_kernel,
        [((8, 2, 8, 512), F32), ((128, 512), BF16), ((32, 16, 128), F32)],
        leaf + [interp_one, interp_two] + list(angles),
        [
            pltpu.VMEM((512, 128), F32),
            pltpu.VMEM((2048, 512), F32),
            *angle_room,
            pltpu.VMEM((8, 2, 8, 512), F32),
            pltpu.VMEM((128, 512), BF16),
            pltpu.VMEM((32, 16, 128), F32),
            pltpu.VMEM((4, 272, 128), I16),
            pltpu.VMEM((4, 128, 128), F32),
            pltpu.VMEM((4, 2, 4, 2, 8, 512), F32),
        ],
        19,
        LARGE,
        "lift",
        landed=(1, 2, 3),
    )
    top = lax.all_to_all(message, "space", 0, 0)
    parents_inner = lax.ppermute(halo, "space", first_swap)
    parents_outer = lax.ppermute(halo, "space", second_swap)

    top, inner, outer = lax.optimization_barrier((top, inner, outer))
    (moved,) = call(
        top_kernel,
        [((64, 8, 128), F32)],
        [kind_two.T, list_two.T, top.reshape(64, 8, 128)] + leaf,
        [
            pltpu.SMEM((8, 64), I32),
            pltpu.SMEM((8, 64), I32),
            pltpu.VMEM((64, 8, 128), F32),
            pltpu.VMEM((4, 144, 128), I16),
            pltpu.VMEM((40, 128), F32),
            pltpu.VMEM((40, 128), F32),
            pltpu.VMEM((64, 8, 128), F32),
        ],
        7,
        LARGE,
        "translate_two",
        landed=(2, 4, 5, 6),
    )
    moved, parents_inner, parents_outer = lax.optimization_barrier((moved, parents_inner, parents_outer))
    arrived = lax.all_to_all(moved.reshape(32, 16, 128), "space", 0, 0)

    near_parts = [
        near_part(start, boxes, near_list.T, near_count, inner, flat, outer, near_blocks)
        for start, boxes in ((0, NEAR_FIRST), (NEAR_FIRST, 32 - NEAR_FIRST))
    ]
    (near_one,) = call(
        parent_kernel,
        [((8, 2, 8, 512), F32)],
        [kind_one, list_one, parents_inner, parent, parents_outer] + leaf,
        [
            pltpu.SMEM((8, 8), I32),
            pltpu.SMEM((8, 8), I32),
            pltpu.VMEM((128, 512), BF16),
            pltpu.VMEM((128, 512), BF16),
            pltpu.VMEM((24, 2, 8, 512), F32),
            pltpu.VMEM((4, 96, 128), I16),
            pltpu.VMEM((4, 80, 128), F32),
            pltpu.VMEM((8, 2, 8, 512), F32),
        ],
        9,
        SMALL,
        "translate_one",
        landed=(2, 4, 6, 7, 8),
    )

    arrived, near_one, near_parts[0], packed = lax.optimization_barrier((arrived, near_one, near_parts[0], packed))
    (lowered,) = call(
        lower_kernel,
        [((528, 128), I16)],
        [arrived, near_one] + list(angles) + [interp_one, interp_two],
        [
            *angle_room,
            pltpu.VMEM((512, 128), F32),
            pltpu.VMEM((2048, 512), F32),
            pltpu.VMEM((32, 16, 128), F32),
            pltpu.VMEM((8, 2, 8, 512), F32),
            pltpu.VMEM((128, 2048), BF16),
            pltpu.VMEM((128, 2048), BF16),
            pltpu.VMEM((512, 128), F32),
            pltpu.VMEM((528, 128), I16),
        ],
        11,
        LARGE,
        "lower",
        landed=(0,),
    )
    shared = [around(lowered, "dir", n_dir, k) for k in (1, 2, 3)]

    (fields,) = call(
        receive_kernel,
        [((32, 2, 32, 64), F32)],
        [lowered] + shared + packed + near_parts,
        [
            pltpu.VMEM((4, 528, 128), I16),
            pltpu.VMEM((4, 1040, 128), I16),
            pltpu.VMEM((4, 8, 2, 4, 8, 128), F32),
            pltpu.VMEM((32, 4, 32, 128), F32),
            pltpu.VMEM((32, 64, 128), F32),
            pltpu.VMEM((32, 2, 32, 64), F32),
        ],
        14,
        LARGE,
        "receive",
        landed=(1, 2, 3, 5, 6, 7),
    )
    return fields


def solution(mesh):
    in_specs = (
        P("space", None, None, None),
        P("space", None, None, "dir", None),
        P("space", None),
        P("space"),
        P("space", None, "dir", None),
        P("space", None, "dir", None),
        P(),
        P(),
        P(),
        P(),
        P(None, None, "dir"),
        P("space", None),
        P("space", None),
        P(None, None, "dir"),
        P(),
        P(),
    )
    out_specs = P("space", None, None, "dir")
    return jax.shard_map(shards, mesh=mesh, in_specs=in_specs, out_specs=out_specs, check_vma=False)
```

```python
import functools

import jax
import jax.numpy as jnp
from jax import lax
from jax.experimental import pallas as pl
from jax.experimental.pallas import tpu as pltpu
from jax.sharding import PartitionSpec as P

F32 = jnp.float32
BF16 = jnp.bfloat16
I32 = jnp.int32
I16 = jnp.int16
IN_HBM = pl.BlockSpec(memory_space=pltpu.HBM)
ANYWHERE = pl.BlockSpec(memory_space=pl.ANY)
NEAR_FIRST = 12
MIB = 1024 * 1024
SMALL = 2**12
LARGE = 2**36


def call(kernel, outs, operands, scratch, copies, cost, name, landed=(), limit=52):
    shapes = tuple(jax.ShapeDtypeStruct(shape, kind) for shape, kind in outs)
    return pl.pallas_call(
        kernel,
        out_shape=shapes,
        in_specs=[ANYWHERE if n in landed else IN_HBM for n in range(len(operands))],
        out_specs=tuple(IN_HBM for _ in outs),
        scratch_shapes=[*scratch, pltpu.SemaphoreType.DMA((copies,))],
        compiler_params=pltpu.CompilerParams(vmem_limit_bytes=limit * MIB),
        cost_estimate=pl.CostEstimate(flops=cost, bytes_accessed=cost, transcendentals=0),
        name=name,
    )(*operands)


def begin(sems, *pairs, first=0):
    copies = [pltpu.make_async_copy(source, target, sems.at[first + n]) for n, (source, target) in enumerate(pairs)]
    for copy in copies:
        copy.start()
    return copies


def finish(*copies):
    for copy in copies:
        copy.wait()


def rows_by_rows(a, b):
    return lax.dot_general(a, b, (((1,), (1,)), ((), ())), preferred_element_type=F32)


def rows_by_cols(a, b):
    return lax.dot_general(a, b, (((1,), (0,)), ((), ())), preferred_element_type=F32)


def halves(x):
    high = x.astype(BF16)
    return high, (x - high.astype(F32)).astype(BF16)


def product(dot, x, high, low):
    x_high, x_low = halves(x)
    return dot(x_high, high) + (dot(x_high, low) + dot(x_low, high))


def lanes_of(shape):
    return lax.broadcasted_iota(I32, shape, len(shape) - 1)


def swap_half(x):
    return pltpu.roll(x, 64, x.ndim - 1)


def sender(k):
    return lax.rem(lax.axis_index("dir") + 4 - k, 4)


def receiver(k):
    return lax.rem(lax.axis_index("dir") + k, 4)


def power_of(largest):
    return jnp.ceil(jnp.log2(jnp.maximum(largest, 2.0**-100)))


def code_of(scaled):
    return jnp.round(scaled).astype(I32).astype(I16)


def value_of(code):
    return code.astype(I32).astype(F32)


def scale_from(power):
    return jnp.exp2(-power) * 32767.0


def unit_from(power):
    return jnp.exp2(power) * (1.0 / 32767.0)


def unit_of(rows):
    return unit_from(value_of(rows)[0:1])


def leaf_kernel(cur_from, rad_from, one_from, two_from, out0, out1, out2, out3, cur, rad, one, trans, held, codes, sems):
    near_half, far_half = slice(0, 16), slice(16, 32)
    copies = begin(
        sems,
        (cur_from.at[near_half], cur.at[near_half]),
        (rad_from.at[near_half], rad.at[near_half]),
        (cur_from.at[far_half], cur.at[far_half]),
        (rad_from.at[far_half], rad.at[far_half]),
        (one_from, one),
        (two_from, trans),
    )
    lane = lanes_of((32, 128)) // 32
    for p in range(8):
        if p == 0:
            finish(*copies[0:2])
        if p == 4:
            finish(*copies[2:4])
        boxes = cur[4 * p : 4 * p + 4].reshape(256, 256)
        re_rows = rad[4 * p : 4 * p + 4, 0].reshape(128, 256)
        im_rows = rad[4 * p : 4 * p + 4, 1].reshape(128, 256)
        with_re = rows_by_rows(boxes, re_rows)
        with_im = rows_by_rows(boxes, im_rows)
        re = jnp.zeros((32, 128), F32)
        im = jnp.zeros((32, 128), F32)
        for j in range(4):
            a = with_re[64 * j : 64 * j + 64]
            b = with_im[64 * j : 64 * j + 64]
            re = jnp.where(lane == j, a[:32] - b[32:], re)
            im = jnp.where(lane == j, a[32:] + b[:32], im)
        for e in range(4):
            held[e, 16 * p : 16 * p + 8] = re[8 * e : 8 * e + 8]
            held[e, 16 * p + 8 : 16 * p + 16] = im[8 * e : 8 * e + 8]
    finish(*copies[4:6])
    part = lax.rem(lax.axis_index("space"), 8)
    at = pl.ds(pl.multiple_of(part // 2 * 128, 128), 128)
    odd = part % 2
    re = trans[:, 0, at]
    im = trans[:, 1, at]
    lane = lanes_of((40, 128)) < 64
    even_cut = jnp.where(lane, re, swap_half(im))
    odd_cut = jnp.where(lane, swap_half(re), im)
    cut = jnp.where(odd == 1, odd_cut, even_cut)
    cut = jnp.concatenate([cut, jnp.zeros((8, 128), F32)], axis=0)
    table = jnp.concatenate([one[:, 0, :], one[:, 1, :]], axis=0)
    row = lax.broadcasted_iota(I32, (16, 128), 0)
    powers = jnp.zeros((16, 128), F32)
    coded = []
    for n, values in enumerate((held[...], cut, table)):
        flat = jnp.abs(values).reshape(-1, 128)
        power = power_of(jnp.max(flat, keepdims=True))
        powers = jnp.where(row == n, power, powers)
        coded.append(code_of(values.reshape(-1, 128) * scale_from(power)))
    for e in range(4):
        codes[e, 0:128] = coded[0][128 * e : 128 * e + 128]
        codes[e, 128:176] = coded[1]
        codes[e, 176:256] = coded[2]
        codes[e, 256:272] = powers.astype(I32).astype(I16)
    finish(*begin(sems, *[(codes.at[receiver(k)], out) for k, out in enumerate((out0, out1, out2, out3))]))


def pack_kernel(rec_from, one_from, two_from, *refs):
    outs = refs[:4]
    angles_to = refs[4:8]
    rec, one, two, cos1, sin1, cos2, sin2, held, sems = refs[8:]
    copies = begin(
        sems, (one_from, one), (two_from, two), (rec_from.at[0:16], rec.at[0:16]), (rec_from.at[16:32], rec.at[16:32])
    )
    finish(*copies[0:2])
    cos1[...] = jnp.cos(one[...])
    sin1[...] = jnp.sin(one[...])
    cos2[...] = jnp.cos(two[...])
    sin2[...] = jnp.sin(two[...])
    angle_copies = begin(sems, *zip((cos1, sin1, cos2, sin2), angles_to), first=4)
    largest = jnp.zeros((32, 256), F32)
    for t in range(2):
        finish(copies[2 + t])

        def look(b, found):
            return jnp.maximum(found, jnp.maximum(jnp.abs(rec[b, 0]), jnp.abs(rec[b, 1])))

        largest = lax.fori_loop(16 * t, 16 * t + 16, look, largest, unroll=4)
    power = power_of(jnp.max(largest, keepdims=True))
    unit = scale_from(power)
    for e in range(4):
        held[e, 1024:1040] = jnp.broadcast_to(power, (16, 128)).astype(I32).astype(I16)
    lane = lanes_of((32, 128)) < 64

    def body(b, carry):
        rows = pl.ds(pl.multiple_of(b * 32, 32), 32)
        for m in range(2):
            re = rec[b, 0, :, 128 * m : 128 * m + 128] * unit
            im = rec[b, 1, :, 128 * m : 128 * m + 128] * unit
            held[2 * m, rows, :] = code_of(jnp.where(lane, re, swap_half(im)))
            held[2 * m + 1, rows, :] = code_of(jnp.where(lane, swap_half(re), im))
        return carry

    lax.fori_loop(0, 32, body, 0, unroll=4)
    finish(*begin(sems, *[(held.at[receiver(k)], out) for k, out in enumerate(outs)]), *angle_copies)


def lift_kernel(r0, r1, r2, r3, *refs):
    one_from, two_from, *angles_from = refs[:6]
    parent_to, halo_to, message_to = refs[6:9]
    one, two, cos1, sin1, cos2, sin2 = refs[9:15]
    parent, halo, message, codes, held, top, sems = refs[15:]
    copies = begin(
        sems,
        *[(r, codes.at[sender(k)]) for k, r in enumerate((r0, r1, r2, r3))],
        (one_from, one),
        *zip(angles_from, (cos1, sin1, cos2, sin2)),
        *[(two_from.at[512 * t : 512 * t + 512], two.at[512 * t : 512 * t + 512]) for t in range(4)],
    )
    finish(*copies[0:9])
    for e in range(4):
        held[e] = value_of(codes[e, 0:128]) * unit_of(codes[e, 256:272])
    w1h, w1l = halves(one[...])
    lane = lanes_of((128, 128)) // 32
    rows = []
    for j in range(4):
        x = jnp.zeros((128, 128), F32)
        for e in range(4):
            piece = held[e]
            shift = (32 * (e - j)) % 128
            if shift:
                piece = pltpu.roll(piece, shift, 1)
            x = jnp.where(lane == e, piece, x)
        rows.append(x)
    up = product(rows_by_rows, jnp.concatenate(rows, axis=0), w1h, w1l)
    up = up.reshape(4, 8, 2, 8, 512)
    re = jnp.zeros((8, 8, 512), F32)
    im = jnp.zeros((8, 8, 512), F32)
    for j in range(4):
        c = cos1[j : j + 1, :][None]
        s = sin1[j : j + 1, :][None]
        re = re + (c * up[j, :, 0] - s * up[j, :, 1])
        im = im + (c * up[j, :, 1] + s * up[j, :, 0])
    parent[:, 0] = re
    parent[:, 1] = im
    whole = parent[...].reshape(128, 512)
    halo[...] = whole.astype(BF16)
    copies += begin(sems, (parent, parent_to), (halo, halo_to), first=13)
    x_high, x_low = halves(whole)
    for t in range(4):
        finish(copies[9 + t])
        rows = slice(512 * t, 512 * t + 512)
        high, low = halves(two[rows, :])
        part = rows_by_rows(x_high, high) + (rows_by_rows(x_high, low) + rows_by_rows(x_low, high))
        top[:, :, :, :, rows] = part.reshape(2, 4, 2, 8, 512)
    lane = lanes_of((16, 128)) < 64
    for m in range(16):
        at = slice(128 * m, 128 * m + 128)
        re = jnp.zeros((2, 8, 128), F32)
        im = jnp.zeros((2, 8, 128), F32)
        for j in range(4):
            c = cos2[j : j + 1, at][None]
            s = sin2[j : j + 1, at][None]
            u_re = top[:, j, 0, :, at]
            u_im = top[:, j, 1, :, at]
            re = re + (c * u_re - s * u_im)
            im = im + (c * u_im + s * u_re)
        re = re.reshape(16, 128)
        im = im.reshape(16, 128)
        message[2 * m] = jnp.where(lane, re, swap_half(im))
        message[2 * m + 1] = jnp.where(lane, swap_half(re), im)
    copies += begin(sems, (message, message_to), first=15)
    finish(*copies[13:])


def top_kernel(kinds_from, lists_from, top_from, m0, m1, m2, m3, out_to, kinds, lists, top, cuts, first, second, out, sems):
    finish(
        *begin(
            sems,
            (kinds_from, kinds),
            (lists_from, lists),
            (top_from, top),
            *[(m.at[128:272], cuts.at[sender(k)]) for k, m in enumerate((m0, m1, m2, m3))],
        )
    )
    chosen = lax.axis_index("space") // 8
    unit = unit_from(value_of(cuts[chosen, 128:144])[1:2])
    table = (value_of(cuts[chosen, 0:48]) * unit)[0:40]
    lane = lanes_of((40, 128)) < 64
    turned = swap_half(table)
    first[...] = jnp.where(lane, table, turned)
    second[...] = jnp.where(lane, turned, -table)

    def body(g, carry):
        straight = jnp.zeros((8, 128), F32)
        crossed = jnp.zeros((8, 128), F32)
        for k in range(8):
            kind = kinds[k, g]
            value = top[lists[k, g]]
            straight = straight + first[pl.ds(kind, 1), :] * value
            crossed = crossed + second[pl.ds(kind, 1), :] * value
        out[g] = straight + swap_half(crossed)
        return carry

    lax.fori_loop(0, 64, body, 0, unroll=8)
    finish(*begin(sems, (out, out_to)))


def parent_kernel(
    kinds_from, lists_from, inner_from, parent_from, outer_from, m0, m1, m2, m3,
    out_to,
    kinds, lists, inner, outer, held, codes, table, out, sems,
):
    finish(
        *begin(
            sems,
            (kinds_from, kinds),
            (lists_from, lists),
            (inner_from, inner),
            (parent_from, held.at[8:16]),
            (outer_from, outer),
            *[(m.at[176:272], codes.at[sender(k)]) for k, m in enumerate((m0, m1, m2, m3))],
        )
    )
    base = lax.axis_index("space") * 8 - 8
    for e in range(4):
        table[e] = value_of(codes[e, 0:80]) * unit_from(value_of(codes[e, 80:96])[2:3])
    odd = lax.rem(lax.axis_index("space"), 2)
    held[pl.ds(16 - 16 * odd, 8)] = inner[...].astype(F32).reshape(8, 2, 8, 512)
    held[pl.ds(16 * odd, 8)] = outer[...].astype(F32).reshape(8, 2, 8, 512)

    def body(p, carry):
        re = [jnp.zeros((8, 128), F32) for _ in range(4)]
        im = [jnp.zeros((8, 128), F32) for _ in range(4)]
        for k in range(8):
            kind = kinds[p, k]
            source = lists[p, k] - base
            for m in range(4):
                at = slice(128 * m, 128 * m + 128)
                s_re = held[source, 0, :, at]
                s_im = held[source, 1, :, at]
                c_re = table[m, pl.ds(kind, 1), :]
                c_im = table[m, pl.ds(kind + 40, 1), :]
                re[m] = re[m] + (c_re * s_re - c_im * s_im)
                im[m] = im[m] + (c_re * s_im + c_im * s_re)
        for m in range(4):
            at = slice(128 * m, 128 * m + 128)
            out[p, 0, :, at] = re[m]
            out[p, 1, :, at] = im[m]
        return carry

    lax.fori_loop(0, 8, body, 0)
    finish(*begin(sems, (out, out_to)))


def lower_kernel(arrived_from, near_one_from, *refs):
    sources = refs[:6]
    out_to = refs[6]
    cos1, sin1, cos2, sin2, one, two = refs[7:13]
    arrived, near_one, child_high, child_low, held, out, sems = refs[13:]
    copies = begin(
        sems,
        (arrived_from, arrived),
        (near_one_from, near_one),
        *zip(sources[:5], refs[7:12]),
        *[(sources[5].at[512 * t : 512 * t + 512], two.at[512 * t : 512 * t + 512]) for t in range(4)],
    )
    finish(copies[0], *copies[4:6])
    lane = lanes_of((16, 128)) < 64
    for m in range(16):
        at = slice(128 * m, 128 * m + 128)
        a = arrived[2 * m]
        b = arrived[2 * m + 1]
        re = jnp.where(lane, a, swap_half(b)).reshape(2, 8, 128)
        im = jnp.where(lane, swap_half(a), b).reshape(2, 8, 128)
        for j in range(4):
            c = cos2[j : j + 1, at][None]
            s = sin2[j : j + 1, at][None]
            both = jnp.concatenate([(c * re + s * im)[:, None], (c * im - s * re)[:, None]], axis=1)
            high, low = halves(both.reshape(2, 16, 128))
            for g in range(2):
                rows = slice(64 * g + 16 * j, 64 * g + 16 * j + 16)
                child_high[rows, at] = high[g]
                child_low[rows, at] = low[g]
    local = jnp.zeros((128, 512), F32)
    for t in range(4):
        finish(copies[7 + t])
        at = slice(512 * t, 512 * t + 512)
        high = child_high[:, at]
        w2h, w2l = halves(two[at, :])
        local = local + (rows_by_cols(high, w2h) + (rows_by_cols(high, w2l) + rows_by_cols(child_low[:, at], w2h)))
    finish(*copies[1:4], copies[6])
    w1h, w1l = halves(one[...])
    local = local.reshape(8, 2, 8, 512) + near_one[...]
    re = local[:, 0]
    im = local[:, 1]
    for j in range(4):
        c = cos1[j : j + 1, :][None]
        s = sin1[j : j + 1, :][None]
        both = jnp.concatenate([(c * re + s * im)[:, None], (c * im - s * re)[:, None]], axis=1)
        down = product(rows_by_cols, both.reshape(128, 512), w1h, w1l)
        held[128 * j : 128 * j + 128] = down
    largest = jnp.max(jnp.abs(held[...]), keepdims=True)
    power = power_of(largest)
    out[0:512] = code_of(held[...] * scale_from(power))
    out[512:528] = jnp.broadcast_to(power, (16, 128)).astype(I32).astype(I16)
    finish(*begin(sems, (out, out_to)))


def near_kernel(start, groups, lists_from, counts_from, inner, current, outer, blocks_from, out_to, lists, counts, held, blocks, out, sems):
    odd = lax.rem(lax.axis_index("space"), 2)
    copies = begin(
        sems,
        (lists_from, lists),
        (counts_from, counts),
        (inner, held.at[pl.ds(64 - 64 * odd, 32)]),
        (current, held.at[32:64]),
        (outer, held.at[pl.ds(64 * odd, 32)]),
        *[
            (blocks_from.at[start + 4 * t : start + 4 * t + 4], blocks.at[4 * t : 4 * t + 4])
            for t in range(groups)
        ],
    )
    held[96] = jnp.zeros((64, 256), BF16)
    finish(*copies[0:5])
    base = lax.axis_index("space") * 32 - 32

    for t in range(groups):
        finish(copies[5 + t])

        def body(n, carry):
            for row in (4 * t + 2 * n, 4 * t + 2 * n + 1):
                box = start + row
                total = jnp.zeros((64, 128), F32)
                for k in range(6):
                    source = jnp.where(k < counts[box], lists[k, box] - base, 96)
                    total = total + rows_by_rows(held[source], blocks[row, k].reshape(128, 256))
                out[row] = total
            return carry

        lax.fori_loop(0, 2, body, 0, unroll=2)
        copies += begin(sems, (out.at[4 * t : 4 * t + 4], out_to.at[4 * t : 4 * t + 4]), first=5 + groups + t)
    finish(*copies[5 + groups :])


def receive_kernel(l0, l1, l2, l3, x0, x1, x2, x3, near_first, near_second, out_to, codes, packs, samples, matrix, near, out, sems):
    copies = begin(
        sems,
        *[(l, codes.at[k]) for k, l in enumerate((l0, l1, l2, l3))],
        *[(x, packs.at[k]) for k, x in enumerate((x0, x1, x2, x3))],
        (near_first, near.at[0:NEAR_FIRST]),
        (near_second, near.at[NEAR_FIRST:32]),
    )
    finish(*copies[0:4])
    for k in range(4):
        values = value_of(codes[k, 0:512]) * unit_of(codes[k, 512:528])
        samples[:, :, :, sender(k)] = values.reshape(4, 8, 2, 8, 128)
    finish(*copies[4:10])
    units = [unit_of(packs[k, 1024:1040]) for k in range(4)]

    def body(p, carry):
        for j in range(4):
            b = 4 * p + j
            rows = pl.ds(pl.multiple_of(32 * b, 32), 32)
            for k in range(4):
                matrix[b, sender(k)] = value_of(packs[k, rows, :]) * units[k]
            left_high, left_low = halves(samples[j, p].reshape(64, 128))
            high, low = halves(matrix[b].reshape(128, 128))
            left = jnp.concatenate([left_high, left_low], axis=1)
            right = jnp.concatenate(
                [jnp.concatenate([high, low], axis=1), jnp.concatenate([high, jnp.zeros_like(low)], axis=1)], axis=0
            )
            both = rows_by_cols(left, right)
            total = near[b] + (both[:, :128] + both[:, 128:])
            turned = swap_half(total)
            out[b, 0] = (total[:32] - turned[32:])[:, :64]
            out[b, 1] = (total[32:] + turned[:32])[:, :64]
        return carry

    for t in range(4):
        lax.fori_loop(2 * t, 2 * t + 2, body, 0, unroll=2)
        part = slice(8 * t, 8 * t + 8)
        copies += begin(sems, (out.at[part], out_to.at[part]), first=10 + t)
    finish(*copies[10:])


def near_part(start, boxes, *operands):
    return call(
        functools.partial(near_kernel, start, boxes // 4),
        [((boxes, 64, 128), F32)],
        list(operands),
        [
            pltpu.SMEM((6, 32), I32),
            pltpu.SMEM((32,), I32),
            pltpu.VMEM((97, 64, 256), BF16),
            pltpu.VMEM((boxes, 6, 2, 64, 256), BF16),
            pltpu.VMEM((boxes, 64, 128), F32),
        ],
        5 + boxes // 2,
        SMALL,
        "near",
        limit=60,
        landed=(2, 4),
    )[0]


def around(x, axis, peers, k):
    return lax.ppermute(x, axis, [(i, (i + k) % peers) for i in range(peers)])


def after_all(values, *tokens):
    return lax.optimization_barrier((*values, *tokens))[: len(values)]


def shards(
    currents,
    near_blocks,
    near_list,
    near_count,
    radiate,
    receive,
    phase_one,
    phase_two,
    interp_one,
    interp_two,
    trans_one,
    kind_one,
    list_one,
    trans_two,
    kind_two,
    list_two,
):
    n_space = lax.axis_size("space")
    n_dir = lax.axis_size("dir")
    first_swap = [(i ^ 1, i) for i in range(n_space)]
    second_swap = [(i, j) for k in range(1, n_space - 1, 2) for i, j in ((k, k + 1), (k + 1, k))]

    flat = currents.reshape(32, 64, 256)
    inner = lax.ppermute(flat, "space", first_swap)
    outer = lax.ppermute(flat, "space", second_swap)

    leaf = call(
        leaf_kernel,
        [((272, 128), I16)] * 4,
        [currents, radiate, trans_one, trans_two],
        [
            pltpu.VMEM((32, 2, 32, 256), BF16),
            pltpu.VMEM((32, 2, 32, 256), BF16),
            pltpu.VMEM((40, 2, 128), F32),
            pltpu.VMEM((40, 2, 512), F32),
            pltpu.VMEM((4, 128, 128), F32),
            pltpu.VMEM((4, 272, 128), I16),
        ],
        6,
        LARGE,
        "leaf",
        limit=62,
    )
    own_leaf = leaf[0]
    leaf = [own_leaf] + [around(leaf[k], "dir", n_dir, k) for k in (1, 2, 3)]
    angle_room = [*[pltpu.VMEM((4, 512), F32)] * 2, *[pltpu.VMEM((4, 2048), F32)] * 2]
    packed = call(
        pack_kernel,
        [((1040, 128), I16)] * 4 + [((4, 512), F32)] * 2 + [((4, 2048), F32)] * 2,
        list(after_all((receive, phase_one, phase_two), own_leaf)),
        [
            pltpu.VMEM((32, 2, 32, 256), F32),
            pltpu.VMEM((4, 512), F32),
            pltpu.VMEM((4, 2048), F32),
            *angle_room,
            pltpu.VMEM((4, 1040, 128), I16),
        ],
        8,
        SMALL,
        "pack",
    )
    packed, angles = packed[:4], packed[4:]
    leaf, packed = lax.optimization_barrier((leaf, packed))
    packed = [packed[0]] + [around(packed[k], "dir", n_dir, k) for k in (1, 2, 3)]


    parent, halo, message = call(
        lift_kernel,
        [((8, 2, 8, 512), F32), ((128, 512), BF16), ((32, 16, 128), F32)],
        leaf + [interp_one, interp_two] + list(angles),
        [
            pltpu.VMEM((512, 128), F32),
            pltpu.VMEM((2048, 512), F32),
            *angle_room,
            pltpu.VMEM((8, 2, 8, 512), F32),
            pltpu.VMEM((128, 512), BF16),
            pltpu.VMEM((32, 16, 128), F32),
            pltpu.VMEM((4, 272, 128), I16),
            pltpu.VMEM((4, 128, 128), F32),
            pltpu.VMEM((2, 4, 2, 8, 2048), F32),
        ],
        16,
        LARGE,
        "lift",
        landed=(1, 2, 3),
    )
    top = lax.all_to_all(message, "space", 0, 0)
    parents_inner = lax.ppermute(halo, "space", first_swap)
    parents_outer = lax.ppermute(halo, "space", second_swap)

    top, inner, outer = lax.optimization_barrier((top, inner, outer))
    (moved,) = call(
        top_kernel,
        [((64, 8, 128), F32)],
        [kind_two.T, list_two.T, top.reshape(64, 8, 128)] + leaf,
        [
            pltpu.SMEM((8, 64), I32),
            pltpu.SMEM((8, 64), I32),
            pltpu.VMEM((64, 8, 128), F32),
            pltpu.VMEM((4, 144, 128), I16),
            pltpu.VMEM((40, 128), F32),
            pltpu.VMEM((40, 128), F32),
            pltpu.VMEM((64, 8, 128), F32),
        ],
        7,
        LARGE,
        "translate_two",
        landed=(2, 4, 5, 6),
    )
    moved, parents_inner, parents_outer = lax.optimization_barrier((moved, parents_inner, parents_outer))
    arrived = lax.all_to_all(moved.reshape(32, 16, 128), "space", 0, 0)

    near_parts = [
        near_part(start, boxes, near_list.T, near_count, inner, flat, outer, near_blocks)
        for start, boxes in ((0, NEAR_FIRST), (NEAR_FIRST, 32 - NEAR_FIRST))
    ]
    (near_one,) = call(
        parent_kernel,
        [((8, 2, 8, 512), F32)],
        [kind_one, list_one, parents_inner, parent, parents_outer] + leaf,
        [
            pltpu.SMEM((8, 8), I32),
            pltpu.SMEM((8, 8), I32),
            pltpu.VMEM((128, 512), BF16),
            pltpu.VMEM((128, 512), BF16),
            pltpu.VMEM((24, 2, 8, 512), F32),
            pltpu.VMEM((4, 96, 128), I16),
            pltpu.VMEM((4, 80, 128), F32),
            pltpu.VMEM((8, 2, 8, 512), F32),
        ],
        9,
        SMALL,
        "translate_one",
        landed=(2, 4, 6, 7, 8),
    )

    arrived, near_one, near_parts[0], packed = lax.optimization_barrier((arrived, near_one, near_parts[0], packed))
    (lowered,) = call(
        lower_kernel,
        [((528, 128), I16)],
        [arrived, near_one] + list(angles) + [interp_one, interp_two],
        [
            *angle_room,
            pltpu.VMEM((512, 128), F32),
            pltpu.VMEM((2048, 512), F32),
            pltpu.VMEM((32, 16, 128), F32),
            pltpu.VMEM((8, 2, 8, 512), F32),
            pltpu.VMEM((128, 2048), BF16),
            pltpu.VMEM((128, 2048), BF16),
            pltpu.VMEM((512, 128), F32),
            pltpu.VMEM((528, 128), I16),
        ],
        11,
        LARGE,
        "lower",
        landed=(0,),
    )
    shared = [around(lowered, "dir", n_dir, k) for k in (1, 2, 3)]

    (fields,) = call(
        receive_kernel,
        [((32, 2, 32, 64), F32)],
        [lowered] + shared + packed + near_parts,
        [
            pltpu.VMEM((4, 528, 128), I16),
            pltpu.VMEM((4, 1040, 128), I16),
            pltpu.VMEM((4, 8, 2, 4, 8, 128), F32),
            pltpu.VMEM((32, 4, 32, 128), F32),
            pltpu.VMEM((32, 64, 128), F32),
            pltpu.VMEM((32, 2, 32, 64), F32),
        ],
        14,
        LARGE,
        "receive",
        landed=(1, 2, 3, 5, 6, 7),
    )
    return fields


def solution(mesh):
    in_specs = (
        P("space", None, None, None),
        P("space", None, None, "dir", None),
        P("space", None),
        P("space"),
        P("space", None, "dir", None),
        P("space", None, "dir", None),
        P(),
        P(),
        P(),
        P(),
        P(None, None, "dir"),
        P("space", None),
        P("space", None),
        P(None, None, "dir"),
        P(),
        P(),
    )
    out_specs = P("space", None, None, "dir")
    return jax.shard_map(shards, mesh=mesh, in_specs=in_specs, out_specs=out_specs, check_vma=False)
```
